128 devices in a mesh: section: 2 (over core), tensor: 4 (over x), dp: 16 (over z, y).
Axes of the slice: x: 4, y: 4, z: 4, core: 2. Of those that a mesh axis runs over, the one named last changes fastest.
Arguments:
- boundary: float32 [2, 2, 2048, 1024], P('section', None, 'dp'), may hold values from -6 to 6
- doc_lengths: int32 [2, 16, 4], P(None, 'dp'), may hold values from 1 to 96, 128 in all within a row
- routes: int32 [2, 2, 2048, 8], P('section', None, 'dp'), may hold values from 0 to 31, all different within a row; in each aligned block of 128 rows (0 to 127, 128 to 255, ..., all dimensions but the last counted through in order) at most 48 rows name the same one
- norm_gains: bfloat16 [2, 2, 1024], P('section', None, 'dp'), may hold values from 0.5 to 1.5
- w_query: bfloat16 [2, 1024, 1024], P('section', 'dp', 'tensor'), may hold values from -0.1875 to 0.1875
- key_value_weight: bfloat16 [2, 2, 1024, 512], P('section', None, 'dp', 'tensor'), may hold values from -0.1875 to 0.1875
- w_out: bfloat16 [2, 1024, 1024], P('section', 'tensor', 'dp'), may hold values from -1 to 1
- w_router: bfloat16 [2, 1024, 32], P('section', 'dp'), may hold values from -0.09375 to 0.09375
- w_gateup: bfloat16 [2, 2, 32, 1024, 512], P('section', None, None, 'dp', 'tensor'), may hold values from -0.1875 to 0.1875
- w_down: bfloat16 [2, 32, 512, 1024], P('section', None, 'tensor', 'dp'), may hold values from -1.25 to 1.25
Outputs:
- layer_outputs: float32 [2, 2, 2048, 1024], P('section', None, 'dp')
- input_grads: float32 [2, 2, 2048, 1024], P('section', None, 'dp')
- grad_gains: float32 [2, 2, 1024], P('section', None, 'dp')
- grad_query: float32 [2, 1024, 1024], P('section', 'dp', 'tensor')
- grad_keyval: float32 [2, 2, 1024, 512], P('section', None, 'dp', 'tensor')
- grad_out: float32 [2, 1024, 1024], P('section', 'tensor', 'dp')
- grad_router: float32 [2, 1024, 32], P('section', 'dp')
- grad_gateup: float32 [2, 2, 32, 1024, 512], P('section', None, None, 'dp', 'tensor')
- grad_down: float32 [2, 32, 512, 1024], P('section', None, 'tensor', 'dp')
The draws below stay inside these ranges and needn't reach their ends.
Inputs may be any that keep to these rules, and one draw needn't show every extreme that they name: `doc_lengths`: each group's 4 documents of a micro-batch fill its 128 rows; the longest has 96. `routes`: a token names 8 different experts; in each aligned block of 128 rows (one group's rows of one micro-batch and layer) no expert is named by more than 48 rows, a bound that some block reaches.
All inputs are finite; a program needn't handle non-finite values.
Results may differ from the reference program's by a relative error of at most 0.035.
Values may be sent and summed in bfloat16 or wider, within the bound.
A program may use at most 256 MiB of HBM per device.

```python
import math
import jax
import jax.numpy as jnp
import numpy as np
from jax import lax

MODEL_WIDTH = 1024
QUERY_HEADS = 16
KEY_VALUE_HEADS = 8
HEAD_SIZE = 64
E = 32
FF = 512
TOPK = 8
TOKG = 128
M = 2
DOCS = 4
CAP = 48
SEQ_MOST = 96
TOK = 2048
N_SECTION = 2
N_DP = 16


def shard_levels(key, extent, split, smallest, largest):
    def one(position, blocks):
        steps = jax.random.uniform(jax.random.fold_in(jax.random.fold_in(key, 6), position), (blocks,), jnp.float32, smallest / len(split), largest / len(split))
        return jnp.repeat(jnp.exp(steps), extent[position] // blocks).reshape((-1,) + (1,) * (len(extent) - position - 1))

    gain = one(*split[0])
    for cut in split[1:]:
        gain = gain * one(*cut)
    return gain


def split_up(amount, total, limit, skew):
    portions = [(1 << 20) // math.isqrt(rank ** skew) + 1 for rank in range(2, amount + 1)]
    surplus, holding = total - limit - (amount - 1), [1] * (amount - 1)
    while surplus > 0:
        candidates = [i for i in range(amount - 1) if holding[i] < limit]
        pool, left = sum([portions[i] for i in candidates]), surplus
        for i in candidates:
            more = min(limit - holding[i], max(1, left * portions[i] // pool), surplus)
            holding[i] = holding[i] + more
            surplus = surplus - more
    return np.array([limit] + holding)


def uneven_parts(key, amount, total, reach, skew):
    if amount == 2:
        one = jax.random.randint(key, (), max(1, total - reach), min(reach, total - 1) + 1)
        return jnp.stack([one, total - one])
    sizes = jnp.asarray(split_up(amount, total, reach, skew), jnp.int32)
    twos = (amount - 1) // 2
    giver, receiver = sizes[1:1 + 2 * twos:2], sizes[2:2 + 2 * twos:2]
    slack = jnp.minimum(giver - 1, reach - receiver)
    moved = jax.random.randint(jax.random.fold_in(key, 1), (twos,), 0, 1 << 20) % (slack + 1)
    sizes = sizes.at[1:1 + 2 * twos:2].set(giver - moved).at[2:2 + 2 * twos:2].set(receiver + moved)
    return sizes[jax.random.permutation(jax.random.fold_in(key, 2), amount)]


def assign_block(rng, own, number, rows, amount, top, reach, skew):
    sequence = jax.random.permutation(rng, amount)
    heavy_load, usual = portions_of(amount, rows * top, reach, skew, True), portions_of(amount, rows * top, reach, skew, False)
    places = jnp.arange(amount)

    def named(tallies, offset_by):
        used = int((tallies > 0).sum())
        fixed = max(1, used // 4)
        moved = fixed + (places - fixed + offset_by * (used - fixed)) % max(1, amount - fixed)
        return jnp.zeros((amount,), jnp.int32).at[sequence[jnp.where(places < fixed, places, moved)]].set(jnp.asarray(tallies, jnp.int32))

    tallies = jnp.where(number % 4 == 0, named(heavy_load, number // 4), named(usual, number - number // 4 - 1))
    mixed = jax.random.permutation(jax.random.fold_in(own, 3), amount)
    giver, receiver = mixed[0:amount // 2 * 2:2], mixed[1:amount // 2 * 2:2]
    slack = jnp.minimum(tallies[giver] - 1, reach - tallies[receiver]) // 2
    slack = jnp.where((giver == sequence[0]) | (receiver == sequence[0]) | (tallies[receiver] == 0), 0, jnp.maximum(slack, 0))
    moved = jax.random.randint(jax.random.fold_in(own, 4), (amount // 2,), 0, 1 << 20) % (slack + 1)
    tallies = tallies.at[giver].add(-moved).at[receiver].add(moved)
    labels = jnp.searchsorted(jnp.cumsum(tallies), jnp.arange(rows * top), side="right").astype(jnp.int32)
    listing = labels.reshape(top, rows).T
    listing = listing[jax.random.permutation(jax.random.fold_in(own, 1), rows)]
    offset_by = jax.random.randint(jax.random.fold_in(own, 2), (rows, 1), 0, top)
    return jnp.take_along_axis(listing, (jnp.arange(top)[None, :] + offset_by) % top, axis=1)


def portions_of(count, total, limit, slope, full):
    loads = [(1 << 20) // math.isqrt(grade ** slope) + 1 for grade in range(1, count + 1)]
    largest = limit if full else min(limit, max(-(-total // count), total * loads[0] // sum(loads)))
    least = 1 if total - largest >= count - 1 else 0
    given, spare = [largest] + [least] * (count - 1), total - largest - least * (count - 1)
    while spare > 0:
        candidates = [i for i in range(1, count) if given[i] < largest] or [i for i in range(1, count) if given[i] < limit]
        mass, remaining = sum([loads[i] for i in candidates]), spare
        for i in candidates:
            addition = min(limit - given[i], max(1, remaining * loads[i] // mass), spare)
            given[i] = given[i] + addition
            spare = spare - addition
    return np.array(given)


def centred(stream_key, shape, spread, limit, pieces=(), kind=jnp.bfloat16):
    level = shard_levels(stream_key, shape, pieces, -0.22, 0.18) if pieces else 1.0
    values = jax.random.normal(stream_key, shape, jnp.float32) * spread * level
    return jnp.minimum(jnp.maximum(values, -limit), limit).astype(kind)


def setup_inputs(seed: int = 0) -> dict:
    streams_of = jax.random.split(jax.random.key(seed), 11)
    boundary = centred(streams_of[0], (N_SECTION, M, TOK, MODEL_WIDTH), 1.0, 6.0, ((0, 2), (2, 16)), jnp.float32)
    doc_lengths = jax.vmap(lambda own: uneven_parts(own, DOCS, TOKG, SEQ_MOST, 2))(jax.random.split(streams_of[1], M * N_DP)).reshape((M, N_DP, DOCS)).astype(jnp.int32)
    routes_keys = jax.random.split(jax.random.fold_in(streams_of[2], 1), N_SECTION * M * TOK // TOKG)
    routes_turns = jax.random.permutation(jax.random.fold_in(streams_of[2], 3), N_SECTION * M * TOK // TOKG)
    routes = jax.vmap(lambda own, number: assign_block(jax.random.fold_in(streams_of[2], 2), own, number, TOKG, E, TOPK, CAP, 2))(routes_keys, routes_turns).reshape((N_SECTION, M, TOK, TOPK))
    norm_gains = jnp.clip(1.0 + 0.1 * jax.random.normal(streams_of[3], (N_SECTION, 2, MODEL_WIDTH), jnp.float32), 0.5, 1.5).astype(jnp.bfloat16)
    w_query = centred(streams_of[4], (N_SECTION, MODEL_WIDTH, QUERY_HEADS * HEAD_SIZE), MODEL_WIDTH ** -0.5, 0.1875, ((0, 2), (1, 16), (2, 4)))
    key_value_weight = centred(streams_of[5], (N_SECTION, 2, MODEL_WIDTH, KEY_VALUE_HEADS * HEAD_SIZE), MODEL_WIDTH ** -0.5, 0.1875, ((0, 2), (2, 16), (3, 4)))
    w_out = centred(streams_of[6], (N_SECTION, QUERY_HEADS * HEAD_SIZE, MODEL_WIDTH), (QUERY_HEADS * HEAD_SIZE // 32) ** -0.5, 1.0, ((0, 2), (1, 4), (2, 16)))
    w_router = centred(streams_of[7], (N_SECTION, MODEL_WIDTH, E), (4 * MODEL_WIDTH) ** -0.5, 0.09375, ((0, 2), (1, 16)))
    w_gateup = centred(streams_of[8], (N_SECTION, 2, E, MODEL_WIDTH, FF), MODEL_WIDTH ** -0.5, 0.1875, ((0, 2), (3, 16), (4, 4)))
    w_down = centred(streams_of[9], (N_SECTION, E, FF, MODEL_WIDTH), (max(FF // 21, 1)) ** -0.5, 1.25, ((0, 2), (2, 4), (3, 16)))
    return dict(boundary=boundary, doc_lengths=doc_lengths, routes=routes, norm_gains=norm_gains, w_query=w_query, key_value_weight=key_value_weight, w_out=w_out, w_router=w_router, w_gateup=w_gateup, w_down=w_down)


epsilon = 1e-06
rope_base = 10000.0
masked_score = -1e+30
HIGHEST = lax.Precision.HIGHEST

@jax.custom_vjp
def low(v):
    return lax.optimization_barrier(v.astype(jnp.bfloat16)).astype(jnp.float32)

@jax.custom_vjp
def low_back(v):
    return v

def low_keep(v):
    return (low(v), None)

def low_pass(kept, grad):
    return (grad,)

def back_keep(v):
    return (v, None)

def back_low(kept, grad):
    return (low(grad),)
low.defvjp(low_keep, low_pass)
low_back.defvjp(back_keep, back_low)

def doc_layout(lengths, count_of_rows):
    doc_ends = jnp.cumsum(lengths)
    doc_starts = doc_ends - lengths
    places = jnp.arange(count_of_rows, dtype=jnp.int32)
    segment = lax.optimization_barrier(jnp.sum((places[:, None] >= doc_ends[None, :]).astype(jnp.int32), axis=1))
    owners = segment[:, None] == jnp.arange(lengths.shape[0], dtype=jnp.int32)[None, :]
    offset = places - lax.optimization_barrier(jnp.sum(jnp.where(owners, doc_starts[None, :], 0), axis=1))
    visible = (segment[:, None] == segment[None, :]) & (places[None, :] <= places[:, None])
    return (offset, visible)

def rope_tables(offset, head_dim):
    half_dim = head_dim // 2
    frequency = rope_base ** (-2.0 * jnp.arange(half_dim, dtype=jnp.float32) / head_dim)
    angles = offset.astype(jnp.float32)[:, None] * frequency[None, :]
    return (jnp.cos(angles), jnp.sin(angles))

def rotate(values, cos_table, sin_table, head_dim):
    count_of_rows = values.shape[0]
    shaped = values.reshape(count_of_rows, -1, head_dim)
    first_half = shaped[..., :head_dim // 2]
    second_half = shaped[..., head_dim // 2:]
    cos_view = cos_table[:, None, :]
    sin_view = sin_table[:, None, :]
    turned = jnp.concatenate([first_half * cos_view - second_half * sin_view, second_half * cos_view + first_half * sin_view], axis=-1)
    return turned.reshape(count_of_rows, -1)

def norm_apply(values, gain_row):
    scale_row = lax.rsqrt(lax.optimization_barrier(jnp.mean(values * values, axis=1, keepdims=True)) + epsilon)
    return (values * scale_row * gain_row[None, :], scale_row)

def route_tables(routes, experts, capacity):
    pair_count = routes.shape[0] * routes.shape[1]
    flat_routes = routes.reshape(pair_count)
    onehot = (flat_routes[:, None] == jnp.arange(experts, dtype=jnp.int32)[None, :]).astype(jnp.int32)
    earlier = jnp.cumsum(onehot, axis=0) - onehot
    slot_index = lax.optimization_barrier(jnp.sum(earlier * onehot, axis=1))
    pair_slot = flat_routes * capacity + slot_index
    slot_pair = jnp.full((experts * capacity,), pair_count, jnp.int32).at[pair_slot].set(jnp.arange(pair_count, dtype=jnp.int32))
    return (pair_slot, slot_pair)

def product(left, right):
    return jnp.dot(left, right, precision=HIGHEST)

def span_layer(params, inputs, routes, lengths):
    gain_rows, w_query, key_value_weight, w_out, w_router, w_gateup, w_down = params
    count_of_rows = inputs.shape[0]
    offset, visible = doc_layout(lengths, count_of_rows)
    cos_table, sin_table = rope_tables(offset, HEAD_SIZE)
    normed_one, scale_one = norm_apply(inputs, gain_rows[0])
    first_in = low(normed_one)
    query_reduced = low(rotate(low_back(product(first_in, w_query)), cos_table, sin_table, HEAD_SIZE))
    key_value = jnp.einsum('nd,sdh->snh', first_in, key_value_weight, precision=HIGHEST)
    key_reduced = low(rotate(low_back(key_value[0]), cos_table, sin_table, HEAD_SIZE))
    value_reduced = low_back(low(key_value[1]))
    query_shaped_rows = query_reduced.reshape(count_of_rows, KEY_VALUE_HEADS, QUERY_HEADS // KEY_VALUE_HEADS, HEAD_SIZE)
    key_shaped_rows = key_reduced.reshape(count_of_rows, KEY_VALUE_HEADS, HEAD_SIZE)
    value_shaped_rows = value_reduced.reshape(count_of_rows, KEY_VALUE_HEADS, HEAD_SIZE)
    scores = low_back(jnp.einsum('qgrd,kgd->grqk', query_shaped_rows, key_shaped_rows, precision=HIGHEST) * HEAD_SIZE ** (-0.5))
    scores = jnp.where(visible[None, None], scores, masked_score)
    prob_rows = jax.nn.softmax(scores, axis=-1)
    mixed_rows = jnp.einsum('grqk,kgd->qgrd', low(prob_rows), value_shaped_rows, precision=HIGHEST).reshape(count_of_rows, -1)
    mixed_low = low_back(low(mixed_rows))
    attended = low_back(product(mixed_low, w_out))
    middle = inputs + attended
    normed_two, scale_two = norm_apply(middle, gain_rows[1])
    second_in = low(normed_two)
    logits = low_back(product(second_in, w_router))
    picker = (routes[:, :, None] == jnp.arange(E, dtype=jnp.int32)[None, None, :]).astype(jnp.float32)
    picked = lax.optimization_barrier(jnp.sum(picker * logits[:, None, :], axis=-1))
    gate_probs = jax.nn.softmax(picked, axis=-1)
    pair_slot, slot_pair = route_tables(routes, E, CAP)
    padded = jnp.concatenate([second_in, jnp.zeros((1, MODEL_WIDTH), jnp.float32)], axis=0)
    expert_in = padded[slot_pair // TOPK].reshape(E, CAP, MODEL_WIDTH)
    gate_up = low_back(jnp.einsum('ecd,sedf->secf', expert_in, w_gateup, precision=HIGHEST))
    hidden_low = low(jax.nn.silu(gate_up[0]) * gate_up[1])
    expert_out = low_back(jnp.einsum('ecf,efd->ecd', hidden_low, w_down, precision=HIGHEST))
    pair_out = expert_out.reshape(E * CAP, MODEL_WIDTH)[pair_slot].reshape(count_of_rows, TOPK, MODEL_WIDTH)
    return middle + lax.optimization_barrier(jnp.sum(gate_probs[:, :, None] * pair_out, axis=1))

def reference(boundary, doc_lengths, routes, norm_gains, w_query, key_value_weight, w_out, w_router, w_gateup, w_down):
    lengths = doc_lengths.reshape(M * N_DP, DOCS)

    def run_layer(layer_no, inputs, params):
        route_spans = routes[layer_no].reshape(M * N_DP, TOKG, TOPK)
        spans = inputs.reshape(M * N_DP, TOKG, MODEL_WIDTH)

        def one_span(packed):
            return span_layer(params, packed[0], packed[1], packed[2])
        produced = lax.map(jax.checkpoint(one_span), (spans, route_spans, lengths))
        return produced.reshape(M, TOK, MODEL_WIDTH)

    def layer_params(layer_no):
        return tuple((weight[layer_no].astype(jnp.float32) for weight in (norm_gains, w_query, key_value_weight, w_out, w_router, w_gateup, w_down)))
    params_one = layer_params(0)
    params_two = layer_params(1)
    block_in = boundary[0]
    cotangent = boundary[1]
    middle_out, back_one = jax.vjp(lambda inputs, params: run_layer(0, inputs, params), block_in, params_one)
    final_out, back_two = jax.vjp(lambda inputs, params: run_layer(1, inputs, params), middle_out, params_two)
    middle_grad, grads_two = back_two(cotangent)
    start_grad, grads_one = back_one(middle_grad)
    stacked = [jnp.stack([first, second]) for first, second in zip(grads_one, grads_two)]
    return (jnp.stack([middle_out, final_out]), jnp.stack([start_grad, middle_grad]), stacked[0], stacked[1], stacked[2], stacked[3], stacked[4], stacked[5], stacked[6])
```

```python
import jax
import jax.numpy as jnp
from jax import lax
from jax.experimental import pallas as pl
from jax.experimental.pallas import tpu as pltpu
from jax.sharding import PartitionSpec as P

HEAD_SIZE = 64
E = 32
TOPK = 8
CAP = 48
ROWS = 128
WIDTH = 1024
FF = 512
PART = 32
LOCAL = 8
DENSE = 896

epsilon = 1e-06
rope_base = 10000.0
masked_score = -1e30
f32 = jnp.float32
bf16 = jnp.bfloat16
MESH = pl.DeviceIdType.MESH


def dot(a, b):
    return lax.dot_general(a, b, (((1,), (0,)), ((), ())), preferred_element_type=f32)


def dot_nt(a, b):
    return lax.dot_general(a, b, (((1,), (1,)), ((), ())), preferred_element_type=f32)


def dot_tn(a, b):
    return lax.dot_general(a, b, (((0,), (0,)), ((), ())), preferred_element_type=f32)


def scale_of(values):
    return lax.rsqrt(jnp.mean(values * values, axis=1, keepdims=True) + epsilon)


def norm_back(values, gain_row, upstream):
    scale = scale_of(values)
    weighted = upstream * gain_row
    inner = jnp.mean(weighted * values, axis=1, keepdims=True)
    back = scale * weighted - values * (scale * scale * scale * inner)
    return back, jnp.sum(upstream * values * scale, axis=0, keepdims=True)


def low_lanes():
    return lax.broadcasted_iota(jnp.int32, (ROWS, 128), 1) < 64


def turn(chunk, cos, sin):
    place = lax.broadcasted_iota(jnp.int32, (ROWS, 128), 1) % 64
    swapped = jnp.where(place < 32, pltpu.roll(chunk, 96, 1), pltpu.roll(chunk, 32, 1))
    return chunk * cos + swapped * sin


def doubled(both):
    wide = both.astype(f32)
    other = pltpu.roll(wide, 64, 1)
    left = low_lanes()
    return (
        jnp.where(left, wide, other).astype(bf16),
        jnp.where(left, other, wide).astype(bf16),
    )


def half(chunk, which):
    left = low_lanes()
    keep = left if which == 0 else jnp.logical_not(left)
    return jnp.where(keep, chunk, jnp.zeros_like(chunk))


def soft(query_half, keys, seen):
    scores = dot_nt(query_half, keys) * HEAD_SIZE ** (-0.5)
    scores = jnp.where(seen, scores, masked_score)
    raised = jnp.exp(scores - jnp.max(scores, axis=1, keepdims=True))
    return raised / jnp.sum(raised, axis=1, keepdims=True)


def body(
    dense, experts, first_x, cotangent, routes, cos_ref, sin_ref, seen_ref,
    out_ref, grad_ref, dense_grad, expert_grad,
    xin, uin, turned, first_in, qkv, mixed, middle, chosen, chance, slot_gate,
    rs_send, rs_recv, ag, small, slots, packed, x_rows, og_rows, gate_s, up_s, hid_s,
    y_rows, ret, gg_low, ug_low, gate_grads, resid, gains, router_back, dqkv, swap_out, swap_in,
    rs_ss, rs_rs, ag_ss, ag_rs, sm_ss, sm_rs, d_ss, d_rs, r_ss, r_rs, w_ss, w_rs,
):
    s = lax.axis_index("section")
    x = lax.axis_index("tensor")
    d = lax.axis_index("dp")
    z, y = d // 4, d % 4
    zz = z % 2
    mine = zz * 4 + y
    rows_mine = pl.ds(pl.multiple_of(x * PART, PART), PART)
    experts_mine = pl.ds(pl.multiple_of(x * LOCAL, LOCAL), LOCAL)
    near = [(kz, ky) for kz in range(2) for ky in range(4)]

    def spot(kz, ky):
        z2, y2 = (zz + kz) % 2, (y + ky) % 4
        return z2 * 4 + y2, ((z // 2) * 2 + z2) * 4 + y2

    barrier = pltpu.get_barrier_semaphore()
    for k in range(1, 4):
        pl.semaphore_signal(
            barrier, inc=1, device_id={"tensor": (x + k) % 4}, device_id_type=MESH
        )
    for kz, ky in near:
        peer = spot(kz, ky)[1]
        if (kz, ky) != (0, 0):
            pl.semaphore_signal(barrier, inc=1, device_id={"dp": peer}, device_id_type=MESH)
        pl.semaphore_signal(
            barrier, inc=1, device_id={"section": 1 - s, "dp": peer}, device_id_type=MESH
        )
    pl.semaphore_wait(barrier, 18)

    def remote(src, dst, send, recv, device):
        return pltpu.make_async_remote_copy(
            src_ref=src, dst_ref=dst, send_sem=send, recv_sem=recv,
            device_id=device, device_id_type=MESH,
        )

    def scatter_copies(l, j):
        copies = []
        for k in range(1, 4):
            p = (x + k) % 4
            src = rs_send.at[l, j, pl.ds(pl.multiple_of(p * PART, PART), PART)]
            copies.append(
                remote(src, rs_recv.at[l, j, k - 1], rs_ss.at[l, j, k - 1],
                       rs_rs.at[l, j, k - 1], {"tensor": p})
            )
        return copies

    def scatter_start(l, j, partial):
        rs_send[l, j] = partial.astype(bf16)
        for copy in scatter_copies(l, j):
            copy.start()

    def scatter_end(l, j):
        for copy in scatter_copies(l, j):
            copy.wait()
        total = rs_send[l, j, rows_mine].astype(f32)
        for k in range(3):
            total = total + rs_recv[l, j, k].astype(f32)
        return total

    def gather_copies(l, j):
        copies = []
        for k in range(1, 4):
            ref = ag.at[l, j, rows_mine]
            copies.append(
                remote(ref, ref, ag_ss.at[l, j, k - 1], ag_rs.at[l, j, k - 1],
                       {"tensor": (x + k) % 4})
            )
        return copies

    def gather_start(l, j, rows):
        ag[l, j, rows_mine] = rows.astype(bf16)
        for copy in gather_copies(l, j):
            copy.start()

    def gather_end(l, j):
        for copy in gather_copies(l, j):
            copy.wait()

    def small_copies(l, j):
        copies = []
        for k in range(1, 4):
            ref = small.at[l, j, x]
            copies.append(
                remote(ref, ref, sm_ss.at[l, j, k - 1], sm_rs.at[l, j, k - 1],
                       {"tensor": (x + k) % 4})
            )
        return copies

    def block(index):
        return pl.ds(pl.multiple_of(index * CAP, CAP), CAP)

    def dispatch_copies(l, way, act):
        rel = (s + l) % 2
        target = x_rows if way == 0 else og_rows
        for kz, ky in near:
            i, peer = spot(kz, ky)
            n = kz * 4 + ky
            src = packed.at[l, way, block(i)]
            dst = target.at[block(rel * 8 + mine)]
            far = remote(src, dst, d_ss.at[l, way, n], d_rs.at[way, rel * 8 + n],
                         {"section": l, "dp": peer})
            if n == 0:
                @pl.when(s == l)
                def _():
                    if act == 0:
                        pltpu.make_async_copy(src, dst, d_rs.at[way, 0]).start()

                @pl.when(s != l)
                def _():
                    if act == 0:
                        far.start()
                    else:
                        far.wait_send()
            elif act == 0:
                far.start()
            else:
                far.wait_send()

    def dispatch_arrived(way, rel):
        target = x_rows if way == 0 else og_rows
        for n in range(8):
            dst = target.at[block(rel * 8 + n)]
            src = packed.at[0, way, block(n)]
            if rel == 0 and n == 0:
                pltpu.make_async_copy(
                    packed.at[0, way, block(mine)], target.at[block(mine)], d_rs.at[way, 0]
                ).wait()
            else:
                remote(src, dst, d_ss.at[0, way, n], d_rs.at[way, rel * 8 + n],
                       {"dp": spot(0, 1)[1]}).wait_recv()

    def return_copies(l, way, rel, act):
        for kz, ky in near:
            i, peer = spot(kz, ky)
            n = kz * 4 + ky
            src = y_rows.at[way, block(rel * 8 + i)]
            dst = ret.at[l, way, block(mine)]
            if rel == 0 and n == 0:
                if act == 0:
                    pltpu.make_async_copy(src, dst, r_rs.at[l, way, 0]).start()
                continue
            far = remote(src, dst, r_ss.at[way, rel * 8 + n], r_rs.at[l, way, n],
                         {"section": (s + rel) % 2, "dp": peer})
            if act == 0:
                far.start()
            else:
                far.wait_send()

    def return_arrived(l, way):
        for kz, ky in near:
            i, peer = spot(kz, ky)
            n = kz * 4 + ky
            src = y_rows.at[way, block(n)]
            dst = ret.at[l, way, block(i)]
            far = remote(src, dst, r_ss.at[way, n], r_rs.at[l, way, n],
                         {"section": 1 - s, "dp": peer})
            if n == 0:
                @pl.when(s == l)
                def _():
                    pltpu.make_async_copy(src, dst, r_rs.at[l, way, 0]).wait()

                @pl.when(s != l)
                def _():
                    far.wait_recv()
            else:
                far.wait_recv()

    def swap_copy(way):
        return remote(swap_out.at[way], swap_in.at[way], w_ss.at[way], w_rs.at[way],
                      {"section": 1 - s})

    def keep_result(way, l, ref):
        @pl.when(s == l)
        def _():
            ref[s] = ag[l, 1 + 2 * way].astype(f32)

        @pl.when(s != l)
        def _():
            swap_out[way] = ag[l, 1 + 2 * way]
            swap_copy(way).start()

    xin[0] = first_x[...]
    uin[1] = cotangent[...]

    def forward(l, carry):
        turned[l] = dense[l, :, 768:896].astype(f32).T
        values = xin[l]
        first = (values * scale_of(values) * turned[l, 32:33]).astype(bf16)
        first_in[l] = first
        made = dot(first, dense[l, :, 0:512])
        cos, sin = cos_ref[...], sin_ref[...]
        for c in range(3):
            cut = slice(128 * c, 128 * c + 128)
            qkv[l, :, cut] = turn(made[:, cut], cos, sin).astype(bf16)
        qkv[l, :, 384:512] = made[:, 384:512].astype(bf16)
        seen = seen_ref[...] > 0
        keys = doubled(qkv[l, :, 256:384])
        vals = doubled(qkv[l, :, 384:512])
        for c in range(2):
            cut = slice(128 * c, 128 * c + 128)
            query = qkv[l, :, cut]
            got = [
                dot(soft(half(query, b), keys[c], seen).astype(bf16), vals[c]) for b in range(2)
            ]
            mixed[l, :, cut] = jnp.where(low_lanes(), got[0], got[1]).astype(bf16)
        scatter_start(l, 0, dot_nt(mixed[l], dense[l, :, 512:768]))

        experts_iota = lax.broadcasted_iota(jnp.int32, (E, ROWS), 0)
        named = jnp.zeros((E, ROWS), f32)
        for k in range(TOPK):
            named = named + (experts_iota == routes[l, k:k + 1]).astype(f32)
        before = (
            lax.broadcasted_iota(jnp.int32, (ROWS, ROWS), 0)
            < lax.broadcasted_iota(jnp.int32, (ROWS, ROWS), 1)
        ).astype(bf16)
        place = dot(named.astype(bf16), before)
        slots[...] = jnp.where(named > 0, place, -1.0)
        place = slots[experts_mine]
        slot_iota = lax.broadcasted_iota(jnp.int32, (CAP, ROWS), 0).astype(f32)
        for i in range(LOCAL):
            chosen[l, CAP * i:CAP * i + CAP] = (slot_iota == place[i:i + 1]).astype(bf16)

        center = xin[l, rows_mine] + scatter_end(l, 0)
        middle[l] = center
        gather_start(l, 0, center * scale_of(center) * turned[l, 33:34])
        gather_end(l, 0)

        second = ag[l, 0]
        packed[l, 0] = dot(chosen[l], second).astype(bf16)
        dispatch_copies(l, 0, 0)
        logits = dot_nt(turned[l, 0:32].astype(bf16), second)
        logits = jnp.where(named > 0, logits, masked_score)
        raised = jnp.where(named > 0, jnp.exp(logits - jnp.max(logits, axis=0, keepdims=True)), 0.0)
        chance[l] = raised / jnp.sum(raised, axis=0, keepdims=True)
        gate = chance[l, experts_mine]
        for i in range(LOCAL):
            cut = slice(CAP * i, CAP * i + CAP)
            weighted = chosen[l, cut].astype(f32) * gate[i:i + 1]
            slot_gate[l, cut] = jnp.sum(weighted, axis=1, keepdims=True)

        @pl.when(s == l)
        def _():
            for rel in range(2):
                dispatch_arrived(0, rel)
                cut = slice(384 * rel, 384 * rel + 384)
                rows = x_rows[cut]
                gate_part = dot(rows, experts[0])
                up_part = dot(rows, experts[1])
                gate_s[cut] = gate_part
                up_s[cut] = up_part
                hidden = (gate_part / (1.0 + jnp.exp(-gate_part)) * up_part).astype(bf16)
                hid_s[cut] = hidden
                y_rows[0, cut] = dot_nt(hidden, experts[2]).astype(bf16)
                return_copies(l, 0, rel, 0)

        return_arrived(l, 0)
        scaled = ret[l, 0].astype(f32) * slot_gate[l]
        scatter_start(l, 1, dot_tn(chosen[l], scaled.astype(bf16)))
        gather_start(l, 1, middle[l] + scatter_end(l, 1))
        gather_end(l, 1)
        xin[l + 1] = ag[l, 1].astype(f32)
        keep_result(0, l, out_ref)
        dispatch_copies(l, 0, 1)
        return carry

    lax.fori_loop(0, 2, forward, 0)

    def backward(step, carry):
        l = 1 - step
        upstream = uin[l].astype(bf16)
        spread = dot(chosen[l], upstream)
        packed[l, 1] = (spread * slot_gate[l]).astype(bf16)
        dispatch_copies(l, 1, 0)
        inner = jnp.sum(spread * ret[l, 0].astype(f32), axis=1, keepdims=True)
        for i in range(LOCAL):
            cut = slice(CAP * i, CAP * i + CAP)
            row = jnp.sum(chosen[l, cut].astype(f32) * inner[cut], axis=0, keepdims=True)
            gate_grads[i:i + 1] = row
        small[l, 0, x, 0:8] = gate_grads[...]
        for copy in small_copies(l, 0):
            copy.start()

        @pl.when(s == l)
        def _():
            for rel in range(2):
                dispatch_arrived(1, rel)
                cut = slice(384 * rel, 384 * rel + 384)
                hidden_grad = dot(og_rows[cut], experts[2])
                gate_part = gate_s[cut]
                up_part = up_s[cut]
                sig = 1.0 / (1.0 + jnp.exp(-gate_part))
                gate_low = (
                    hidden_grad * up_part * sig * (1.0 + gate_part * (1.0 - sig))
                ).astype(bf16)
                up_low = (hidden_grad * gate_part * sig).astype(bf16)
                gg_low[cut] = gate_low
                ug_low[cut] = up_low
                back = dot_nt(gate_low, experts[0]) + dot_nt(up_low, experts[1])
                y_rows[1, cut] = back.astype(bf16)
                return_copies(l, 1, rel, 0)
            expert_grad[0] = dot_tn(x_rows[...], gg_low[...]).astype(bf16)
            expert_grad[1] = dot_tn(x_rows[...], ug_low[...]).astype(bf16)
            expert_grad[2] = dot_tn(og_rows[...], hid_s[...]).astype(bf16)

        for copy in small_copies(l, 0):
            copy.wait()
        gate = chance[l]
        gate_total = jnp.concatenate([small[l, 0, p, 0:8] for p in range(4)], axis=0)
        picked = gate * (gate_total - jnp.sum(gate * gate_total, axis=0, keepdims=True))
        logit_low = picked.astype(bf16)
        router_back[...] = dot_tn(logit_low, turned[l, 0:32].astype(bf16))
        return_arrived(l, 1)
        scatter_start(l, 2, dot_tn(chosen[l], ret[l, 1]))
        router_grad = dot(logit_low, ag[l, 0])
        arrived = scatter_end(l, 2) + router_back[rows_mine]
        back, gain_two = norm_back(middle[l], turned[l, 33:34], arrived)
        kept = uin[l, rows_mine] + back
        resid[...] = kept
        gather_start(l, 2, kept)
        gather_end(l, 2)

        branch = ag[l, 2]
        mixed_grad = dot(branch, dense[l, :, 512:768]).astype(bf16)
        seen = seen_ref[...] > 0
        cos, sin = cos_ref[...], -sin_ref[...]
        left = low_lanes()
        keys = doubled(qkv[l, :, 256:384])
        vals = doubled(qkv[l, :, 384:512])
        key_grads, value_grads = [], []
        for c in range(2):
            cut = slice(128 * c, 128 * c + 128)
            query, above = qkv[l, :, cut], mixed_grad[:, cut]
            parts, key_grad, value_grad = [], 0.0, 0.0
            for b in range(2):
                query_half, above_half = half(query, b), half(above, b)
                prob = soft(query_half, keys[c], seen)
                value_grad = value_grad + dot_tn(prob.astype(bf16), above_half)
                prob_grad = dot_nt(above_half, vals[c])
                mean = jnp.sum(prob * prob_grad, axis=1, keepdims=True)
                score_low = (prob * (prob_grad - mean)).astype(bf16)
                parts.append(dot(score_low, keys[c]))
                key_grad = key_grad + dot_tn(score_low, query_half)
            query_grad = jnp.where(left, parts[0], parts[1]) * HEAD_SIZE ** (-0.5)
            dqkv[:, cut] = turn(query_grad, cos, sin).astype(bf16)
            key_grads.append(key_grad + pltpu.roll(key_grad, 64, 1))
            value_grads.append(value_grad + pltpu.roll(value_grad, 64, 1))
        key_grad = jnp.where(left, key_grads[0], key_grads[1]) * HEAD_SIZE ** (-0.5)
        dqkv[:, 256:384] = turn(key_grad, cos, sin).astype(bf16)
        dqkv[:, 384:512] = jnp.where(left, value_grads[0], value_grads[1]).astype(bf16)
        scatter_start(l, 3, dot_nt(dqkv[...], dense[l, :, 0:512]))
        dense_grad[l, :, 0:512] = dot_tn(first_in[l], dqkv[...]).astype(bf16)
        dense_grad[l, :, 512:768] = dot_tn(branch, mixed[l]).astype(bf16)
        back, gain_one = norm_back(xin[l, rows_mine], turned[l, 32:33], scatter_end(l, 3))
        gather_start(l, 3, resid[...] + back)
        gains[l, x, 0:1] = gain_one
        gains[l, x, 1:2] = gain_two
        for k in range(1, 4):
            ref = gains.at[l, x]
            remote(ref, ref, sm_ss.at[l, 1, k - 1], sm_rs.at[l, 1, k - 1],
                   {"tensor": (x + k) % 4}).start()
        gather_end(l, 3)
        uin[1 - l] = ag[l, 3].astype(f32)
        keep_result(1, l, grad_ref)
        for k in range(1, 4):
            ref = gains.at[l, x]
            remote(ref, ref, sm_ss.at[l, 1, k - 1], sm_rs.at[l, 1, k - 1],
                   {"tensor": (x + k) % 4}).wait()
        total = gains[l, 0] + gains[l, 1] + gains[l, 2] + gains[l, 3]
        last = jnp.concatenate([router_grad, total, jnp.zeros((88, WIDTH), f32)], axis=0)
        dense_grad[l, :, 768:896] = last.T.astype(bf16)
        dispatch_copies(l, 1, 1)
        return carry

    lax.fori_loop(0, 2, backward, 0)

    for way, ref in ((0, out_ref), (1, grad_ref)):
        swap_copy(way).wait()
        ref[1 - s] = swap_in[way].astype(f32)
        for rel in range(2):
            return_copies(s, way, rel, 1)


def layers(*operands):
    shape = jax.ShapeDtypeStruct
    scratch = [
        pltpu.VMEM((3, ROWS, WIDTH), f32),
        pltpu.VMEM((2, ROWS, WIDTH), f32),
        pltpu.VMEM((2, ROWS, WIDTH), f32),
        pltpu.VMEM((2, ROWS, WIDTH), bf16),
        pltpu.VMEM((2, ROWS, 512), bf16),
        pltpu.VMEM((2, ROWS, 256), bf16),
        pltpu.VMEM((2, PART, WIDTH), f32),
        pltpu.VMEM((2, LOCAL * CAP, ROWS), bf16),
        pltpu.VMEM((2, E, ROWS), f32),
        pltpu.VMEM((2, LOCAL * CAP, 1), f32),
        pltpu.VMEM((2, 4, ROWS, WIDTH), bf16),
        pltpu.VMEM((2, 4, 3, PART, WIDTH), bf16),
        pltpu.VMEM((2, 4, ROWS, WIDTH), bf16),
        pltpu.VMEM((2, 1, 4, 8, ROWS), f32),
        pltpu.VMEM((E, ROWS), f32),
        pltpu.VMEM((2, 2, LOCAL * CAP, WIDTH), bf16),
        pltpu.VMEM((2 * LOCAL * CAP, WIDTH), bf16),
        pltpu.VMEM((2 * LOCAL * CAP, WIDTH), bf16),
        pltpu.VMEM((2 * LOCAL * CAP, FF), f32),
        pltpu.VMEM((2 * LOCAL * CAP, FF), f32),
        pltpu.VMEM((2 * LOCAL * CAP, FF), bf16),
        pltpu.VMEM((2, 2 * LOCAL * CAP, WIDTH), bf16),
        pltpu.VMEM((2, 2, LOCAL * CAP, WIDTH), bf16),
        pltpu.VMEM((2 * LOCAL * CAP, FF), bf16),
        pltpu.VMEM((2 * LOCAL * CAP, FF), bf16),
        pltpu.VMEM((8, ROWS), f32),
        pltpu.VMEM((PART, WIDTH), f32),
        pltpu.VMEM((2, 4, 8, WIDTH), f32),
        pltpu.VMEM((ROWS, WIDTH), f32),
        pltpu.VMEM((ROWS, 512), bf16),
        pltpu.VMEM((2, ROWS, WIDTH), bf16),
        pltpu.VMEM((2, ROWS, WIDTH), bf16),
        pltpu.SemaphoreType.DMA((2, 4, 3)),
        pltpu.SemaphoreType.DMA((2, 4, 3)),
        pltpu.SemaphoreType.DMA((2, 4, 3)),
        pltpu.SemaphoreType.DMA((2, 4, 3)),
        pltpu.SemaphoreType.DMA((2, 2, 3)),
        pltpu.SemaphoreType.DMA((2, 2, 3)),
        pltpu.SemaphoreType.DMA((2, 2, 8)),
        pltpu.SemaphoreType.DMA((2, 16)),
        pltpu.SemaphoreType.DMA((2, 16)),
        pltpu.SemaphoreType.DMA((2, 2, 8)),
        pltpu.SemaphoreType.DMA((2,)),
        pltpu.SemaphoreType.DMA((2,)),
    ]
    return pl.pallas_call(
        body,
        out_shape=(
            shape((2, ROWS, WIDTH), f32),
            shape((2, ROWS, WIDTH), f32),
            shape((2, WIDTH, DENSE), bf16),
            shape((3, WIDTH, FF), bf16),
        ),
        in_specs=[pl.BlockSpec(memory_space=pltpu.VMEM)] * 8,
        out_specs=tuple(pl.BlockSpec(memory_space=pltpu.VMEM) for _ in range(4)),
        scratch_shapes=scratch,
        compiler_params=pltpu.CompilerParams(
            collective_id=0, has_side_effects=True, vmem_limit_bytes=60 * 1024 * 1024
        ),
        name="layers",
    )(*operands)


def doc_tables(lengths):
    doc_ends = jnp.cumsum(lengths)
    doc_starts = doc_ends - lengths
    places = jnp.arange(ROWS, dtype=jnp.int32)
    segment = jnp.sum((places[:, None] >= doc_ends[None, :]).astype(jnp.int32), axis=1)
    owners = segment[:, None] == jnp.arange(lengths.shape[0], dtype=jnp.int32)[None, :]
    offset = places - jnp.sum(jnp.where(owners, doc_starts[None, :], 0), axis=1)
    visible = (segment[:, None] == segment[None, :]) & (places[None, :] <= places[:, None])
    half_dim = HEAD_SIZE // 2
    frequency = rope_base ** (-2.0 * jnp.arange(half_dim, dtype=f32) / HEAD_SIZE)
    angles = offset.astype(f32)[:, None] * frequency[None, :]
    cos, sin = jnp.cos(angles), jnp.sin(angles)
    return (
        jnp.concatenate([cos] * 4, axis=1),
        jnp.concatenate([-sin, sin, -sin, sin], axis=1),
        visible.astype(f32),
    )


def local(
    boundary,
    doc_lengths,
    routes,
    norm_gains,
    w_query,
    key_value_weight,
    w_out,
    w_router,
    w_gateup,
    w_down,
):
    s = lax.axis_index("section")
    low = s == 0
    swap = [(0, 1), (1, 0)]

    def exchanged(pair):
        own = jnp.where(low, pair[0], pair[1])
        sent = jnp.where(low, pair[1], pair[0])
        got = lax.ppermute(sent, "section", swap)
        return jnp.where(low, own, got), jnp.where(low, got, own)

    first_x, cotangent = exchanged(boundary[0])
    routes_here = jnp.stack(exchanged(jnp.swapaxes(routes[0], 1, 2)))
    cos, sin, seen = doc_tables(jnp.where(low, doc_lengths[0, 0], doc_lengths[1, 0]))

    depth = w_query.shape[1]
    piece = jnp.concatenate(
        [
            w_query[0],
            key_value_weight[0, 0],
            key_value_weight[0, 1],
            w_out[0].T,
            w_router[0],
            norm_gains[0].T,
            jnp.zeros((depth, DENSE - 802), bf16),
        ],
        axis=1,
    )
    dense = lax.all_gather(piece, ("section", "dp"), axis=0, tiled=True)
    dense = dense.reshape(2, WIDTH, DENSE)

    own = jnp.concatenate(
        [jnp.swapaxes(w_gateup[0], 0, 1), jnp.swapaxes(w_down[0], 1, 2)[:, None]], axis=1
    )
    own = own.reshape(4, 1, 2, 4, 3, 64, 128)
    own = jnp.broadcast_to(own, (4, 2, 2, 4, 3, 64, 128)).reshape(64, 3, 64, 128)
    arrived = lax.all_to_all(own, ("tensor", "dp"), split_axis=0, concat_axis=0, tiled=True)
    experts = arrived.reshape(4, 16, 3, 64, 128).transpose(2, 1, 3, 0, 4).reshape(3, WIDTH, FF)

    outs, grads, dense_grad, expert_grad = layers(
        dense, experts, first_x, cotangent, routes_here, cos, sin, seen
    )

    parts = lax.all_to_all(
        dense_grad.reshape(32, 64, DENSE), ("section", "dp"), split_axis=0, concat_axis=0, tiled=True
    )
    parts = jnp.sum(parts.astype(f32), axis=0)
    pieces = expert_grad.reshape(3, 16, 64, 4, 128).transpose(3, 1, 0, 2, 4).reshape(64, 3, 64, 128)
    pieces = lax.all_to_all(pieces, ("tensor", "dp"), split_axis=0, concat_axis=0, tiled=True)
    pieces = jnp.sum(pieces.reshape(4, 2, 8, 3, 64, 128).astype(f32), axis=1)
    pieces = pieces.reshape(E, 3, 64, 128)
    return (
        outs[None],
        grads[None],
        parts[:, 800:802].T[None],
        parts[:, 0:256][None],
        jnp.stack([parts[:, 256:384], parts[:, 384:512]])[None],
        parts[:, 512:768].T[None],
        parts[:, 768:800][None],
        jnp.swapaxes(pieces[:, 0:2], 0, 1)[None],
        jnp.swapaxes(pieces[:, 2], 1, 2)[None],
    )


def solution(mesh):
    placed = (
        P("section", None, "dp", None),
        P(None, "dp", None),
        P("section", None, "dp", None),
        P("section", None, "dp"),
        P("section", "dp", "tensor"),
        P("section", None, "dp", "tensor"),
        P("section", "tensor", "dp"),
        P("section", "dp", None),
        P("section", None, None, "dp", "tensor"),
        P("section", None, "tensor", "dp"),
    )
    return jax.shard_map(
        local,
        mesh=mesh,
        in_specs=placed,
        out_specs=(
            P("section", None, "dp", None),
            P("section", None, "dp", None),
            P("section", None, "dp"),
            P("section", "dp", "tensor"),
            P("section", None, "dp", "tensor"),
            P("section", "tensor", "dp"),
            P("section", "dp", None),
            P("section", None, None, "dp", "tensor"),
            P("section", None, "tensor", "dp"),
        ),
        check_vma=False,
    )
```

```python
import math

import jax
import jax.numpy as jnp
from jax import lax
from jax.experimental import pallas as pl
from jax.experimental.pallas import tpu as pltpu
from jax.sharding import PartitionSpec as P

HEAD_SIZE = 64
E = 32
TOPK = 8
CAP = 48
ROWS = 128
WIDTH = 1024
FF = 512
PART = 32
LOCAL = 8
DENSE = 896

epsilon = 1e-06
rope_base = 10000.0
masked_score = -1e30
f32 = jnp.float32
bf16 = jnp.bfloat16
MESH = pl.DeviceIdType.MESH


def dot(a, b):
    return lax.dot_general(a, b, (((1,), (0,)), ((), ())), preferred_element_type=f32)


def dot_nt(a, b):
    return lax.dot_general(a, b, (((1,), (1,)), ((), ())), preferred_element_type=f32)


def dot_tn(a, b):
    return lax.dot_general(a, b, (((0,), (0,)), ((), ())), preferred_element_type=f32)


def scale_of(values):
    return lax.rsqrt(jnp.mean(values * values, axis=1, keepdims=True) + epsilon)


def norm_back(values, gain_row, upstream):
    scale = scale_of(values)
    weighted = upstream * gain_row
    inner = jnp.mean(weighted * values, axis=1, keepdims=True)
    back = scale * weighted - values * (scale * scale * scale * inner)
    return back, jnp.sum(upstream * values * scale, axis=0, keepdims=True)


def low_lanes():
    return lax.broadcasted_iota(jnp.int32, (ROWS, 128), 1) < 64


def turn(chunk, cos, sin):
    place = lax.broadcasted_iota(jnp.int32, (ROWS, 128), 1) % 64
    swapped = jnp.where(place < 32, pltpu.roll(chunk, 96, 1), pltpu.roll(chunk, 32, 1))
    return chunk * cos + swapped * sin


def doubled(both):
    wide = both.astype(f32)
    other = pltpu.roll(wide, 64, 1)
    left = low_lanes()
    return (
        jnp.where(left, wide, other).astype(bf16),
        jnp.where(left, other, wide).astype(bf16),
    )


def half(chunk, which):
    left = low_lanes()
    keep = left if which == 0 else jnp.logical_not(left)
    return jnp.where(keep, chunk, jnp.zeros_like(chunk))


def soft(query_half, keys, seen):
    scores = dot_nt(query_half, keys) * HEAD_SIZE ** (-0.5)
    scores = jnp.where(seen, scores, masked_score)
    raised = jnp.exp(scores - jnp.max(scores, axis=1, keepdims=True))
    return raised / jnp.sum(raised, axis=1, keepdims=True)


def body(
    lengths, piece, own, boundary, routes_own,
    out_ref, grad_ref, parts, pieces,
    dense, experts, dense_grad, expert_grad, other, routes, cos_ref, sin_ref, seen_ref,
    xin, uin, turned, first_in, qkv, mixed, middle, chosen, chance, slot_gate,
    rs_send, rs_recv, ag, small, slots, packed, x_rows, og_rows, gate_s, up_s, hid_s,
    y_rows, ret, gg_low, ug_low, gate_grads, resid, gains, router_back, dqkv, swap_out, swap_in,
    rs_ss, rs_rs, ag_ss, ag_rs, sm_ss, sm_rs, d_ss, d_rs, r_ss, r_rs, w_ss, w_rs,
    a_ss, a_rs, b_ss, b_rs, e_ss, e_rs, g_ss, g_rs, p_ss, p_rs,
):
    s = lax.axis_index("section")
    x = lax.axis_index("tensor")
    d = lax.axis_index("dp")
    z, y = d // 4, d % 4
    zz = z % 2
    mine = zz * 4 + y
    rows_mine = pl.ds(pl.multiple_of(x * PART, PART), PART)
    experts_mine = pl.ds(pl.multiple_of(x * LOCAL, LOCAL), LOCAL)
    near = [(kz, ky) for kz in range(2) for ky in range(4)]

    def spot(kz, ky):
        z2, y2 = (zz + kz) % 2, (y + ky) % 4
        return z2 * 4 + y2, ((z // 2) * 2 + z2) * 4 + y2

    barrier = pltpu.get_barrier_semaphore()

    def greet(k, carry):
        there, at = (x + k // 16) % 4, (d + k % 16) % 16

        @pl.when(k > 0)
        def _():
            pl.semaphore_signal(
                barrier, inc=1, device_id={"tensor": there, "dp": at}, device_id_type=MESH
            )

        @pl.when(k < 16)
        def _():
            pl.semaphore_signal(
                barrier, inc=1, device_id={"section": 1 - s, "dp": at}, device_id_type=MESH
            )

        return carry

    lax.fori_loop(0, 64, greet, 0)

    row = lax.broadcasted_iota(jnp.int32, (ROWS, 128), 0)
    lane = lax.broadcasted_iota(jnp.int32, (ROWS, 128), 1)
    start, row_doc, lane_doc, end = 0, 0, 0, 0
    for k in range(3):
        size = lengths[s, k]
        end = end + size
        start = start + jnp.where(row >= end, size, 0)
        row_doc = row_doc + jnp.where(row >= end, 1, 0)
        lane_doc = lane_doc + jnp.where(lane >= end, 1, 0)
    step = (lane % 32).astype(f32) * (-2.0 / HEAD_SIZE * math.log(rope_base))
    angles = (row - start).astype(f32) * jnp.exp(step)
    sine = jnp.sin(angles)
    cos_ref[...] = jnp.cos(angles)
    sin_ref[...] = jnp.where(lane % 64 < 32, -sine, sine)
    seen_ref[...] = jnp.where((row_doc == lane_doc) & (lane <= row), 1.0, 0.0)

    pl.semaphore_wait(barrier, 79)

    def remote(src, dst, send, recv, device):
        return pltpu.make_async_remote_copy(
            src_ref=src, dst_ref=dst, send_sem=send, recv_sem=recv,
            device_id=device, device_id_type=MESH,
        )

    def scatter_copies(l, j):
        copies = []
        for k in range(1, 4):
            p = (x + k) % 4
            src = rs_send.at[l, j, pl.ds(pl.multiple_of(p * PART, PART), PART)]
            copies.append(
                remote(src, rs_recv.at[l, j, k - 1], rs_ss.at[l, j, k - 1],
                       rs_rs.at[l, j, k - 1], {"tensor": p})
            )
        return copies

    def scatter_start(l, j, partial):
        rs_send[l, j] = partial.astype(bf16)
        for copy in scatter_copies(l, j):
            copy.start()

    def scatter_end(l, j):
        for copy in scatter_copies(l, j):
            copy.wait()
        total = rs_send[l, j, rows_mine].astype(f32)
        for k in range(3):
            total = total + rs_recv[l, j, k].astype(f32)
        return total

    def gather_copies(l, j):
        copies = []
        for k in range(1, 4):
            ref = ag.at[l, j, rows_mine]
            copies.append(
                remote(ref, ref, ag_ss.at[l, j, k - 1], ag_rs.at[l, j, k - 1],
                       {"tensor": (x + k) % 4})
            )
        return copies

    def gather_start(l, j, rows):
        ag[l, j, rows_mine] = rows.astype(bf16)
        for copy in gather_copies(l, j):
            copy.start()

    def gather_end(l, j):
        for copy in gather_copies(l, j):
            copy.wait()

    def small_copies(l, j):
        copies = []
        for k in range(1, 4):
            ref = small.at[l, j, x]
            copies.append(
                remote(ref, ref, sm_ss.at[l, j, k - 1], sm_rs.at[l, j, k - 1],
                       {"tensor": (x + k) % 4})
            )
        return copies

    def block(index):
        return pl.ds(pl.multiple_of(index * CAP, CAP), CAP)

    def dispatch_copies(l, way, act):
        rel = (s + l) % 2
        target = x_rows if way == 0 else og_rows
        for kz, ky in near:
            i, peer = spot(kz, ky)
            n = kz * 4 + ky
            src = packed.at[l, way, block(i)]
            dst = target.at[block(rel * 8 + mine)]
            far = remote(src, dst, d_ss.at[l, way, n], d_rs.at[way, rel * 8 + n],
                         {"section": l, "dp": peer})
            if n == 0:
                @pl.when(s == l)
                def _():
                    if act == 0:
                        pltpu.make_async_copy(src, dst, d_rs.at[way, 0]).start()

                @pl.when(s != l)
                def _():
                    if act == 0:
                        far.start()
                    else:
                        far.wait_send()
            elif act == 0:
                far.start()
            else:
                far.wait_send()

    def dispatch_arrived(way, rel):
        target = x_rows if way == 0 else og_rows
        for n in range(8):
            dst = target.at[block(rel * 8 + n)]
            src = packed.at[0, way, block(n)]
            if rel == 0 and n == 0:
                pltpu.make_async_copy(
                    packed.at[0, way, block(mine)], target.at[block(mine)], d_rs.at[way, 0]
                ).wait()
            else:
                remote(src, dst, d_ss.at[0, way, n], d_rs.at[way, rel * 8 + n],
                       {"dp": spot(0, 1)[1]}).wait_recv()

    def return_copies(l, way, rel, act):
        for kz, ky in near:
            i, peer = spot(kz, ky)
            n = kz * 4 + ky
            src = y_rows.at[way, block(rel * 8 + i)]
            dst = ret.at[l, way, block(mine)]
            if rel == 0 and n == 0:
                if act == 0:
                    pltpu.make_async_copy(src, dst, r_rs.at[l, way, 0]).start()
                continue
            far = remote(src, dst, r_ss.at[way, rel * 8 + n], r_rs.at[l, way, n],
                         {"section": (s + rel) % 2, "dp": peer})
            if act == 0:
                far.start()
            else:
                far.wait_send()

    def return_arrived(l, way):
        for kz, ky in near:
            i, peer = spot(kz, ky)
            n = kz * 4 + ky
            src = y_rows.at[way, block(n)]
            dst = ret.at[l, way, block(i)]
            far = remote(src, dst, r_ss.at[way, n], r_rs.at[l, way, n],
                         {"section": 1 - s, "dp": peer})
            if n == 0:
                @pl.when(s == l)
                def _():
                    pltpu.make_async_copy(src, dst, r_rs.at[l, way, 0]).wait()

                @pl.when(s != l)
                def _():
                    far.wait_recv()
            else:
                far.wait_recv()

    def swap_copy(way):
        return remote(swap_out.at[way], swap_in.at[way], w_ss.at[way], w_rs.at[way],
                      {"section": 1 - s})

    def keep_result(way, l, ref):
        @pl.when(s == l)
        def _():
            ref[s] = ag[l, 1 + 2 * way].astype(f32)

        @pl.when(s != l)
        def _():
            swap_out[way] = ag[l, 1 + 2 * way]
            swap_copy(way).start()

    def block64(index):
        return pl.ds(pl.multiple_of(index * 64, 64), 64)

    def block128(index):
        return pl.ds(pl.multiple_of(index * 128, 128), 128)

    left, right = slice(0, 512), slice(512, DENSE)

    def along_y(k):
        return {"dp": z * 4 + (y + k) % 4}

    def along_z(k):
        return {"dp": ((z + k) % 4) * 4 + y}

    def spread_copies(part, phase):
        copies = []
        for k in range(1, 4):
            if part == 0:
                ref = dense.at[s, z, y, :, left] if phase == 0 else dense.at[s, z, :, :, left]
                device = along_y(k) if phase == 0 else along_z(k)
            else:
                ref = dense.at[s, z, y, :, right] if phase == 0 else dense.at[s, :, y, :, right]
                device = along_z(k) if phase == 0 else along_y(k)
            n = k - 1
            copies.append(
                remote(ref, ref, a_ss.at[part, phase, n], a_rs.at[part, phase, n], device)
            )
        return copies

    def sibling_copy(part, k, layer):
        if part == 0:
            ref = dense.at[layer, (z + k) % 4, :, :, left]
        else:
            ref = dense.at[layer, :, (y + k) % 4, :, right]
        return remote(ref, ref, b_ss.at[part, k], b_rs.at[part, k], {"section": 1 - s})

    def exchange_copies():
        return [
            remote(boundary.at[1 - s], other, b_ss.at[2, 0], b_rs.at[2, 0], {"section": 1 - s}),
            remote(routes_own.at[1 - s], routes.at[s], b_ss.at[2, 1], b_rs.at[2, 1],
                   {"section": 1 - s}),
        ]

    def expert_copy(k, local_only=False):
        there, at = (x + k // 16) % 4, (d + k % 16) % 16
        e = there * 8 + (at // 4 % 2) * 4 + at % 4
        src, dst = own.at[e], experts.at[:, block64(d), block128(x)]
        if local_only:
            return pltpu.make_async_copy(src, dst, e_rs.at[0])
        return remote(src, dst, e_ss.at[k], e_rs.at[k], {"tensor": there, "dp": at})

    def piece_copy(k, local_only=False):
        there, at = (x + k // 16) % 4, (d + k % 16) % 16
        src = expert_grad.at[:, block64(at), block128(there)]
        dst = pieces.at[z // 2, x * 8 + mine]
        if local_only:
            return pltpu.make_async_copy(src, dst, p_rs.at[0])
        return remote(src, dst, p_ss.at[k], p_rs.at[k], {"tensor": there, "dp": at})

    def all_but_own(copy, act):
        def one(k, carry):
            getattr(copy(k), act)()
            return carry

        lax.fori_loop(1, 64, one, 0)

    def push(copy):
        copy(0, True).start()
        all_but_own(copy, "start")

    def arrive(copy):
        copy(0, True).wait()
        all_but_own(copy, "wait_recv")

    wide = (slice(0, 512), slice(512, 768), slice(768, DENSE))

    def part_copy(l, c, k, rel, local_only=False):
        at = (d + k) % 16
        src = dense_grad.at[l, block64(at), wide[c]]
        dst = parts.at[rel * 16 + d, :, wide[c]]
        if local_only:
            return pltpu.make_async_copy(src, dst, g_rs.at[c, 0])
        return remote(src, dst, g_ss.at[l, c, k], g_rs.at[c, rel * 16 + k],
                      {"section": l, "dp": at})

    def part_push(l, c):
        rel = (s + l) % 2

        @pl.when(s == l)
        def _():
            part_copy(l, c, 0, 0, True).start()

        @pl.when(s != l)
        def _():
            part_copy(l, c, 0, 1).start()

        def one(k, carry):
            part_copy(l, c, k, rel).start()
            return carry

        lax.fori_loop(1, 16, one, 0)

    for copy in exchange_copies():
        copy.start()
    routes[s] = routes_own[s]
    dense[s, z, y] = piece[...]
    for part in range(2):
        for copy in spread_copies(part, 0):
            copy.start()

    @pl.when(s == 0)
    def _():
        xin[0] = boundary[0]

    @pl.when(s == 1)
    def _():
        uin[1] = boundary[1]

    for part in range(2):
        for copy in spread_copies(part, 0):
            copy.wait()
        for copy in spread_copies(part, 1):
            copy.start()
        sibling_copy(part, 0, s).start()

    @pl.when(s == 0)
    def _():
        push(expert_copy)

    for part in range(2):
        for k in range(3):
            spread_copies(part, 1)[k].wait()
            sibling_copy(part, 3 - k, s).start()

    @pl.when(s == 1)
    def _():
        for copy in exchange_copies()[:1]:
            copy.wait()
        xin[0] = other[...]

    def weight(l, low, high):
        return dense[l, :, :, :, low:high].reshape(WIDTH, high - low)

    def forward(l, carry):
        @pl.when(s != l)
        def _():
            for part in range(2):
                for k in range(4):
                    sibling_copy(part, k, s).wait()
            exchange_copies()[1].wait()

        turned[l] = weight(l, 768, 896).astype(f32).T
        values = xin[l]
        first = (values * scale_of(values) * turned[l, 32:33]).astype(bf16)
        first_in[l] = first
        made = dot(first, weight(l, 0, 512))
        cos, sin = cos_ref[...], sin_ref[...]
        for c in range(3):
            cut = slice(128 * c, 128 * c + 128)
            qkv[l, :, cut] = turn(made[:, cut], cos, sin).astype(bf16)
        qkv[l, :, 384:512] = made[:, 384:512].astype(bf16)
        seen = seen_ref[...] > 0
        keys = doubled(qkv[l, :, 256:384])
        vals = doubled(qkv[l, :, 384:512])
        for c in range(2):
            cut = slice(128 * c, 128 * c + 128)
            query = qkv[l, :, cut]
            got = [
                dot(soft(half(query, b), keys[c], seen).astype(bf16), vals[c]) for b in range(2)
            ]
            mixed[l, :, cut] = jnp.where(low_lanes(), got[0], got[1]).astype(bf16)
        scatter_start(l, 0, dot_nt(mixed[l], weight(l, 512, 768)))

        @pl.when((s == 1) & (l == 0))
        def _():
            push(expert_copy)

        experts_iota = lax.broadcasted_iota(jnp.int32, (E, ROWS), 0)
        named = jnp.zeros((E, ROWS), f32)
        for k in range(TOPK):
            named = named + (experts_iota == routes[l, k:k + 1]).astype(f32)
        before = (
            lax.broadcasted_iota(jnp.int32, (ROWS, ROWS), 0)
            < lax.broadcasted_iota(jnp.int32, (ROWS, ROWS), 1)
        ).astype(bf16)
        place = dot(named.astype(bf16), before)
        slots[...] = jnp.where(named > 0, place, -1.0)
        place = slots[experts_mine]
        slot_iota = lax.broadcasted_iota(jnp.int32, (CAP, ROWS), 0).astype(f32)
        for i in range(LOCAL):
            chosen[l, CAP * i:CAP * i + CAP] = (slot_iota == place[i:i + 1]).astype(bf16)

        center = xin[l, rows_mine] + scatter_end(l, 0)
        middle[l] = center
        gather_start(l, 0, center * scale_of(center) * turned[l, 33:34])
        gather_end(l, 0)

        second = ag[l, 0]
        packed[l, 0] = dot(chosen[l], second).astype(bf16)
        dispatch_copies(l, 0, 0)
        logits = dot_nt(turned[l, 0:32].astype(bf16), second)
        logits = jnp.where(named > 0, logits, masked_score)
        raised = jnp.where(named > 0, jnp.exp(logits - jnp.max(logits, axis=0, keepdims=True)), 0.0)
        chance[l] = raised / jnp.sum(raised, axis=0, keepdims=True)
        gate = chance[l, experts_mine]
        for i in range(LOCAL):
            cut = slice(CAP * i, CAP * i + CAP)
            weighted = chosen[l, cut].astype(f32) * gate[i:i + 1]
            slot_gate[l, cut] = jnp.sum(weighted, axis=1, keepdims=True)

        @pl.when(s == l)
        def _():
            arrive(expert_copy)
            for rel in range(2):
                dispatch_arrived(0, rel)
                cut = slice(384 * rel, 384 * rel + 384)
                rows = x_rows[cut]
                gate_part = dot(rows, experts[0])
                up_part = dot(rows, experts[1])
                gate_s[cut] = gate_part
                up_s[cut] = up_part
                hidden = (gate_part / (1.0 + jnp.exp(-gate_part)) * up_part).astype(bf16)
                hid_s[cut] = hidden
                y_rows[0, cut] = dot_nt(hidden, experts[2]).astype(bf16)
                return_copies(l, 0, rel, 0)

        return_arrived(l, 0)
        scaled = ret[l, 0].astype(f32) * slot_gate[l]
        scatter_start(l, 1, dot_tn(chosen[l], scaled.astype(bf16)))
        gather_start(l, 1, middle[l] + scatter_end(l, 1))
        gather_end(l, 1)
        xin[l + 1] = ag[l, 1].astype(f32)
        keep_result(0, l, out_ref)
        dispatch_copies(l, 0, 1)
        return carry

    lax.fori_loop(0, 2, forward, 0)

    @pl.when(s == 0)
    def _():
        for copy in exchange_copies()[:1]:
            copy.wait()
        uin[1] = other[...]

    def backward(step, carry):
        l = 1 - step
        upstream = uin[l].astype(bf16)
        spread = dot(chosen[l], upstream)
        packed[l, 1] = (spread * slot_gate[l]).astype(bf16)
        dispatch_copies(l, 1, 0)
        inner = jnp.sum(spread * ret[l, 0].astype(f32), axis=1, keepdims=True)
        for i in range(LOCAL):
            cut = slice(CAP * i, CAP * i + CAP)
            row = jnp.sum(chosen[l, cut].astype(f32) * inner[cut], axis=0, keepdims=True)
            gate_grads[i:i + 1] = row
        small[l, 0, x, 0:8] = gate_grads[...]
        for copy in small_copies(l, 0):
            copy.start()

        @pl.when(s == l)
        def _():
            for rel in range(2):
                dispatch_arrived(1, rel)
                cut = slice(384 * rel, 384 * rel + 384)
                hidden_grad = dot(og_rows[cut], experts[2])
                gate_part = gate_s[cut]
                up_part = up_s[cut]
                sig = 1.0 / (1.0 + jnp.exp(-gate_part))
                gate_low = (
                    hidden_grad * up_part * sig * (1.0 + gate_part * (1.0 - sig))
                ).astype(bf16)
                up_low = (hidden_grad * gate_part * sig).astype(bf16)
                gg_low[cut] = gate_low
                ug_low[cut] = up_low
                back = dot_nt(gate_low, experts[0]) + dot_nt(up_low, experts[1])
                y_rows[1, cut] = back.astype(bf16)
                return_copies(l, 1, rel, 0)
            expert_grad[0] = dot_tn(x_rows[...], gg_low[...]).astype(bf16)
            expert_grad[1] = dot_tn(x_rows[...], ug_low[...]).astype(bf16)
            expert_grad[2] = dot_tn(og_rows[...], hid_s[...]).astype(bf16)
            push(piece_copy)

        for copy in small_copies(l, 0):
            copy.wait()
        gate = chance[l]
        gate_total = jnp.concatenate([small[l, 0, p, 0:8] for p in range(4)], axis=0)
        picked = gate * (gate_total - jnp.sum(gate * gate_total, axis=0, keepdims=True))
        logit_low = picked.astype(bf16)
        router_back[...] = dot_tn(logit_low, turned[l, 0:32].astype(bf16))
        return_arrived(l, 1)
        scatter_start(l, 2, dot_tn(chosen[l], ret[l, 1]))
        router_grad = dot(logit_low, ag[l, 0])
        arrived = scatter_end(l, 2) + router_back[rows_mine]
        back, gain_two = norm_back(middle[l], turned[l, 33:34], arrived)
        kept = uin[l, rows_mine] + back
        resid[...] = kept
        gather_start(l, 2, kept)
        gather_end(l, 2)

        branch = ag[l, 2]
        dense_grad[l, :, 512:768] = dot_tn(branch, mixed[l]).astype(bf16)
        part_push(l, 1)
        mixed_grad = dot(branch, weight(l, 512, 768)).astype(bf16)
        seen = seen_ref[...] > 0
        cos, sin = cos_ref[...], -sin_ref[...]
        left = low_lanes()
        keys = doubled(qkv[l, :, 256:384])
        vals = doubled(qkv[l, :, 384:512])
        key_grads, value_grads = [], []
        for c in range(2):
            cut = slice(128 * c, 128 * c + 128)
            query, above = qkv[l, :, cut], mixed_grad[:, cut]
            parts, key_grad, value_grad = [], 0.0, 0.0
            for b in range(2):
                query_half, above_half = half(query, b), half(above, b)
                prob = soft(query_half, keys[c], seen)
                value_grad = value_grad + dot_tn(prob.astype(bf16), above_half)
                prob_grad = dot_nt(above_half, vals[c])
                mean = jnp.sum(prob * prob_grad, axis=1, keepdims=True)
                score_low = (prob * (prob_grad - mean)).astype(bf16)
                parts.append(dot(score_low, keys[c]))
                key_grad = key_grad + dot_tn(score_low, query_half)
            query_grad = jnp.where(left, parts[0], parts[1]) * HEAD_SIZE ** (-0.5)
            dqkv[:, cut] = turn(query_grad, cos, sin).astype(bf16)
            key_grads.append(key_grad + pltpu.roll(key_grad, 64, 1))
            value_grads.append(value_grad + pltpu.roll(value_grad, 64, 1))
        key_grad = jnp.where(left, key_grads[0], key_grads[1]) * HEAD_SIZE ** (-0.5)
        dqkv[:, 256:384] = turn(key_grad, cos, sin).astype(bf16)
        dqkv[:, 384:512] = jnp.where(left, value_grads[0], value_grads[1]).astype(bf16)
        scatter_start(l, 3, dot_nt(dqkv[...], weight(l, 0, 512)))
        dense_grad[l, :, 0:512] = dot_tn(first_in[l], dqkv[...]).astype(bf16)
        part_push(l, 0)
        back, gain_one = norm_back(xin[l, rows_mine], turned[l, 32:33], scatter_end(l, 3))
        gather_start(l, 3, resid[...] + back)
        gains[l, x, 0:1] = gain_one
        gains[l, x, 1:2] = gain_two
        for k in range(1, 4):
            ref = gains.at[l, x]
            remote(ref, ref, sm_ss.at[l, 1, k - 1], sm_rs.at[l, 1, k - 1],
                   {"tensor": (x + k) % 4}).start()
        gather_end(l, 3)
        uin[1 - l] = ag[l, 3].astype(f32)
        keep_result(1, l, grad_ref)
        for k in range(1, 4):
            ref = gains.at[l, x]
            remote(ref, ref, sm_ss.at[l, 1, k - 1], sm_rs.at[l, 1, k - 1],
                   {"tensor": (x + k) % 4}).wait()
        total = gains[l, 0] + gains[l, 1] + gains[l, 2] + gains[l, 3]
        last = jnp.concatenate([router_grad, total, jnp.zeros((88, WIDTH), f32)], axis=0)
        dense_grad[l, :, 768:896] = last.T.astype(bf16)
        part_push(l, 2)
        dispatch_copies(l, 1, 1)
        return carry

    lax.fori_loop(0, 2, backward, 0)

    for way, ref in ((0, out_ref), (1, grad_ref)):
        swap_copy(way).wait()
        ref[1 - s] = swap_in[way].astype(f32)
        for rel in range(2):
            return_copies(s, way, rel, 1)
    all_but_own(expert_copy, "wait_send")
    all_but_own(piece_copy, "wait_send")
    arrive(piece_copy)
    for c in range(3):
        part_copy(s, c, 0, 0, True).wait()
        part_copy(1 - s, c, 0, 1).wait()

        def one(k, carry):
            part_copy(s, c, k, 0).wait()
            part_copy(1 - s, c, k, 1).wait()
            return carry

        lax.fori_loop(1, 16, one, 0)


def layers(*operands):
    shape = jax.ShapeDtypeStruct
    scratch = [
        pltpu.VMEM((2, 4, 4, 64, DENSE), bf16),
        pltpu.VMEM((3, WIDTH, FF), bf16),
        pltpu.VMEM((2, WIDTH, DENSE), bf16),
        pltpu.VMEM((3, WIDTH, FF), bf16),
        pltpu.VMEM((ROWS, WIDTH), f32),
        pltpu.VMEM((2, TOPK, ROWS), jnp.int32),
        pltpu.VMEM((ROWS, 128), f32),
        pltpu.VMEM((ROWS, 128), f32),
        pltpu.VMEM((ROWS, 128), f32),
        pltpu.VMEM((3, ROWS, WIDTH), f32),
        pltpu.VMEM((2, ROWS, WIDTH), f32),
        pltpu.VMEM((2, ROWS, WIDTH), f32),
        pltpu.VMEM((2, ROWS, WIDTH), bf16),
        pltpu.VMEM((2, ROWS, 512), bf16),
        pltpu.VMEM((2, ROWS, 256), bf16),
        pltpu.VMEM((2, PART, WIDTH), f32),
        pltpu.VMEM((2, LOCAL * CAP, ROWS), bf16),
        pltpu.VMEM((2, E, ROWS), f32),
        pltpu.VMEM((2, LOCAL * CAP, 1), f32),
        pltpu.VMEM((2, 4, ROWS, WIDTH), bf16),
        pltpu.VMEM((2, 4, 3, PART, WIDTH), bf16),
        pltpu.VMEM((2, 4, ROWS, WIDTH), bf16),
        pltpu.VMEM((2, 1, 4, 8, ROWS), f32),
        pltpu.VMEM((E, ROWS), f32),
        pltpu.VMEM((2, 2, LOCAL * CAP, WIDTH), bf16),
        pltpu.VMEM((2 * LOCAL * CAP, WIDTH), bf16),
        pltpu.VMEM((2 * LOCAL * CAP, WIDTH), bf16),
        pltpu.VMEM((2 * LOCAL * CAP, FF), f32),
        pltpu.VMEM((2 * LOCAL * CAP, FF), f32),
        pltpu.VMEM((2 * LOCAL * CAP, FF), bf16),
        pltpu.VMEM((2, 2 * LOCAL * CAP, WIDTH), bf16),
        pltpu.VMEM((2, 2, LOCAL * CAP, WIDTH), bf16),
        pltpu.VMEM((2 * LOCAL * CAP, FF), bf16),
        pltpu.VMEM((2 * LOCAL * CAP, FF), bf16),
        pltpu.VMEM((8, ROWS), f32),
        pltpu.VMEM((PART, WIDTH), f32),
        pltpu.VMEM((2, 4, 8, WIDTH), f32),
        pltpu.VMEM((ROWS, WIDTH), f32),
        pltpu.VMEM((ROWS, 512), bf16),
        pltpu.VMEM((2, ROWS, WIDTH), bf16),
        pltpu.VMEM((2, ROWS, WIDTH), bf16),
        pltpu.SemaphoreType.DMA((2, 4, 3)),
        pltpu.SemaphoreType.DMA((2, 4, 3)),
        pltpu.SemaphoreType.DMA((2, 4, 3)),
        pltpu.SemaphoreType.DMA((2, 4, 3)),
        pltpu.SemaphoreType.DMA((2, 2, 3)),
        pltpu.SemaphoreType.DMA((2, 2, 3)),
        pltpu.SemaphoreType.DMA((2, 2, 8)),
        pltpu.SemaphoreType.DMA((2, 16)),
        pltpu.SemaphoreType.DMA((2, 16)),
        pltpu.SemaphoreType.DMA((2, 2, 8)),
        pltpu.SemaphoreType.DMA((2,)),
        pltpu.SemaphoreType.DMA((2,)),
        pltpu.SemaphoreType.DMA((2, 2, 3)),
        pltpu.SemaphoreType.DMA((2, 2, 3)),
        pltpu.SemaphoreType.DMA((3, 4)),
        pltpu.SemaphoreType.DMA((3, 4)),
        pltpu.SemaphoreType.DMA((64,)),
        pltpu.SemaphoreType.DMA((64,)),
        pltpu.SemaphoreType.DMA((2, 3, 16)),
        pltpu.SemaphoreType.DMA((3, 32)),
        pltpu.SemaphoreType.DMA((64,)),
        pltpu.SemaphoreType.DMA((64,)),
    ]
    return pl.pallas_call(
        body,
        out_shape=(
            shape((2, ROWS, WIDTH), f32),
            shape((2, ROWS, WIDTH), f32),
            shape((32, 64, DENSE), bf16),
            shape((2, E, 3, 64, 128), bf16),
        ),
        in_specs=[
            pl.BlockSpec(memory_space=pltpu.SMEM),
            pl.BlockSpec(memory_space=pltpu.VMEM),
            pl.BlockSpec(memory_space=pl.ANY),
            pl.BlockSpec(memory_space=pltpu.VMEM),
            pl.BlockSpec(memory_space=pltpu.VMEM),
        ],
        out_specs=(
            pl.BlockSpec(memory_space=pltpu.VMEM),
            pl.BlockSpec(memory_space=pltpu.VMEM),
            pl.BlockSpec(memory_space=pl.ANY),
            pl.BlockSpec(memory_space=pl.ANY),
        ),
        scratch_shapes=scratch,
        compiler_params=pltpu.CompilerParams(
            collective_id=0, has_side_effects=True, vmem_limit_bytes=60 * 1024 * 1024
        ),
        name="layers",
    )(*operands)


def local(
    boundary,
    doc_lengths,
    routes,
    norm_gains,
    w_query,
    key_value_weight,
    w_out,
    w_router,
    w_gateup,
    w_down,
):
    depth = w_query.shape[1]
    piece = jnp.concatenate(
        [
            w_query[0],
            key_value_weight[0, 0],
            key_value_weight[0, 1],
            w_out[0].T,
            w_router[0],
            norm_gains[0].T,
            jnp.zeros((depth, DENSE - 802), bf16),
        ],
        axis=1,
    )
    own = jnp.concatenate(
        [jnp.swapaxes(w_gateup[0], 0, 1), jnp.swapaxes(w_down[0], 1, 2)[:, None]], axis=1
    )
    outs, grads, parts, pieces = layers(
        doc_lengths[:, 0], piece, own, boundary[0], jnp.swapaxes(routes[0], 1, 2)
    )
    parts = jnp.sum(parts.astype(f32), axis=0)
    pieces = jnp.sum(pieces.astype(f32), axis=0)
    return (
        outs[None],
        grads[None],
        parts[:, 800:802].T[None],
        parts[:, 0:256][None],
        jnp.stack([parts[:, 256:384], parts[:, 384:512]])[None],
        parts[:, 512:768].T[None],
        parts[:, 768:800][None],
        jnp.swapaxes(pieces[:, 0:2], 0, 1)[None],
        jnp.swapaxes(pieces[:, 2], 1, 2)[None],
    )


def solution(mesh):
    placed = (
        P("section", None, "dp", None),
        P(None, "dp", None),
        P("section", None, "dp", None),
        P("section", None, "dp"),
        P("section", "dp", "tensor"),
        P("section", None, "dp", "tensor"),
        P("section", "tensor", "dp"),
        P("section", "dp", None),
        P("section", None, None, "dp", "tensor"),
        P("section", None, "tensor", "dp"),
    )
    return jax.shard_map(
        local,
        mesh=mesh,
        in_specs=placed,
        out_specs=(
            P("section", None, "dp", None),
            P("section", None, "dp", None),
            P("section", None, "dp"),
            P("section", "dp", "tensor"),
            P("section", None, "dp", "tensor"),
            P("section", "tensor", "dp"),
            P("section", "dp", None),
            P("section", None, None, "dp", "tensor"),
            P("section", None, "tensor", "dp"),
        ),
        check_vma=False,
    )
```

```python
import math

import jax
import jax.numpy as jnp
from jax import lax
from jax.experimental import pallas as pl
from jax.experimental.pallas import tpu as pltpu
from jax.sharding import PartitionSpec as P

HEAD_SIZE = 64
E = 32
TOPK = 8
CAP = 48
ROWS = 128
WIDTH = 1024
FF = 512
PART = 32
LOCAL = 8
DENSE = 896

epsilon = 1e-06
rope_base = 10000.0
masked_score = -1e30
f32 = jnp.float32
bf16 = jnp.bfloat16
MESH = pl.DeviceIdType.MESH


def dot(a, b):
    return lax.dot_general(a, b, (((1,), (0,)), ((), ())), preferred_element_type=f32)


def dot_nt(a, b):
    return lax.dot_general(a, b, (((1,), (1,)), ((), ())), preferred_element_type=f32)


def dot_tn(a, b):
    return lax.dot_general(a, b, (((0,), (0,)), ((), ())), preferred_element_type=f32)


def unit(rows, columns, shift):
    row = lax.broadcasted_iota(jnp.int32, (rows, columns), 0)
    column = lax.broadcasted_iota(jnp.int32, (rows, columns), 1)
    return (row + shift == column).astype(bf16)


def scale_of(values):
    return lax.rsqrt(jnp.mean(values * values, axis=1, keepdims=True) + epsilon)


def norm_back(values, gain_row, upstream):
    scale = scale_of(values)
    weighted = upstream * gain_row
    inner = jnp.mean(weighted * values, axis=1, keepdims=True)
    back = scale * weighted - values * (scale * scale * scale * inner)
    return back, jnp.sum(upstream * values * scale, axis=0, keepdims=True)


def low_lanes():
    return lax.broadcasted_iota(jnp.int32, (ROWS, 128), 1) < 64


def turn(chunk, cos, sin):
    place = lax.broadcasted_iota(jnp.int32, (ROWS, 128), 1) % 64
    swapped = jnp.where(place < 32, pltpu.roll(chunk, 96, 1), pltpu.roll(chunk, 32, 1))
    return chunk * cos + swapped * sin


def doubled(both):
    wide = both.astype(f32)
    other = pltpu.roll(wide, 64, 1)
    left = low_lanes()
    return (
        jnp.where(left, wide, other).astype(bf16),
        jnp.where(left, other, wide).astype(bf16),
    )


def half(chunk, which):
    left = low_lanes()
    keep = left if which == 0 else jnp.logical_not(left)
    return jnp.where(keep, chunk, jnp.zeros_like(chunk))


def soft(query_half, keys, seen):
    scores = dot_nt(query_half, keys) * HEAD_SIZE ** (-0.5)
    scores = jnp.where(seen, scores, masked_score)
    raised = jnp.exp(scores - jnp.max(scores, axis=1, keepdims=True))
    return raised / jnp.sum(raised, axis=1, keepdims=True)


def body(
    lengths, query_own, keyval_own, out_own, router_own, gains_own, gateup_own, down_own,
    boundary, routes_own,
    out_ref, grad_ref, parts, pieces,
    own, dense, experts, dense_grad, shared, expert_grad, other, routes, cos_ref, sin_ref, seen_ref,
    xin, uin, turned, first_in, qkv, mixed, middle, chosen, chance, slot_gate,
    rs_send, rs_recv, ag, small, slots, packed, x_rows, og_rows, gate_s, up_s, hid_s,
    y_rows, ret, gg_low, ug_low, gate_grads, resid, gains, router_back, dqkv, swap_out, swap_in,
    rs_ss, rs_rs, ag_ss, ag_rs, sm_ss, sm_rs, d_ss, d_rs, r_ss, r_rs, w_ss, w_rs,
    a_ss, a_rs, b_ss, b_rs, e_ss, e_rs, g_ss, g_rs, p_ss, p_rs, h_ss, h_rs, c_ss,
):
    s = lax.axis_index("section")
    x = lax.axis_index("tensor")
    d = lax.axis_index("dp")
    z, y = d // 4, d % 4
    zz = z % 2
    mine = zz * 4 + y
    rows_mine = pl.ds(pl.multiple_of(x * PART, PART), PART)
    experts_mine = pl.ds(pl.multiple_of(x * LOCAL, LOCAL), LOCAL)
    near = [(kz, ky) for kz in range(2) for ky in range(4)]

    def spot(kz, ky):
        z2, y2 = (zz + kz) % 2, (y + ky) % 4
        return z2 * 4 + y2, ((z // 2) * 2 + z2) * 4 + y2

    barrier = pltpu.get_barrier_semaphore()

    def greet(k, carry):
        there, at = (x + k // 16) % 4, (d + k % 16) % 16

        @pl.when(k > 0)
        def _():
            pl.semaphore_signal(
                barrier, inc=1, device_id={"tensor": there, "dp": at}, device_id_type=MESH
            )

        return carry

    lax.fori_loop(0, 64, greet, 0)
    for kz, ky in near:
        pl.semaphore_signal(
            barrier, inc=1, device_id={"section": 1 - s, "dp": spot(kz, ky)[1]},
            device_id_type=MESH,
        )

    row = lax.broadcasted_iota(jnp.int32, (ROWS, 128), 0)
    lane = lax.broadcasted_iota(jnp.int32, (ROWS, 128), 1)
    start, row_doc, lane_doc, end = 0, 0, 0, 0
    for k in range(3):
        size = lengths[s, k]
        end = end + size
        start = start + jnp.where(row >= end, size, 0)
        row_doc = row_doc + jnp.where(row >= end, 1, 0)
        lane_doc = lane_doc + jnp.where(lane >= end, 1, 0)
    step = (lane % 32).astype(f32) * (-2.0 / HEAD_SIZE * math.log(rope_base))
    angles = (row - start).astype(f32) * jnp.exp(step)
    sine = jnp.sin(angles)
    cos_ref[...] = jnp.cos(angles)
    sin_ref[...] = jnp.where(lane % 64 < 32, -sine, sine)
    seen_ref[...] = jnp.where((row_doc == lane_doc) & (lane <= row), 1.0, 0.0)

    pl.semaphore_wait(barrier, 71)

    def remote(src, dst, send, recv, device):
        return pltpu.make_async_remote_copy(
            src_ref=src, dst_ref=dst, send_sem=send, recv_sem=recv,
            device_id=device, device_id_type=MESH,
        )

    def scatter_copies(l, j):
        copies = []
        for k in range(1, 4):
            p = (x + k) % 4
            src = rs_send.at[l, j, pl.ds(pl.multiple_of(p * PART, PART), PART)]
            copies.append(
                remote(src, rs_recv.at[l, j, k - 1], rs_ss.at[l, j, k - 1],
                       rs_rs.at[l, j, k - 1], {"tensor": p})
            )
        return copies

    def scatter_start(l, j, partial):
        rs_send[l, j] = partial.astype(bf16)
        for copy in scatter_copies(l, j):
            copy.start()

    def scatter_end(l, j):
        for copy in scatter_copies(l, j):
            copy.wait()
        total = rs_send[l, j, rows_mine].astype(f32)
        for k in range(3):
            total = total + rs_recv[l, j, k].astype(f32)
        return total

    def gather_copies(l, j):
        copies = []
        for k in range(1, 4):
            ref = ag.at[l, j, rows_mine]
            copies.append(
                remote(ref, ref, ag_ss.at[l, j, k - 1], ag_rs.at[l, j, k - 1],
                       {"tensor": (x + k) % 4})
            )
        return copies

    def gather_start(l, j, rows):
        ag[l, j, rows_mine] = rows.astype(bf16)
        for copy in gather_copies(l, j):
            copy.start()

    def gather_end(l, j):
        for copy in gather_copies(l, j):
            copy.wait()

    def small_copies(l, j):
        copies = []
        for k in range(1, 4):
            ref = small.at[l, j, x]
            copies.append(
                remote(ref, ref, sm_ss.at[l, j, k - 1], sm_rs.at[l, j, k - 1],
                       {"tensor": (x + k) % 4})
            )
        return copies

    def block(index):
        return pl.ds(pl.multiple_of(index * CAP, CAP), CAP)

    def dispatch_copies(l, way, act):
        rel = (s + l) % 2
        target = x_rows if way == 0 else og_rows
        for kz, ky in near:
            i, peer = spot(kz, ky)
            n = kz * 4 + ky
            src = packed.at[l, way, block(i)]
            dst = target.at[block(rel * 8 + mine)]
            far = remote(src, dst, d_ss.at[l, way, n], d_rs.at[way, rel * 8 + n],
                         {"section": l, "dp": peer})
            if n == 0:
                @pl.when(s == l)
                def _():
                    if act == 0:
                        pltpu.make_async_copy(src, dst, d_rs.at[way, 0]).start()

                @pl.when(s != l)
                def _():
                    if act == 0:
                        far.start()
                    else:
                        far.wait_send()
            elif act == 0:
                far.start()
            else:
                far.wait_send()

    def dispatch_arrived(way, rel):
        target = x_rows if way == 0 else og_rows

        def far(n):
            return remote(
                packed.at[0, way, block(n)], target.at[block(rel * 8 + n)],
                d_ss.at[0, way, n], d_rs.at[way, rel * 8 + n], {"dp": spot(0, 1)[1]},
            )

        @pl.when(rel == 0)
        def _():
            pltpu.make_async_copy(
                packed.at[0, way, block(mine)], target.at[block(mine)], d_rs.at[way, 0]
            ).wait()

        @pl.when(rel != 0)
        def _():
            far(0).wait_recv()

        for n in range(1, 8):
            far(n).wait_recv()

    def return_copies(l, way, rel, act):
        for kz, ky in near:
            i, peer = spot(kz, ky)
            n = kz * 4 + ky
            src = y_rows.at[way, block(rel * 8 + i)]
            dst = ret.at[l, way, block(mine)]
            def far():
                return remote(src, dst, r_ss.at[way, rel * 8 + n], r_rs.at[l, way, n],
                              {"section": (s + rel) % 2, "dp": peer})

            def go():
                if act == 0:
                    far().start()
                else:
                    far().wait_send()

            if n > 0:
                go()
            else:
                pl.when(rel != 0)(go)
                if act == 0:
                    @pl.when(rel == 0)
                    def _():
                        pltpu.make_async_copy(src, dst, r_rs.at[l, way, 0]).start()

    def return_arrived(l, way):
        for kz, ky in near:
            i, peer = spot(kz, ky)
            n = kz * 4 + ky
            src = y_rows.at[way, block(n)]
            dst = ret.at[l, way, block(i)]
            far = remote(src, dst, r_ss.at[way, n], r_rs.at[l, way, n],
                         {"section": 1 - s, "dp": peer})
            if n == 0:
                @pl.when(s == l)
                def _():
                    pltpu.make_async_copy(src, dst, r_rs.at[l, way, 0]).wait()

                @pl.when(s != l)
                def _():
                    far.wait_recv()
            else:
                far.wait_recv()

    def swap_copy(way):
        return remote(swap_out.at[way], swap_in.at[way], w_ss.at[way], w_rs.at[way],
                      {"section": 1 - s})

    def keep_result(way, l, ref):
        @pl.when(s == l)
        def _():
            ref[s] = ag[l, 1 + 2 * way]

        @pl.when(s != l)
        def _():
            swap_out[way] = ag[l, 1 + 2 * way]
            swap_copy(way).start()

    def block64(index):
        return pl.ds(pl.multiple_of(index * 64, 64), 64)

    def block128(index):
        return pl.ds(pl.multiple_of(index * 128, 128), 128)

    left, right = slice(0, 512), slice(512, DENSE)

    def along_y(k):
        return {"dp": z * 4 + (y + k) % 4}

    def along_z(k):
        return {"dp": ((z + k) % 4) * 4 + y}

    def spread_copies(part, phase):
        copies = []
        for k in range(1, 4):
            if part == 0:
                ref = dense.at[s, z, y, :, left] if phase == 0 else dense.at[s, z, :, :, left]
                device = along_y(k) if phase == 0 else along_z(k)
            else:
                ref = dense.at[s, z, y, :, right] if phase == 0 else dense.at[s, :, y, :, right]
                device = along_z(k) if phase == 0 else along_y(k)
            n = k - 1
            copies.append(
                remote(ref, ref, a_ss.at[part, phase, n], a_rs.at[part, phase, n], device)
            )
        return copies

    def sibling_copy(part, k, layer):
        if part == 0:
            ref = dense.at[layer, (z + k) % 4, :, :, left]
        else:
            ref = dense.at[layer, :, (y + k) % 4, :, right]
        return remote(ref, ref, b_ss.at[part, k], b_rs.at[part, k], {"section": 1 - s})

    def weight_copy(kind):
        src = gateup_own.at[kind] if kind < 2 else down_own
        return pltpu.make_async_copy(src, own.at[:, kind], c_ss.at[kind])

    def exchange_copies():
        return [
            remote(boundary.at[1 - s], other, b_ss.at[2, 0], b_rs.at[2, 0], {"section": 1 - s}),
            remote(routes_own.at[1 - s], routes.at[s], b_ss.at[2, 1], b_rs.at[2, 1],
                   {"section": 1 - s}),
        ]

    def expert_copy(k, local_only=False):
        there, at = (x + k // 16) % 4, (d + k % 16) % 16
        e = there * 8 + (at // 4 % 2) * 4 + at % 4
        src, dst = own.at[e], experts.at[:, block64(d), block128(x)]
        if local_only:
            return pltpu.make_async_copy(src, dst, e_rs.at[0])
        return remote(src, dst, e_ss.at[k], e_rs.at[k], {"tensor": there, "dp": at})

    def piece_copy(k, local_only=False):
        there, at = (x + k // 16) % 4, (d + k % 16) % 16
        src = expert_grad.at[:, block64(at), block128(there)]
        dst = pieces.at[z // 2, :, x * 8 + mine]
        if local_only:
            return pltpu.make_async_copy(src, dst, p_rs.at[0])
        return remote(src, dst, p_ss.at[k], p_rs.at[k], {"tensor": there, "dp": at})

    def all_but_own(copy, act, low=1, high=64):
        def one(n, carry):
            getattr(copy(n * 13 % 64), act)()
            return carry

        lax.fori_loop(low, high, one, 0)

    def push(copy, low, high):
        whole = isinstance(low, int) and low == 0
        if whole:
            copy(0, True).start()
        all_but_own(copy, "start", 1 if whole else low, high)

    def push_when(condition, copy, low, high):
        pl.when(condition)(lambda: push(copy, low, high))

    def arrive(copy):
        copy(0, True).wait()
        all_but_own(copy, "wait_recv")

    wide = (slice(0, 512), slice(512, 768), slice(768, DENSE))

    def part_copy(c, k, local_only=False):
        at = (d + k) % 16
        src = dense_grad.at[s, block64(at), wide[c]]
        dst = parts.at[d, :, wide[c]]
        if local_only:
            return pltpu.make_async_copy(src, dst, g_rs.at[c, 0])
        return remote(src, dst, g_ss.at[c, k], g_rs.at[c, k], {"dp": at})

    def share_copy(c):
        return remote(dense_grad.at[1 - s, :, wide[c]], shared.at[:, wide[c]],
                      h_ss.at[c], h_rs.at[c], {"section": 1 - s})

    def share(l, c):
        @pl.when(s != l)
        def _():
            share_copy(c).start()

    def part_push(l, c):
        @pl.when(s == l)
        def _():
            share_copy(c).wait_recv()
            both = dense_grad[l, :, wide[c]].astype(f32) + shared[:, wide[c]].astype(f32)
            dense_grad[l, :, wide[c]] = both.astype(bf16)
            part_copy(c, 0, True).start()

            def one(k, carry):
                part_copy(c, k).start()
                return carry

            lax.fori_loop(1, 16, one, 0)

    for copy in exchange_copies():
        copy.start()
    for kind in range(3):
        weight_copy(kind).start()
    routes[s] = routes_own[s]
    dense[s, z, y, :, 0:256] = query_own[...]
    dense[s, z, y, :, 256:384] = keyval_own[0]
    dense[s, z, y, :, 384:512] = keyval_own[1]
    dense[s, z, y, :, 512:768] = out_own[...]
    last = dot_tn(router_own[...], unit(E, 128, 0)) + dot_tn(gains_own[...], unit(2, 128, E))
    dense[s, z, y, :, 768:896] = last.astype(bf16)
    for part in range(2):
        for copy in spread_copies(part, 0):
            copy.start()


    @pl.when(s == 0)
    def _():
        xin[0] = boundary[0]

    @pl.when(s == 1)
    def _():
        uin[1] = boundary[1]

    for part in range(2):
        for copy in spread_copies(part, 0):
            copy.wait()
    for kind in range(3):
        weight_copy(kind).wait()

    def spread_start():
        for part in range(2):
            for copy in spread_copies(part, 1):
                copy.start()
            sibling_copy(part, 0, s).start()

    def spread_end():
        for part in range(2):
            for k in range(3):
                spread_copies(part, 1)[k].wait()
                sibling_copy(part, 3 - k, s).start()

    @pl.when(s == 0)
    def _():
        spread_start()
        push(expert_copy, 0, 64)
        spread_end()

    @pl.when(s == 1)
    def _():
        for copy in exchange_copies()[:1]:
            copy.wait()
        xin[0] = other[...]

    def weight(l, low, high):
        return dense[l, :, :, :, low:high].reshape(WIDTH, high - low)

    def forward(l, carry):
        @pl.when(s != l)
        def _():
            for part in range(2):
                for k in range(4):
                    sibling_copy(part, k, s).wait_recv()
            exchange_copies()[1].wait()

        turned[l] = weight(l, 768, 896).astype(f32).T
        values = xin[l]
        first = (values * scale_of(values) * turned[l, 32:33]).astype(bf16)
        first_in[l] = first
        made = dot(first, weight(l, 0, 512))
        cos, sin = cos_ref[...], sin_ref[...]
        for c in range(3):
            cut = slice(128 * c, 128 * c + 128)
            qkv[l, :, cut] = turn(made[:, cut], cos, sin).astype(bf16)
        qkv[l, :, 384:512] = made[:, 384:512].astype(bf16)
        seen = seen_ref[...] > 0
        keys = doubled(qkv[l, :, 256:384])
        vals = doubled(qkv[l, :, 384:512])
        for c in range(2):
            cut = slice(128 * c, 128 * c + 128)
            query = qkv[l, :, cut]
            got = [
                dot(soft(half(query, b), keys[c], seen).astype(bf16), vals[c]) for b in range(2)
            ]
            mixed[l, :, cut] = jnp.where(low_lanes(), got[0], got[1]).astype(bf16)
        scatter_start(l, 0, dot_nt(mixed[l], weight(l, 512, 768)))


        @pl.when((s == 1) & (l == 0))
        def _():
            spread_start()
            push(expert_copy, 0, 64)

        experts_iota = lax.broadcasted_iota(jnp.int32, (E, ROWS), 0)
        named = jnp.zeros((E, ROWS), f32)
        for k in range(TOPK):
            named = named + (experts_iota == routes[l, k:k + 1]).astype(f32)
        before = (
            lax.broadcasted_iota(jnp.int32, (ROWS, ROWS), 0)
            < lax.broadcasted_iota(jnp.int32, (ROWS, ROWS), 1)
        ).astype(bf16)
        place = dot(named.astype(bf16), before)
        slots[...] = jnp.where(named > 0, place, -1.0)
        place = slots[experts_mine]
        slot_iota = lax.broadcasted_iota(jnp.int32, (CAP, ROWS), 0).astype(f32)
        for i in range(LOCAL):
            chosen[l, CAP * i:CAP * i + CAP] = (slot_iota == place[i:i + 1]).astype(bf16)

        center = xin[l, rows_mine] + scatter_end(l, 0)
        middle[l] = center
        gather_start(l, 0, center * scale_of(center) * turned[l, 33:34])
        gather_end(l, 0)

        second = ag[l, 0]
        packed[l, 0] = dot(chosen[l], second).astype(bf16)
        dispatch_copies(l, 0, 0)
        logits = dot_nt(turned[l, 0:32].astype(bf16), second)
        logits = jnp.where(named > 0, logits, masked_score)
        raised = jnp.where(named > 0, jnp.exp(logits - jnp.max(logits, axis=0, keepdims=True)), 0.0)
        chance[l] = raised / jnp.sum(raised, axis=0, keepdims=True)
        gate = chance[l, experts_mine]
        for i in range(LOCAL):
            cut = slice(CAP * i, CAP * i + CAP)
            weighted = chosen[l, cut].astype(f32) * gate[i:i + 1]
            slot_gate[l, cut] = jnp.sum(weighted, axis=1, keepdims=True)

        @pl.when(s == l)
        def _():
            arrive(expert_copy)
            for turn_no in range(2):
                rel = (l + turn_no) % 2
                dispatch_arrived(0, rel)
                cut = pl.ds(pl.multiple_of(384 * rel, 384), 384)
                rows = x_rows[cut]
                gate_part = dot(rows, experts[0])
                up_part = dot(rows, experts[1])
                gate_s[cut] = gate_part
                up_s[cut] = up_part
                hidden = (gate_part / (1.0 + jnp.exp(-gate_part)) * up_part).astype(bf16)
                hid_s[cut] = hidden
                y_rows[0, cut] = dot_nt(hidden, experts[2]).astype(bf16)
                return_copies(l, 0, rel, 0)

        @pl.when((s == 1) & (l == 0))
        def _():
            spread_end()

        return_arrived(l, 0)
        scaled = ret[l, 0].astype(f32) * slot_gate[l]
        scatter_start(l, 1, dot_tn(chosen[l], scaled.astype(bf16)))
        gather_start(l, 1, middle[l] + scatter_end(l, 1))
        gather_end(l, 1)
        xin[l + 1] = ag[l, 1].astype(f32)
        keep_result(0, l, out_ref)
        dispatch_copies(l, 0, 1)
        return carry

    lax.fori_loop(0, 2, forward, 0)

    @pl.when(s == 0)
    def _():
        for copy in exchange_copies()[:1]:
            copy.wait()
        uin[1] = other[...]

    def backward(step, carry):
        l = 1 - step
        upstream = uin[l].astype(bf16)
        spread = dot(chosen[l], upstream)
        packed[l, 1] = (spread * slot_gate[l]).astype(bf16)
        dispatch_copies(l, 1, 0)
        inner = jnp.sum(spread * ret[l, 0].astype(f32), axis=1, keepdims=True)
        for i in range(LOCAL):
            cut = slice(CAP * i, CAP * i + CAP)
            row = jnp.sum(chosen[l, cut].astype(f32) * inner[cut], axis=0, keepdims=True)
            gate_grads[i:i + 1] = row
        small[l, 0, x, 0:8] = gate_grads[...]
        for copy in small_copies(l, 0):
            copy.start()

        @pl.when(s == l)
        def _():
            for turn_no in range(2):
                rel = (l + turn_no) % 2
                dispatch_arrived(1, rel)
                cut = pl.ds(pl.multiple_of(384 * rel, 384), 384)
                hidden_grad = dot(og_rows[cut], experts[2])
                gate_part = gate_s[cut]
                up_part = up_s[cut]
                sig = 1.0 / (1.0 + jnp.exp(-gate_part))
                gate_low = (
                    hidden_grad * up_part * sig * (1.0 + gate_part * (1.0 - sig))
                ).astype(bf16)
                up_low = (hidden_grad * gate_part * sig).astype(bf16)
                gg_low[cut] = gate_low
                ug_low[cut] = up_low
                back = dot_nt(gate_low, experts[0]) + dot_nt(up_low, experts[1])
                y_rows[1, cut] = back.astype(bf16)
                return_copies(l, 1, rel, 0)
            expert_grad[0] = dot_tn(x_rows[...], gg_low[...]).astype(bf16)
            expert_grad[1] = dot_tn(x_rows[...], ug_low[...]).astype(bf16)
            expert_grad[2] = dot_tn(og_rows[...], hid_s[...]).astype(bf16)
            push(piece_copy, 0, 8)

        for copy in small_copies(l, 0):
            copy.wait()
        gate = chance[l]
        gate_total = jnp.concatenate([small[l, 0, p, 0:8] for p in range(4)], axis=0)
        picked = gate * (gate_total - jnp.sum(gate * gate_total, axis=0, keepdims=True))
        logit_low = picked.astype(bf16)
        router_back[...] = dot_tn(logit_low, turned[l, 0:32].astype(bf16))
        return_arrived(l, 1)
        scatter_start(l, 2, dot_tn(chosen[l], ret[l, 1]))
        push_when(s == l, piece_copy, 8, 16)
        router_grad = dot(logit_low, ag[l, 0])
        arrived = scatter_end(l, 2) + router_back[rows_mine]
        back, gain_two = norm_back(middle[l], turned[l, 33:34], arrived)
        kept = uin[l, rows_mine] + back
        resid[...] = kept
        gather_start(l, 2, kept)
        push_when(s == l, piece_copy, 16, 24)
        gather_end(l, 2)

        branch = ag[l, 2]
        dense_grad[l, :, 512:768] = dot_tn(branch, mixed[l]).astype(bf16)
        share(l, 1)
        push_when(s == l, piece_copy, 24, 40)
        mixed_grad = dot(branch, weight(l, 512, 768)).astype(bf16)
        seen = seen_ref[...] > 0
        cos, sin = cos_ref[...], -sin_ref[...]
        left = low_lanes()
        keys = doubled(qkv[l, :, 256:384])
        vals = doubled(qkv[l, :, 384:512])
        key_grads, value_grads = [], []
        for c in range(2):
            cut = slice(128 * c, 128 * c + 128)
            query, above = qkv[l, :, cut], mixed_grad[:, cut]
            parts, key_grad, value_grad = [], 0.0, 0.0
            for b in range(2):
                query_half, above_half = half(query, b), half(above, b)
                prob = soft(query_half, keys[c], seen)
                value_grad = value_grad + dot_tn(prob.astype(bf16), above_half)
                prob_grad = dot_nt(above_half, vals[c])
                mean = jnp.sum(prob * prob_grad, axis=1, keepdims=True)
                score_low = (prob * (prob_grad - mean)).astype(bf16)
                parts.append(dot(score_low, keys[c]))
                key_grad = key_grad + dot_tn(score_low, query_half)
            query_grad = jnp.where(left, parts[0], parts[1]) * HEAD_SIZE ** (-0.5)
            dqkv[:, cut] = turn(query_grad, cos, sin).astype(bf16)
            key_grads.append(key_grad + pltpu.roll(key_grad, 64, 1))
            value_grads.append(value_grad + pltpu.roll(value_grad, 64, 1))
        key_grad = jnp.where(left, key_grads[0], key_grads[1]) * HEAD_SIZE ** (-0.5)
        dqkv[:, 256:384] = turn(key_grad, cos, sin).astype(bf16)
        dqkv[:, 384:512] = jnp.where(left, value_grads[0], value_grads[1]).astype(bf16)
        scatter_start(l, 3, dot_nt(dqkv[...], weight(l, 0, 512)))
        push_when(s == l, piece_copy, 40, 48)
        dense_grad[l, :, 0:512] = dot_tn(first_in[l], dqkv[...]).astype(bf16)
        share(l, 0)
        part_push(l, 1)
        back, gain_one = norm_back(xin[l, rows_mine], turned[l, 32:33], scatter_end(l, 3))
        gather_start(l, 3, resid[...] + back)
        push_when(s == l, piece_copy, 48, 56)
        gains[l, x, 0:1] = gain_one
        gains[l, x, 1:2] = gain_two
        for k in range(1, 4):
            ref = gains.at[l, x]
            remote(ref, ref, sm_ss.at[l, 1, k - 1], sm_rs.at[l, 1, k - 1],
                   {"tensor": (x + k) % 4}).start()
        part_push(l, 0)
        gather_end(l, 3)
        uin[1 - l] = ag[l, 3].astype(f32)
        keep_result(1, l, grad_ref)
        for k in range(1, 4):
            ref = gains.at[l, x]
            remote(ref, ref, sm_ss.at[l, 1, k - 1], sm_rs.at[l, 1, k - 1],
                   {"tensor": (x + k) % 4}).wait()
        total = gains[l, 0] + gains[l, 1] + gains[l, 2] + gains[l, 3]
        last = jnp.concatenate([router_grad, total, jnp.zeros((88, WIDTH), f32)], axis=0)
        dense_grad[l, :, 768:896] = last.T.astype(bf16)
        push_when(s == l, piece_copy, 56, 64)
        share(l, 2)
        part_push(l, 2)
        dispatch_copies(l, 1, 1)
        return carry

    lax.fori_loop(0, 2, backward, 0)

    for way, ref in ((0, out_ref), (1, grad_ref)):
        swap_copy(way).wait()
        ref[1 - s] = swap_in[way]
        for rel in range(2):
            return_copies(s, way, jnp.int32(rel), 1)
    for part in range(2):
        for k in range(4):
            sibling_copy(part, k, s).wait_send()
    all_but_own(expert_copy, "wait_send")
    all_but_own(piece_copy, "wait_send")
    arrive(piece_copy)
    for c in range(3):
        share_copy(c).wait_send()
        part_copy(c, 0, True).wait()

        def one(k, carry):
            part_copy(c, k).wait()
            return carry

        lax.fori_loop(1, 16, one, 0)


def layers(*operands):
    shape = jax.ShapeDtypeStruct
    scratch = [
        pltpu.VMEM((E, 3, 64, 128), bf16),
        pltpu.VMEM((2, 4, 4, 64, DENSE), bf16),
        pltpu.VMEM((3, WIDTH, FF), bf16),
        pltpu.VMEM((2, WIDTH, DENSE), bf16),
        pltpu.VMEM((WIDTH, DENSE), bf16),
        pltpu.VMEM((3, WIDTH, FF), bf16),
        pltpu.VMEM((ROWS, WIDTH), f32),
        pltpu.VMEM((2, TOPK, ROWS), jnp.int32),
        pltpu.VMEM((ROWS, 128), f32),
        pltpu.VMEM((ROWS, 128), f32),
        pltpu.VMEM((ROWS, 128), f32),
        pltpu.VMEM((3, ROWS, WIDTH), f32),
        pltpu.VMEM((2, ROWS, WIDTH), f32),
        pltpu.VMEM((2, ROWS, WIDTH), f32),
        pltpu.VMEM((2, ROWS, WIDTH), bf16),
        pltpu.VMEM((2, ROWS, 512), bf16),
        pltpu.VMEM((2, ROWS, 256), bf16),
        pltpu.VMEM((2, PART, WIDTH), f32),
        pltpu.VMEM((2, LOCAL * CAP, ROWS), bf16),
        pltpu.VMEM((2, E, ROWS), f32),
        pltpu.VMEM((2, LOCAL * CAP, 1), f32),
        pltpu.VMEM((2, 4, ROWS, WIDTH), bf16),
        pltpu.VMEM((2, 4, 3, PART, WIDTH), bf16),
        pltpu.VMEM((2, 4, ROWS, WIDTH), bf16),
        pltpu.VMEM((2, 1, 4, 8, ROWS), f32),
        pltpu.VMEM((E, ROWS), f32),
        pltpu.VMEM((2, 2, LOCAL * CAP, WIDTH), bf16),
        pltpu.VMEM((2 * LOCAL * CAP, WIDTH), bf16),
        pltpu.VMEM((2 * LOCAL * CAP, WIDTH), bf16),
        pltpu.VMEM((2 * LOCAL * CAP, FF), f32),
        pltpu.VMEM((2 * LOCAL * CAP, FF), f32),
        pltpu.VMEM((2 * LOCAL * CAP, FF), bf16),
        pltpu.VMEM((2, 2 * LOCAL * CAP, WIDTH), bf16),
        pltpu.VMEM((2, 2, LOCAL * CAP, WIDTH), bf16),
        pltpu.VMEM((2 * LOCAL * CAP, FF), bf16),
        pltpu.VMEM((2 * LOCAL * CAP, FF), bf16),
        pltpu.VMEM((8, ROWS), f32),
        pltpu.VMEM((PART, WIDTH), f32),
        pltpu.VMEM((2, 4, 8, WIDTH), f32),
        pltpu.VMEM((ROWS, WIDTH), f32),
        pltpu.VMEM((ROWS, 512), bf16),
        pltpu.VMEM((2, ROWS, WIDTH), bf16),
        pltpu.VMEM((2, ROWS, WIDTH), bf16),
        pltpu.SemaphoreType.DMA((2, 4, 3)),
        pltpu.SemaphoreType.DMA((2, 4, 3)),
        pltpu.SemaphoreType.DMA((2, 4, 3)),
        pltpu.SemaphoreType.DMA((2, 4, 3)),
        pltpu.SemaphoreType.DMA((2, 2, 3)),
        pltpu.SemaphoreType.DMA((2, 2, 3)),
        pltpu.SemaphoreType.DMA((2, 2, 8)),
        pltpu.SemaphoreType.DMA((2, 16)),
        pltpu.SemaphoreType.DMA((2, 16)),
        pltpu.SemaphoreType.DMA((2, 2, 8)),
        pltpu.SemaphoreType.DMA((2,)),
        pltpu.SemaphoreType.DMA((2,)),
        pltpu.SemaphoreType.DMA((2, 2, 3)),
        pltpu.SemaphoreType.DMA((2, 2, 3)),
        pltpu.SemaphoreType.DMA((3, 4)),
        pltpu.SemaphoreType.DMA((3, 4)),
        pltpu.SemaphoreType.DMA((64,)),
        pltpu.SemaphoreType.DMA((64,)),
        pltpu.SemaphoreType.DMA((3, 16)),
        pltpu.SemaphoreType.DMA((3, 16)),
        pltpu.SemaphoreType.DMA((64,)),
        pltpu.SemaphoreType.DMA((64,)),
        pltpu.SemaphoreType.DMA((3,)),
        pltpu.SemaphoreType.DMA((3,)),
        pltpu.SemaphoreType.DMA((3,)),
    ]
    return pl.pallas_call(
        body,
        out_shape=(
            shape((2, ROWS, WIDTH), bf16),
            shape((2, ROWS, WIDTH), bf16),
            shape((16, 64, DENSE), bf16),
            shape((2, 3, E, 64, 128), bf16),
        ),
        in_specs=[
            pl.BlockSpec(memory_space=pltpu.SMEM),
            *[pl.BlockSpec(memory_space=pltpu.VMEM) for _ in range(5)],
            *[pl.BlockSpec(memory_space=pl.ANY) for _ in range(2)],
            *[pl.BlockSpec(memory_space=pltpu.VMEM) for _ in range(2)],
        ],
        out_specs=(
            pl.BlockSpec(memory_space=pltpu.VMEM),
            pl.BlockSpec(memory_space=pltpu.VMEM),
            pl.BlockSpec(memory_space=pl.ANY),
            pl.BlockSpec(memory_space=pl.ANY),
        ),
        scratch_shapes=scratch,
        compiler_params=pltpu.CompilerParams(
            collective_id=0, has_side_effects=True, vmem_limit_bytes=60 * 1024 * 1024
        ),
        name="layers",
    )(*operands)


def local(
    boundary,
    doc_lengths,
    routes,
    norm_gains,
    w_query,
    key_value_weight,
    w_out,
    w_router,
    w_gateup,
    w_down,
):
    outs, grads, parts, pieces = layers(
        doc_lengths[:, 0], w_query[0], key_value_weight[0], w_out[0].T, w_router[0].T, norm_gains[0],
        w_gateup[0], jnp.swapaxes(w_down[0], 1, 2), boundary[0], jnp.swapaxes(routes[0], 1, 2),
    )
    parts = jnp.sum(parts.astype(f32), axis=0)
    pieces = pieces.astype(f32)
    return (
        outs.astype(f32)[None],
        grads.astype(f32)[None],
        parts[:, 800:802].T[None],
        parts[:, 0:256][None],
        jnp.stack([parts[:, 256:384], parts[:, 384:512]])[None],
        parts[:, 512:768].T[None],
        parts[:, 768:800][None],
        (pieces[0, 0:2] + pieces[1, 0:2])[None],
        jnp.swapaxes(pieces[0, 2] + pieces[1, 2], 1, 2)[None],
    )


def solution(mesh):
    placed = (
        P("section", None, "dp", None),
        P(None, "dp", None),
        P("section", None, "dp", None),
        P("section", None, "dp"),
        P("section", "dp", "tensor"),
        P("section", None, "dp", "tensor"),
        P("section", "tensor", "dp"),
        P("section", "dp", None),
        P("section", None, None, "dp", "tensor"),
        P("section", None, "tensor", "dp"),
    )
    return jax.shard_map(
        local,
        mesh=mesh,
        in_specs=placed,
        out_specs=(
            P("section", None, "dp", None),
            P("section", None, "dp", None),
            P("section", None, "dp"),
            P("section", "dp", "tensor"),
            P("section", None, "dp", "tensor"),
            P("section", "tensor", "dp"),
            P("section", "dp", None),
            P("section", None, None, "dp", "tensor"),
            P("section", None, "tensor", "dp"),
        ),
        check_vma=False,
    )
```

```python
import math

import jax
import jax.numpy as jnp
from jax import lax
from jax.experimental import pallas as pl
from jax.experimental.pallas import tpu as pltpu
from jax.sharding import PartitionSpec as P

HEAD_SIZE = 64
E = 32
TOPK = 8
CAP = 48
ROWS = 128
WIDTH = 1024
FF = 512
PART = 32
LOCAL = 8
DENSE = 896

epsilon = 1e-06
rope_base = 10000.0
masked_score = -1e30
f32 = jnp.float32
bf16 = jnp.bfloat16
MESH = pl.DeviceIdType.MESH


def dot(a, b):
    return lax.dot_general(a, b, (((1,), (0,)), ((), ())), preferred_element_type=f32)


def dot_nt(a, b):
    return lax.dot_general(a, b, (((1,), (1,)), ((), ())), preferred_element_type=f32)


def dot_tn(a, b):
    return lax.dot_general(a, b, (((0,), (0,)), ((), ())), preferred_element_type=f32)


def unit(rows, columns, shift):
    row = lax.broadcasted_iota(jnp.int32, (rows, columns), 0)
    column = lax.broadcasted_iota(jnp.int32, (rows, columns), 1)
    return (row + shift == column).astype(bf16)


def scale_of(values):
    return lax.rsqrt(jnp.mean(values * values, axis=1, keepdims=True) + epsilon)


def norm_back(values, gain_row, upstream):
    scale = scale_of(values)
    weighted = upstream * gain_row
    inner = jnp.mean(weighted * values, axis=1, keepdims=True)
    back = scale * weighted - values * (scale * scale * scale * inner)
    return back, jnp.sum(upstream * values * scale, axis=0, keepdims=True)


def low_lanes():
    return lax.broadcasted_iota(jnp.int32, (ROWS, 128), 1) < 64


def turn(chunk, cos, sin):
    place = lax.broadcasted_iota(jnp.int32, (ROWS, 128), 1) % 64
    swapped = jnp.where(place < 32, pltpu.roll(chunk, 96, 1), pltpu.roll(chunk, 32, 1))
    return chunk * cos + swapped * sin


def doubled(both):
    wide = both.astype(f32)
    other = pltpu.roll(wide, 64, 1)
    left = low_lanes()
    return (
        jnp.where(left, wide, other).astype(bf16),
        jnp.where(left, other, wide).astype(bf16),
    )


def half(chunk, which):
    left = low_lanes()
    keep = left if which == 0 else jnp.logical_not(left)
    return jnp.where(keep, chunk, jnp.zeros_like(chunk))


def soft(query_half, keys, seen):
    scores = dot_nt(query_half, keys) * HEAD_SIZE ** (-0.5)
    scores = jnp.where(seen, scores, masked_score)
    raised = jnp.exp(scores - jnp.max(scores, axis=1, keepdims=True))
    return raised / jnp.sum(raised, axis=1, keepdims=True)


def body(
    lengths, query_own, keyval_own, out_own, router_own, gains_own, gateup_own, down_own,
    boundary, routes_own,
    out_ref, grad_ref, parts, pieces,
    own, dense, experts, dense_grad, shared, expert_grad, other, routes, cos_ref, sin_ref, seen_ref,
    xin, uin, turned, first_in, qkv, mixed, middle, chosen, chance, slot_gate,
    rs_send, rs_recv, ag, small, slots, packed, x_rows, og_rows, gate_s, up_s, hid_s,
    y_rows, ret, gu_low, probs, gate_grads, resid, gains, router_back, dqkv, swap_out, swap_in,
    rs_ss, rs_rs, ag_ss, ag_rs, sm_ss, sm_rs, d_ss, d_rs, r_ss, r_rs, w_ss, w_rs,
    a_ss, a_rs, b_ss, b_rs, e_ss, e_rs, g_ss, g_rs, p_ss, p_rs, h_ss, h_rs, c_ss,
):
    s = lax.axis_index("section")
    x = lax.axis_index("tensor")
    d = lax.axis_index("dp")
    z, y = d // 4, d % 4
    zz = z % 2
    mine = zz * 4 + (y + 2 * (z // 2)) % 4
    rows_mine = pl.ds(pl.multiple_of(x * PART, PART), PART)
    experts_mine = pl.ds(pl.multiple_of(x * LOCAL, LOCAL), LOCAL)
    odd = (y + z) % 2
    steps = (
        (0, 0), (1, 0), (3, 0), (0, 1), (0, 3),
        (1 + 2 * odd, 1 + 2 * odd), (3 - 2 * odd, 1 + 2 * odd), (2 - 2 * odd, 2 * odd),
    )

    def holder(n):
        y2, z2 = (y + steps[n][0]) % 4, (z + steps[n][1]) % 4
        return z2 % 2 * 4 + (y2 + 2 * (z2 // 2)) % 4, z2 * 4 + y2

    def sender(n):
        return (z + 4 - steps[n][1]) % 4 * 4 + (y + 4 - steps[n][0]) % 4

    barrier = pltpu.get_barrier_semaphore()

    def greet(k, carry):
        there, at = (x + k // 16) % 4, (d + k % 16) % 16

        @pl.when(k > 0)
        def _():
            pl.semaphore_signal(
                barrier, inc=1, device_id={"tensor": there, "dp": at}, device_id_type=MESH
            )

        return carry

    lax.fori_loop(0, 64, greet, 0)
    for peer in [holder(n)[1] for n in range(8)] + [sender(5), sender(6)]:
        pl.semaphore_signal(
            barrier, inc=1, device_id={"section": 1 - s, "dp": peer}, device_id_type=MESH
        )

    row = lax.broadcasted_iota(jnp.int32, (ROWS, 128), 0)
    lane = lax.broadcasted_iota(jnp.int32, (ROWS, 128), 1)
    start, row_doc, lane_doc, end = 0, 0, 0, 0
    for k in range(3):
        size = lengths[s, k]
        end = end + size
        start = start + jnp.where(row >= end, size, 0)
        row_doc = row_doc + jnp.where(row >= end, 1, 0)
        lane_doc = lane_doc + jnp.where(lane >= end, 1, 0)
    step = (lane % 32).astype(f32) * (-2.0 / HEAD_SIZE * math.log(rope_base))
    angles = (row - start).astype(f32) * jnp.exp(step)
    sine = jnp.sin(angles)
    cos_ref[...] = jnp.cos(angles)
    sin_ref[...] = jnp.where(lane % 64 < 32, -sine, sine)
    seen_ref[...] = jnp.where((row_doc == lane_doc) & (lane <= row), 1.0, 0.0)

    pl.semaphore_wait(barrier, 73)

    def remote(src, dst, send, recv, device):
        return pltpu.make_async_remote_copy(
            src_ref=src, dst_ref=dst, send_sem=send, recv_sem=recv,
            device_id=device, device_id_type=MESH,
        )

    def scatter_copies(l, j):
        copies = []
        for k in (2, 1, 3):
            p = (x + k) % 4
            src = rs_send.at[l, j, pl.ds(pl.multiple_of(p * PART, PART), PART)]
            copies.append(
                remote(src, rs_recv.at[l, j, k - 1], rs_ss.at[l, j, k - 1],
                       rs_rs.at[l, j, k - 1], {"tensor": p})
            )
        return copies

    def scatter_start(l, j, partial):
        rs_send[l, j] = partial.astype(bf16)
        for copy in scatter_copies(l, j):
            copy.start()

    def scatter_end(l, j):
        for copy in scatter_copies(l, j):
            copy.wait()
        total = rs_send[l, j, rows_mine].astype(f32)
        for k in range(3):
            total = total + rs_recv[l, j, k].astype(f32)
        return total

    def gather_copies(l, j):
        copies = []
        for k in (2, 1, 3):
            ref = ag.at[l, j, rows_mine]
            copies.append(
                remote(ref, ref, ag_ss.at[l, j, k - 1], ag_rs.at[l, j, k - 1],
                       {"tensor": (x + k) % 4})
            )
        return copies

    def gather_start(l, j, rows):
        ag[l, j, rows_mine] = rows.astype(bf16)
        for copy in gather_copies(l, j):
            copy.start()

    def gather_end(l, j):
        for copy in gather_copies(l, j):
            copy.wait()

    def small_copies(l, j):
        copies = []
        for k in range(1, 4):
            ref = small.at[l, j, x]
            copies.append(
                remote(ref, ref, sm_ss.at[l, j, k - 1], sm_rs.at[l, j, k - 1],
                       {"tensor": (x + k) % 4})
            )
        return copies

    def block(index):
        return pl.ds(pl.multiple_of(index * CAP, CAP), CAP)

    def dispatch_copies(l, way, act):
        rel = (s + l) % 2
        target = x_rows if way == 0 else og_rows
        for n in (5, 6, 7, 1, 2, 3, 4, 0):
            i, peer = holder(n)
            src = packed.at[l, way, block(i)]
            dst = target.at[block(rel * 8 + n)]
            far = remote(src, dst, d_ss.at[l, way, n], d_rs.at[way, rel * 8 + n],
                         {"section": l, "dp": peer})
            if n == 0:
                @pl.when(s == l)
                def _():
                    if act == 0:
                        pltpu.make_async_copy(src, dst, d_rs.at[way, 0]).start()

                @pl.when(s != l)
                def _():
                    if act == 0:
                        far.start()
                    else:
                        far.wait_send()
            elif act == 0:
                far.start()
            else:
                far.wait_send()

    def dispatch_arrived(way, rel):
        target = x_rows if way == 0 else og_rows

        def far(n):
            return remote(
                packed.at[0, way, block(n)], target.at[block(rel * 8 + n)],
                d_ss.at[0, way, n], d_rs.at[way, rel * 8 + n], {"dp": holder(1)[1]},
            )

        @pl.when(rel == 0)
        def _():
            pltpu.make_async_copy(
                packed.at[0, way, block(mine)], target.at[block(0)], d_rs.at[way, 0]
            ).wait()

        @pl.when(rel != 0)
        def _():
            far(0).wait_recv()

        for n in range(1, 8):
            far(n).wait_recv()

    def return_copies(l, way, rel, act):
        for n in (5, 6, 7, 1, 2, 3, 4, 0):
            peer = sender(n)
            src = y_rows.at[way, block(rel * 8 + n)]
            dst = ret.at[l, way, block(mine)]
            def far():
                return remote(src, dst, r_ss.at[way, rel * 8 + n], r_rs.at[l, way, n],
                              {"section": (s + rel) % 2, "dp": peer})

            def go():
                if act == 0:
                    far().start()
                else:
                    far().wait_send()

            if n > 0:
                go()
            else:
                pl.when(rel != 0)(go)
                if act == 0:
                    @pl.when(rel == 0)
                    def _():
                        pltpu.make_async_copy(src, dst, r_rs.at[l, way, 0]).start()

    def return_arrived(l, way):
        for n in range(8):
            i, peer = holder(n)
            src = y_rows.at[way, block(n)]
            dst = ret.at[l, way, block(i)]
            far = remote(src, dst, r_ss.at[way, n], r_rs.at[l, way, n],
                         {"section": 1 - s, "dp": peer})
            if n == 0:
                @pl.when(s == l)
                def _():
                    pltpu.make_async_copy(src, dst, r_rs.at[l, way, 0]).wait()

                @pl.when(s != l)
                def _():
                    far.wait_recv()
            else:
                far.wait_recv()

    def swap_copy(way):
        return remote(swap_out.at[way], swap_in.at[way], w_ss.at[way], w_rs.at[way],
                      {"section": 1 - s})

    def keep_result(way, l, ref):
        @pl.when(s == l)
        def _():
            ref[s] = ag[l, 1 + 2 * way]

        @pl.when(s != l)
        def _():
            swap_out[way] = ag[l, 1 + 2 * way]
            swap_copy(way).start()

    def block64(index):
        return pl.ds(pl.multiple_of(index * 64, 64), 64)

    def block128(index):
        return pl.ds(pl.multiple_of(index * 128, 128), 128)

    left, right = slice(0, 512), slice(512, DENSE)

    def along_y(k):
        return {"dp": z * 4 + (y + k) % 4}

    def along_z(k):
        return {"dp": ((z + k) % 4) * 4 + y}

    def spread_copies(part, phase):
        copies = []
        for k in range(1, 4):
            if part == 0:
                ref = dense.at[s, z, y, :, left] if phase == 0 else dense.at[s, z, :, :, left]
                device = along_y(k) if phase == 0 else along_z(k)
            else:
                ref = dense.at[s, z, y, :, right] if phase == 0 else dense.at[s, :, y, :, right]
                device = along_z(k) if phase == 0 else along_y(k)
            n = k - 1
            copies.append(
                remote(ref, ref, a_ss.at[part, phase, n], a_rs.at[part, phase, n], device)
            )
        return copies

    def sibling_copy(part, k, layer):
        if part == 0:
            ref = dense.at[layer, (z + k) % 4, :, :, left]
        else:
            ref = dense.at[layer, :, (y + k) % 4, :, right]
        return remote(ref, ref, b_ss.at[part, k], b_rs.at[part, k], {"section": 1 - s})

    def weight_copy(kind):
        src = gateup_own.at[kind] if kind < 2 else down_own
        return pltpu.make_async_copy(src, own.at[:, kind], c_ss.at[kind])

    def exchange_copies():
        return [
            remote(boundary.at[1 - s], other, b_ss.at[2, 0], b_rs.at[2, 0], {"section": 1 - s}),
            remote(routes_own.at[1 - s], routes.at[s], b_ss.at[2, 1], b_rs.at[2, 1],
                   {"section": 1 - s}),
        ]

    def expert_copy(k, local_only=False):
        there, at = (x + k // 16) % 4, (d + k % 16) % 16
        e = there * 8 + at // 4 % 2 * 4 + (at % 4 + 2 * (at // 8)) % 4
        src, dst = own.at[e], experts.at[:, block64(d), block128(x)]
        if local_only:
            return pltpu.make_async_copy(src, dst, e_rs.at[0])
        return remote(src, dst, e_ss.at[k], e_rs.at[k], {"tensor": there, "dp": at})

    def piece_copy(k, local_only=False):
        there, at = (x + k // 16) % 4, (d + k % 16) % 16
        src = expert_grad.at[:, block64(at), block128(there)]
        dst = pieces.at[z // 2, :, x * 8 + mine]
        if local_only:
            return pltpu.make_async_copy(src, dst, p_rs.at[0])
        return remote(src, dst, p_ss.at[k], p_rs.at[k], {"tensor": there, "dp": at})

    def all_but_own(copy, act, low=1, high=64):
        def one(n, carry):
            getattr(copy(n * 13 % 64), act)()
            return carry

        lax.fori_loop(low, high, one, 0)

    def push(copy, low, high):
        whole = isinstance(low, int) and low == 0
        if whole:
            copy(0, True).start()
        all_but_own(copy, "start", 1 if whole else low, high)

    def push_when(condition, copy, low, high):
        pl.when(condition)(lambda: push(copy, low, high))

    def arrive(copy):
        copy(0, True).wait()
        all_but_own(copy, "wait_recv")

    wide = (slice(0, 512), slice(512, 768), slice(768, DENSE))

    def part_copy(c, k, local_only=False):
        at = (d + k) % 16
        src = dense_grad.at[s, block64(at), wide[c]]
        dst = parts.at[d, :, wide[c]]
        if local_only:
            return pltpu.make_async_copy(src, dst, g_rs.at[c, 0])
        return remote(src, dst, g_ss.at[c, k], g_rs.at[c, k], {"dp": at})

    def share_copy(c):
        return remote(dense_grad.at[1 - s, :, wide[c]], shared.at[:, wide[c]],
                      h_ss.at[c], h_rs.at[c], {"section": 1 - s})

    def share(l, c):
        @pl.when(s != l)
        def _():
            share_copy(c).start()

    def part_push(l, c):
        @pl.when(s == l)
        def _():
            share_copy(c).wait_recv()
            both = dense_grad[l, :, wide[c]].astype(f32) + shared[:, wide[c]].astype(f32)
            dense_grad[l, :, wide[c]] = both.astype(bf16)
            part_copy(c, 0, True).start()

            def one(k, carry):
                part_copy(c, k).start()
                return carry

            lax.fori_loop(1, 16, one, 0)

    for copy in exchange_copies():
        copy.start()
    for kind in range(3):
        weight_copy(kind).start()
    routes[s] = routes_own[s]
    dense[s, z, y, :, 0:256] = query_own[...]
    dense[s, z, y, :, 256:384] = keyval_own[0]
    dense[s, z, y, :, 384:512] = keyval_own[1]
    dense[s, z, y, :, 512:768] = out_own[...]
    last = dot_tn(router_own[...], unit(E, 128, 0)) + dot_tn(gains_own[...], unit(2, 128, E))
    dense[s, z, y, :, 768:896] = last.astype(bf16)
    for part in range(2):
        for copy in spread_copies(part, 0):
            copy.start()


    @pl.when(s == 0)
    def _():
        xin[0] = boundary[0]

    @pl.when(s == 1)
    def _():
        uin[1] = boundary[1]

    for part in range(2):
        for copy in spread_copies(part, 0):
            copy.wait()
    for kind in range(3):
        weight_copy(kind).wait()

    def spread_start():
        for part in range(2):
            for copy in spread_copies(part, 1):
                copy.start()
            sibling_copy(part, 0, s).start()

    def spread_end():
        for part in range(2):
            for k in range(3):
                spread_copies(part, 1)[k].wait()
                sibling_copy(part, 3 - k, s).start()

    @pl.when(s == 0)
    def _():
        spread_start()
        push(expert_copy, 0, 64)
        spread_end()

    @pl.when(s == 1)
    def _():
        for copy in exchange_copies()[:1]:
            copy.wait()
        xin[0] = other[...]

    def weight(l, low, high):
        return dense[l, :, :, :, low:high].reshape(WIDTH, high - low)

    def forward(l, carry):
        @pl.when(s != l)
        def _():
            for part in range(2):
                for k in range(4):
                    sibling_copy(part, k, s).wait_recv()
            exchange_copies()[1].wait()

        turned[l] = weight(l, 768, 896).astype(f32).T
        values = xin[l]
        first = (values * scale_of(values) * turned[l, 32:33]).astype(bf16)
        first_in[l] = first
        made = dot(first, weight(l, 0, 512))
        cos, sin = cos_ref[...], sin_ref[...]
        for c in range(3):
            cut = slice(128 * c, 128 * c + 128)
            qkv[l, :, cut] = turn(made[:, cut], cos, sin).astype(bf16)
        qkv[l, :, 384:512] = made[:, 384:512].astype(bf16)
        seen = seen_ref[...] > 0
        keys = doubled(qkv[l, :, 256:384])
        vals = doubled(qkv[l, :, 384:512])
        for c in range(2):
            cut = slice(128 * c, 128 * c + 128)
            query = qkv[l, :, cut]
            got = [
                dot(soft(half(query, b), keys[c], seen).astype(bf16), vals[c]) for b in range(2)
            ]
            mixed[l, :, cut] = jnp.where(low_lanes(), got[0], got[1]).astype(bf16)
        scatter_start(l, 0, dot_nt(mixed[l], weight(l, 512, 768)))


        @pl.when((s == 1) & (l == 0))
        def _():
            spread_start()
            push(expert_copy, 0, 64)

        experts_iota = lax.broadcasted_iota(jnp.int32, (E, ROWS), 0)
        named = jnp.zeros((E, ROWS), f32)
        for k in range(TOPK):
            named = named + (experts_iota == routes[l, k:k + 1]).astype(f32)
        before = (
            lax.broadcasted_iota(jnp.int32, (ROWS, ROWS), 0)
            < lax.broadcasted_iota(jnp.int32, (ROWS, ROWS), 1)
        ).astype(bf16)
        place = dot(named.astype(bf16), before)
        slots[...] = jnp.where(named > 0, place, -1.0)
        place = slots[experts_mine]
        slot_iota = lax.broadcasted_iota(jnp.int32, (CAP, ROWS), 0).astype(f32)
        for i in range(LOCAL):
            chosen[l, CAP * i:CAP * i + CAP] = (slot_iota == place[i:i + 1]).astype(bf16)

        center = xin[l, rows_mine] + scatter_end(l, 0)
        middle[l] = center
        gather_start(l, 0, center * scale_of(center) * turned[l, 33:34])
        gather_end(l, 0)

        second = ag[l, 0]
        packed[l, 0] = dot(chosen[l], second).astype(bf16)
        dispatch_copies(l, 0, 0)
        logits = dot_nt(turned[l, 0:32].astype(bf16), second)
        logits = jnp.where(named > 0, logits, masked_score)
        raised = jnp.where(named > 0, jnp.exp(logits - jnp.max(logits, axis=0, keepdims=True)), 0.0)
        chance[l] = raised / jnp.sum(raised, axis=0, keepdims=True)
        gate = chance[l, experts_mine]
        for i in range(LOCAL):
            cut = slice(CAP * i, CAP * i + CAP)
            weighted = chosen[l, cut].astype(f32) * gate[i:i + 1]
            slot_gate[l, cut] = jnp.sum(weighted, axis=1, keepdims=True)

        @pl.when(s == l)
        def _():
            arrive(expert_copy)
            for turn_no in range(2):
                rel = (l + turn_no) % 2
                dispatch_arrived(0, rel)
                cut = pl.ds(pl.multiple_of(384 * rel, 384), 384)
                rows = x_rows[cut]
                gate_part = dot(rows, experts[0])
                up_part = dot(rows, experts[1])
                gate_s[cut] = gate_part
                up_s[cut] = up_part
                hidden = (gate_part / (1.0 + jnp.exp(-gate_part)) * up_part).astype(bf16)
                hid_s[cut] = hidden
                y_rows[0, cut] = dot_nt(hidden, experts[2]).astype(bf16)
                return_copies(l, 0, rel, 0)

        @pl.when((s == 1) & (l == 0))
        def _():
            spread_end()

        return_arrived(l, 0)
        scaled = ret[l, 0].astype(f32) * slot_gate[l]
        scatter_start(l, 1, dot_tn(chosen[l], scaled.astype(bf16)))
        gather_start(l, 1, middle[l] + scatter_end(l, 1))
        gather_end(l, 1)
        xin[l + 1] = ag[l, 1].astype(f32)
        keep_result(0, l, out_ref)
        dispatch_copies(l, 0, 1)
        return carry

    lax.fori_loop(0, 2, forward, 0)

    @pl.when(s == 0)
    def _():
        for copy in exchange_copies()[:1]:
            copy.wait()
        uin[1] = other[...]

    def backward(step, carry):
        l = 1 - step
        upstream = uin[l].astype(bf16)
        spread = dot(chosen[l], upstream)
        packed[l, 1] = (spread * slot_gate[l]).astype(bf16)
        dispatch_copies(l, 1, 0)
        inner = jnp.sum(spread * ret[l, 0].astype(f32), axis=1, keepdims=True)
        for i in range(LOCAL):
            cut = slice(CAP * i, CAP * i + CAP)
            row = jnp.sum(chosen[l, cut].astype(f32) * inner[cut], axis=0, keepdims=True)
            gate_grads[i:i + 1] = row
        small[l, 0, x, 0:8] = gate_grads[...]
        for copy in small_copies(l, 0):
            copy.start()

        @pl.when(s == l)
        def _():
            for turn_no in range(2):
                rel = (l + turn_no) % 2
                dispatch_arrived(1, rel)
                cut = pl.ds(pl.multiple_of(384 * rel, 384), 384)
                hidden_grad = dot(og_rows[cut], experts[2])
                gate_part = gate_s[cut]
                up_part = up_s[cut]
                sig = 1.0 / (1.0 + jnp.exp(-gate_part))
                gate_low = (
                    hidden_grad * up_part * sig * (1.0 + gate_part * (1.0 - sig))
                ).astype(bf16)
                up_low = (hidden_grad * gate_part * sig).astype(bf16)
                gu_low[cut, 0:FF] = gate_low
                gu_low[cut, FF:2 * FF] = up_low
                back = dot_nt(gate_low, experts[0]) + dot_nt(up_low, experts[1])
                y_rows[1, cut] = back.astype(bf16)
                return_copies(l, 1, rel, 0)
            both = dot_tn(x_rows[...], gu_low[...])
            expert_grad[0] = both[:, 0:FF].astype(bf16)
            expert_grad[1] = both[:, FF:2 * FF].astype(bf16)

        for copy in small_copies(l, 0):
            copy.wait()
        gate = chance[l]
        gate_total = jnp.concatenate([small[l, 0, p, 0:8] for p in range(4)], axis=0)
        picked = gate * (gate_total - jnp.sum(gate * gate_total, axis=0, keepdims=True))
        logit_low = picked.astype(bf16)
        router_back[...] = dot_tn(logit_low, turned[l, 0:32].astype(bf16))
        return_arrived(l, 1)
        scatter_start(l, 2, dot_tn(chosen[l], ret[l, 1]))

        @pl.when(s == l)
        def _():
            expert_grad[2] = dot_tn(og_rows[...], hid_s[...]).astype(bf16)
            push(piece_copy, 0, 16)

        router_grad = dot(logit_low, ag[l, 0])
        arrived = scatter_end(l, 2) + router_back[rows_mine]
        back, gain_two = norm_back(middle[l], turned[l, 33:34], arrived)
        kept = uin[l, rows_mine] + back
        resid[...] = kept
        gather_start(l, 2, kept)
        push_when(s == l, piece_copy, 16, 24)
        seen = seen_ref[...] > 0
        keys = doubled(qkv[l, :, 256:384])
        for h in range(4):
            query = qkv[l, :, 128 * (h // 2):128 * (h // 2) + 128]
            probs[h] = soft(half(query, h % 2), keys[h // 2], seen)
        gather_end(l, 2)

        branch = ag[l, 2]
        push_when(s == l, piece_copy, 24, 40)
        mixed_grad = dot(branch, weight(l, 512, 768)).astype(bf16)
        cos, sin = cos_ref[...], -sin_ref[...]
        left = low_lanes()
        vals = doubled(qkv[l, :, 384:512])
        key_grads, value_grads = [], []
        for c in range(2):
            cut = slice(128 * c, 128 * c + 128)
            query, above = qkv[l, :, cut], mixed_grad[:, cut]
            parts, key_grad, value_grad = [], 0.0, 0.0
            for b in range(2):
                query_half, above_half = half(query, b), half(above, b)
                prob = probs[2 * c + b]
                value_grad = value_grad + dot_tn(prob.astype(bf16), above_half)
                prob_grad = dot_nt(above_half, vals[c])
                mean = jnp.sum(prob * prob_grad, axis=1, keepdims=True)
                score_low = (prob * (prob_grad - mean)).astype(bf16)
                parts.append(dot(score_low, keys[c]))
                key_grad = key_grad + dot_tn(score_low, query_half)
            query_grad = jnp.where(left, parts[0], parts[1]) * HEAD_SIZE ** (-0.5)
            dqkv[:, cut] = turn(query_grad, cos, sin).astype(bf16)
            key_grads.append(key_grad + pltpu.roll(key_grad, 64, 1))
            value_grads.append(value_grad + pltpu.roll(value_grad, 64, 1))
        key_grad = jnp.where(left, key_grads[0], key_grads[1]) * HEAD_SIZE ** (-0.5)
        dqkv[:, 256:384] = turn(key_grad, cos, sin).astype(bf16)
        dqkv[:, 384:512] = jnp.where(left, value_grads[0], value_grads[1]).astype(bf16)
        scatter_start(l, 3, dot_nt(dqkv[...], weight(l, 0, 512)))
        push_when(s == l, piece_copy, 40, 48)
        dense_grad[l, :, 512:768] = dot_tn(branch, mixed[l]).astype(bf16)
        share(l, 1)
        dense_grad[l, :, 0:512] = dot_tn(first_in[l], dqkv[...]).astype(bf16)
        share(l, 0)
        part_push(l, 1)
        back, gain_one = norm_back(xin[l, rows_mine], turned[l, 32:33], scatter_end(l, 3))
        gather_start(l, 3, resid[...] + back)
        push_when(s == l, piece_copy, 48, 56)
        gains[l, x, 0:1] = gain_one
        gains[l, x, 1:2] = gain_two
        for k in range(1, 4):
            ref = gains.at[l, x]
            remote(ref, ref, sm_ss.at[l, 1, k - 1], sm_rs.at[l, 1, k - 1],
                   {"tensor": (x + k) % 4}).start()
        part_push(l, 0)
        gather_end(l, 3)
        uin[1 - l] = ag[l, 3].astype(f32)
        keep_result(1, l, grad_ref)
        for k in range(1, 4):
            ref = gains.at[l, x]
            remote(ref, ref, sm_ss.at[l, 1, k - 1], sm_rs.at[l, 1, k - 1],
                   {"tensor": (x + k) % 4}).wait()
        total = gains[l, 0] + gains[l, 1] + gains[l, 2] + gains[l, 3]
        last = jnp.concatenate([router_grad, total, jnp.zeros((88, WIDTH), f32)], axis=0)
        dense_grad[l, :, 768:896] = last.T.astype(bf16)
        push_when(s == l, piece_copy, 56, 64)
        share(l, 2)
        part_push(l, 2)
        dispatch_copies(l, 1, 1)
        return carry

    lax.fori_loop(0, 2, backward, 0)

    for way, ref in ((0, out_ref), (1, grad_ref)):
        swap_copy(way).wait()
        ref[1 - s] = swap_in[way]
        for rel in range(2):
            return_copies(s, way, jnp.int32(rel), 1)
    for part in range(2):
        for k in range(4):
            sibling_copy(part, k, s).wait_send()
    all_but_own(expert_copy, "wait_send")
    all_but_own(piece_copy, "wait_send")
    arrive(piece_copy)
    for c in range(3):
        share_copy(c).wait_send()
        part_copy(c, 0, True).wait()

        def one(k, carry):
            part_copy(c, k).wait()
            return carry

        lax.fori_loop(1, 16, one, 0)


def layers(*operands):
    shape = jax.ShapeDtypeStruct
    scratch = [
        pltpu.VMEM((E, 3, 64, 128), bf16),
        pltpu.VMEM((2, 4, 4, 64, DENSE), bf16),
        pltpu.VMEM((3, WIDTH, FF), bf16),
        pltpu.VMEM((2, WIDTH, DENSE), bf16),
        pltpu.VMEM((WIDTH, DENSE), bf16),
        pltpu.VMEM((3, WIDTH, FF), bf16),
        pltpu.VMEM((ROWS, WIDTH), f32),
        pltpu.VMEM((2, TOPK, ROWS), jnp.int32),
        pltpu.VMEM((ROWS, 128), f32),
        pltpu.VMEM((ROWS, 128), f32),
        pltpu.VMEM((ROWS, 128), f32),
        pltpu.VMEM((3, ROWS, WIDTH), f32),
        pltpu.VMEM((2, ROWS, WIDTH), f32),
        pltpu.VMEM((2, ROWS, WIDTH), f32),
        pltpu.VMEM((2, ROWS, WIDTH), bf16),
        pltpu.VMEM((2, ROWS, 512), bf16),
        pltpu.VMEM((2, ROWS, 256), bf16),
        pltpu.VMEM((2, PART, WIDTH), f32),
        pltpu.VMEM((2, LOCAL * CAP, ROWS), bf16),
        pltpu.VMEM((2, E, ROWS), f32),
        pltpu.VMEM((2, LOCAL * CAP, 1), f32),
        pltpu.VMEM((2, 4, ROWS, WIDTH), bf16),
        pltpu.VMEM((2, 4, 3, PART, WIDTH), bf16),
        pltpu.VMEM((2, 4, ROWS, WIDTH), bf16),
        pltpu.VMEM((2, 1, 4, 8, ROWS), f32),
        pltpu.VMEM((E, ROWS), f32),
        pltpu.VMEM((2, 2, LOCAL * CAP, WIDTH), bf16),
        pltpu.VMEM((2 * LOCAL * CAP, WIDTH), bf16),
        pltpu.VMEM((2 * LOCAL * CAP, WIDTH), bf16),
        pltpu.VMEM((2 * LOCAL * CAP, FF), f32),
        pltpu.VMEM((2 * LOCAL * CAP, FF), f32),
        pltpu.VMEM((2 * LOCAL * CAP, FF), bf16),
        pltpu.VMEM((2, 2 * LOCAL * CAP, WIDTH), bf16),
        pltpu.VMEM((2, 2, LOCAL * CAP, WIDTH), bf16),
        pltpu.VMEM((2 * LOCAL * CAP, 2 * FF), bf16),
        pltpu.VMEM((4, ROWS, ROWS), f32),
        pltpu.VMEM((8, ROWS), f32),
        pltpu.VMEM((PART, WIDTH), f32),
        pltpu.VMEM((2, 4, 8, WIDTH), f32),
        pltpu.VMEM((ROWS, WIDTH), f32),
        pltpu.VMEM((ROWS, 512), bf16),
        pltpu.VMEM((2, ROWS, WIDTH), bf16),
        pltpu.VMEM((2, ROWS, WIDTH), bf16),
        pltpu.SemaphoreType.DMA((2, 4, 3)),
        pltpu.SemaphoreType.DMA((2, 4, 3)),
        pltpu.SemaphoreType.DMA((2, 4, 3)),
        pltpu.SemaphoreType.DMA((2, 4, 3)),
        pltpu.SemaphoreType.DMA((2, 2, 3)),
        pltpu.SemaphoreType.DMA((2, 2, 3)),
        pltpu.SemaphoreType.DMA((2, 2, 8)),
        pltpu.SemaphoreType.DMA((2, 16)),
        pltpu.SemaphoreType.DMA((2, 16)),
        pltpu.SemaphoreType.DMA((2, 2, 8)),
        pltpu.SemaphoreType.DMA((2,)),
        pltpu.SemaphoreType.DMA((2,)),
        pltpu.SemaphoreType.DMA((2, 2, 3)),
        pltpu.SemaphoreType.DMA((2, 2, 3)),
        pltpu.SemaphoreType.DMA((3, 4)),
        pltpu.SemaphoreType.DMA((3, 4)),
        pltpu.SemaphoreType.DMA((64,)),
        pltpu.SemaphoreType.DMA((64,)),
        pltpu.SemaphoreType.DMA((3, 16)),
        pltpu.SemaphoreType.DMA((3, 16)),
        pltpu.SemaphoreType.DMA((64,)),
        pltpu.SemaphoreType.DMA((64,)),
        pltpu.SemaphoreType.DMA((3,)),
        pltpu.SemaphoreType.DMA((3,)),
        pltpu.SemaphoreType.DMA((3,)),
    ]
    return pl.pallas_call(
        body,
        out_shape=(
            shape((2, ROWS, WIDTH), bf16),
            shape((2, ROWS, WIDTH), bf16),
            shape((16, 64, DENSE), bf16),
            shape((2, 3, E, 64, 128), bf16),
        ),
        in_specs=[
            pl.BlockSpec(memory_space=pltpu.SMEM),
            *[pl.BlockSpec(memory_space=pltpu.VMEM) for _ in range(5)],
            *[pl.BlockSpec(memory_space=pl.ANY) for _ in range(2)],
            *[pl.BlockSpec(memory_space=pltpu.VMEM) for _ in range(2)],
        ],
        out_specs=(
            pl.BlockSpec(memory_space=pltpu.VMEM),
            pl.BlockSpec(memory_space=pltpu.VMEM),
            pl.BlockSpec(memory_space=pl.ANY),
            pl.BlockSpec(memory_space=pl.ANY),
        ),
        scratch_shapes=scratch,
        compiler_params=pltpu.CompilerParams(
            collective_id=0, has_side_effects=True, vmem_limit_bytes=60 * 1024 * 1024
        ),
        name="layers",
    )(*operands)


def local(
    boundary,
    doc_lengths,
    routes,
    norm_gains,
    w_query,
    key_value_weight,
    w_out,
    w_router,
    w_gateup,
    w_down,
):
    outs, grads, parts, pieces = layers(
        doc_lengths[:, 0], w_query[0], key_value_weight[0], w_out[0].T, w_router[0].T, norm_gains[0],
        w_gateup[0], jnp.swapaxes(w_down[0], 1, 2), boundary[0], jnp.swapaxes(routes[0], 1, 2),
    )
    parts = jnp.sum(parts.astype(f32), axis=0)
    pieces = pieces.astype(f32)
    return (
        outs.astype(f32)[None],
        grads.astype(f32)[None],
        parts[:, 800:802].T[None],
        parts[:, 0:256][None],
        jnp.stack([parts[:, 256:384], parts[:, 384:512]])[None],
        parts[:, 512:768].T[None],
        parts[:, 768:800][None],
        (pieces[0, 0:2] + pieces[1, 0:2])[None],
        jnp.swapaxes(pieces[0, 2] + pieces[1, 2], 1, 2)[None],
    )


def solution(mesh):
    placed = (
        P("section", None, "dp", None),
        P(None, "dp", None),
        P("section", None, "dp", None),
        P("section", None, "dp"),
        P("section", "dp", "tensor"),
        P("section", None, "dp", "tensor"),
        P("section", "tensor", "dp"),
        P("section", "dp", None),
        P("section", None, None, "dp", "tensor"),
        P("section", None, "tensor", "dp"),
    )
    return jax.shard_map(
        local,
        mesh=mesh,
        in_specs=placed,
        out_specs=(
            P("section", None, "dp", None),
            P("section", None, "dp", None),
            P("section", None, "dp"),
            P("section", "dp", "tensor"),
            P("section", None, "dp", "tensor"),
            P("section", "tensor", "dp"),
            P("section", "dp", None),
            P("section", None, None, "dp", "tensor"),
            P("section", None, "tensor", "dp"),
        ),
        check_vma=False,
    )
```

```python
import math

import jax
import jax.numpy as jnp
from jax import lax
from jax.experimental import pallas as pl
from jax.experimental.pallas import tpu as pltpu
from jax.sharding import PartitionSpec as P

HEAD_SIZE = 64
E = 32
TOPK = 8
CAP = 48
ROWS = 128
WIDTH = 1024
FF = 512
PART = 32
LOCAL = 8
DENSE = 896

epsilon = 1e-06
rope_base = 10000.0
masked_score = -1e30
f32 = jnp.float32
bf16 = jnp.bfloat16
MESH = pl.DeviceIdType.MESH


def dot(a, b):
    return lax.dot_general(a, b, (((1,), (0,)), ((), ())), preferred_element_type=f32)


def dot_nt(a, b):
    return lax.dot_general(a, b, (((1,), (1,)), ((), ())), preferred_element_type=f32)


def dot_tn(a, b):
    return lax.dot_general(a, b, (((0,), (0,)), ((), ())), preferred_element_type=f32)


def unit(rows, columns, shift):
    row = lax.broadcasted_iota(jnp.int32, (rows, columns), 0)
    column = lax.broadcasted_iota(jnp.int32, (rows, columns), 1)
    return (row + shift == column).astype(bf16)


def scale_of(values):
    return lax.rsqrt(jnp.mean(values * values, axis=1, keepdims=True) + epsilon)


def norm_back(values, gain_row, upstream):
    scale = scale_of(values)
    weighted = upstream * gain_row
    inner = jnp.mean(weighted * values, axis=1, keepdims=True)
    back = scale * weighted - values * (scale * scale * scale * inner)
    return back, jnp.sum(upstream * values * scale, axis=0, keepdims=True)


def low_lanes():
    return lax.broadcasted_iota(jnp.int32, (ROWS, 128), 1) < 64


def turn(chunk, cos, sin):
    place = lax.broadcasted_iota(jnp.int32, (ROWS, 128), 1) % 64
    swapped = jnp.where(place < 32, pltpu.roll(chunk, 96, 1), pltpu.roll(chunk, 32, 1))
    return chunk * cos + swapped * sin


def doubled(both):
    wide = both.astype(f32)
    other = pltpu.roll(wide, 64, 1)
    left = low_lanes()
    return (
        jnp.where(left, wide, other).astype(bf16),
        jnp.where(left, other, wide).astype(bf16),
    )


def half(chunk, which):
    left = low_lanes()
    keep = left if which == 0 else jnp.logical_not(left)
    return jnp.where(keep, chunk, jnp.zeros_like(chunk))


def soft(query_half, keys, seen):
    scores = dot_nt(query_half, keys) * HEAD_SIZE ** (-0.5)
    scores = jnp.where(seen, scores, masked_score)
    raised = jnp.exp(scores - jnp.max(scores, axis=1, keepdims=True))
    return raised / jnp.sum(raised, axis=1, keepdims=True)


def body(
    lengths, query_own, keyval_own, out_own, router_own, gains_own, gateup_own, down_own,
    boundary, routes_own,
    out_ref, grad_ref, parts, pieces,
    own, dense, experts, dense_grad, shared, expert_grad, other, routes, cos_ref, sin_ref, seen_ref,
    xin, uin, turned, first_in, qkv, mixed, middle, chosen, chance, slot_gate,
    rs_send, rs_recv, ag, small, slots, packed, x_rows, og_rows, gate_s, up_s, hid_s,
    y_rows, ret, gu_low, probs, gate_grads, resid, gains, router_back, dqkv, swap_out, swap_in,
    rs_ss, rs_rs, ag_ss, ag_rs, sm_ss, sm_rs, d_ss, d_rs, r_ss, r_rs, w_ss, w_rs,
    a_ss, a_rs, b_ss, b_rs, e_ss, e_rs, g_ss, g_rs, p_ss, p_rs, h_ss, h_rs, c_ss,
):
    s = lax.axis_index("section")
    x = lax.axis_index("tensor")
    d = lax.axis_index("dp")
    z, y = d // 4, d % 4
    zz = z % 2
    mine = zz * 4 + (y + 2 * (z // 2)) % 4
    rows_mine = pl.ds(pl.multiple_of(x * PART, PART), PART)
    experts_mine = pl.ds(pl.multiple_of(x * LOCAL, LOCAL), LOCAL)
    odd = (y + z) % 2
    steps = (
        (0, 0), (1, 0), (3, 0), (0, 1), (0, 3),
        (1 + 2 * odd, 1 + 2 * odd), (3 - 2 * odd, 1 + 2 * odd), (2 - 2 * odd, 2 * odd),
    )

    def holder(n):
        y2, z2 = (y + steps[n][0]) % 4, (z + steps[n][1]) % 4
        return z2 % 2 * 4 + (y2 + 2 * (z2 // 2)) % 4, z2 * 4 + y2

    def sender(n):
        return (z + 4 - steps[n][1]) % 4 * 4 + (y + 4 - steps[n][0]) % 4

    barrier = pltpu.get_barrier_semaphore()

    def greet(k, carry):
        there, at = (x + k // 16) % 4, (d + k % 16) % 16

        @pl.when(k > 0)
        def _():
            pl.semaphore_signal(
                barrier, inc=1, device_id={"tensor": there, "dp": at}, device_id_type=MESH
            )

        return carry

    lax.fori_loop(0, 64, greet, 0)
    for peer in [holder(n)[1] for n in range(8)] + [sender(5), sender(6)]:
        pl.semaphore_signal(
            barrier, inc=1, device_id={"section": 1 - s, "dp": peer}, device_id_type=MESH
        )

    row = lax.broadcasted_iota(jnp.int32, (ROWS, 128), 0)
    lane = lax.broadcasted_iota(jnp.int32, (ROWS, 128), 1)
    start, row_doc, lane_doc, end = 0, 0, 0, 0
    for k in range(3):
        size = lengths[s, k]
        end = end + size
        start = start + jnp.where(row >= end, size, 0)
        row_doc = row_doc + jnp.where(row >= end, 1, 0)
        lane_doc = lane_doc + jnp.where(lane >= end, 1, 0)
    step = (lane % 32).astype(f32) * (-2.0 / HEAD_SIZE * math.log(rope_base))
    angles = (row - start).astype(f32) * jnp.exp(step)
    sine = jnp.sin(angles)
    cos_ref[...] = jnp.cos(angles)
    sin_ref[...] = jnp.where(lane % 64 < 32, -sine, sine)
    seen_ref[...] = jnp.where((row_doc == lane_doc) & (lane <= row), 1.0, 0.0)

    pl.semaphore_wait(barrier, 73)

    def remote(src, dst, send, recv, device):
        return pltpu.make_async_remote_copy(
            src_ref=src, dst_ref=dst, send_sem=send, recv_sem=recv,
            device_id=device, device_id_type=MESH,
        )

    def scatter_copies(l, j):
        copies = []
        for k in (2, 1, 3):
            p = (x + k) % 4
            src = rs_send.at[l, j, pl.ds(pl.multiple_of(p * PART, PART), PART)]
            copies.append(
                remote(src, rs_recv.at[l, j, k - 1], rs_ss.at[l, j, k - 1],
                       rs_rs.at[l, j, k - 1], {"tensor": p})
            )
        return copies

    def scatter_start(l, j, partial):
        rs_send[l, j] = partial.astype(bf16)
        for copy in scatter_copies(l, j):
            copy.start()

    def scatter_end(l, j):
        for copy in scatter_copies(l, j):
            copy.wait()
        total = rs_send[l, j, rows_mine].astype(f32)
        for k in range(3):
            total = total + rs_recv[l, j, k].astype(f32)
        return total

    def gather_copies(l, j):
        copies = []
        for k in (2, 1, 3):
            ref = ag.at[l, j, rows_mine]
            copies.append(
                remote(ref, ref, ag_ss.at[l, j, k - 1], ag_rs.at[l, j, k - 1],
                       {"tensor": (x + k) % 4})
            )
        return copies

    def gather_start(l, j, rows):
        ag[l, j, rows_mine] = rows.astype(bf16)
        for copy in gather_copies(l, j):
            copy.start()

    def gather_end(l, j):
        for copy in gather_copies(l, j):
            copy.wait()

    def small_copies(l, j):
        copies = []
        for k in range(1, 4):
            ref = small.at[l, j, x]
            copies.append(
                remote(ref, ref, sm_ss.at[l, j, k - 1], sm_rs.at[l, j, k - 1],
                       {"tensor": (x + k) % 4})
            )
        return copies

    def block(index):
        return pl.ds(pl.multiple_of(index * CAP, CAP), CAP)

    def dispatch_copies(l, way, act):
        rel = (s + l) % 2
        target = x_rows if way == 0 else og_rows
        for n in (5, 6, 7, 1, 2, 3, 4, 0):
            i, peer = holder(n)
            src = packed.at[l, way, block(i)]
            dst = target.at[block(rel * 8 + n)]
            far = remote(src, dst, d_ss.at[l, way, n], d_rs.at[way, rel * 8 + n],
                         {"section": l, "dp": peer})
            if n == 0:
                @pl.when(s == l)
                def _():
                    if act == 0:
                        pltpu.make_async_copy(src, dst, d_rs.at[way, 0]).start()

                @pl.when(s != l)
                def _():
                    if act == 0:
                        far.start()
                    else:
                        far.wait_send()
            elif act == 0:
                far.start()
            else:
                far.wait_send()

    def dispatch_arrived(way, rel):
        target = x_rows if way == 0 else og_rows

        def far(n):
            return remote(
                packed.at[0, way, block(n)], target.at[block(rel * 8 + n)],
                d_ss.at[0, way, n], d_rs.at[way, rel * 8 + n], {"dp": holder(1)[1]},
            )

        @pl.when(rel == 0)
        def _():
            pltpu.make_async_copy(
                packed.at[0, way, block(mine)], target.at[block(0)], d_rs.at[way, 0]
            ).wait()

        @pl.when(rel != 0)
        def _():
            far(0).wait_recv()

        for n in range(1, 8):
            far(n).wait_recv()

    def return_copies(l, way, rel, act):
        for n in (5, 6, 7, 1, 2, 3, 4, 0):
            peer = sender(n)
            src = y_rows.at[way, block(rel * 8 + n)]
            dst = ret.at[l, way, block(mine)]
            def far():
                return remote(src, dst, r_ss.at[way, rel * 8 + n], r_rs.at[l, way, n],
                              {"section": (s + rel) % 2, "dp": peer})

            def go():
                if act == 0:
                    far().start()
                else:
                    far().wait_send()

            if n > 0:
                go()
            else:
                pl.when(rel != 0)(go)
                if act == 0:
                    @pl.when(rel == 0)
                    def _():
                        pltpu.make_async_copy(src, dst, r_rs.at[l, way, 0]).start()

    def return_arrived(l, way):
        for n in range(8):
            i, peer = holder(n)
            src = y_rows.at[way, block(n)]
            dst = ret.at[l, way, block(i)]
            far = remote(src, dst, r_ss.at[way, n], r_rs.at[l, way, n],
                         {"section": 1 - s, "dp": peer})
            if n == 0:
                @pl.when(s == l)
                def _():
                    pltpu.make_async_copy(src, dst, r_rs.at[l, way, 0]).wait()

                @pl.when(s != l)
                def _():
                    far.wait_recv()
            else:
                far.wait_recv()

    def swap_copy(way):
        return remote(swap_out.at[way], swap_in.at[way], w_ss.at[way], w_rs.at[way],
                      {"section": 1 - s})

    def keep_result(way, l, ref):
        @pl.when(s == l)
        def _():
            ref[s] = ag[l, 1 + 2 * way]

        @pl.when(s != l)
        def _():
            swap_out[way] = ag[l, 1 + 2 * way]
            swap_copy(way).start()

    def block64(index):
        return pl.ds(pl.multiple_of(index * 64, 64), 64)

    def block128(index):
        return pl.ds(pl.multiple_of(index * 128, 128), 128)

    left, right = slice(0, 512), slice(512, DENSE)

    def along_y(k):
        return {"dp": z * 4 + (y + k) % 4}

    def along_z(k):
        return {"dp": ((z + k) % 4) * 4 + y}

    def spread_copies(part, phase):
        copies = []
        for k in range(1, 4):
            if part == 0:
                ref = dense.at[s, z, y, :, left] if phase == 0 else dense.at[s, z, :, :, left]
                device = along_y(k) if phase == 0 else along_z(k)
            else:
                ref = dense.at[s, z, y, :, right] if phase == 0 else dense.at[s, :, y, :, right]
                device = along_z(k) if phase == 0 else along_y(k)
            n = k - 1
            copies.append(
                remote(ref, ref, a_ss.at[part, phase, n], a_rs.at[part, phase, n], device)
            )
        return copies

    def sibling_copy(part, k, layer):
        if part == 0:
            ref = dense.at[layer, (z + k) % 4, :, :, left]
        else:
            ref = dense.at[layer, :, (y + k) % 4, :, right]
        return remote(ref, ref, b_ss.at[part, k], b_rs.at[part, k], {"section": 1 - s})

    def weight_copy(kind):
        src = gateup_own.at[kind] if kind < 2 else down_own
        return pltpu.make_async_copy(src, own.at[:, kind], c_ss.at[kind])

    def exchange_copies():
        return [
            remote(boundary.at[1 - s], other, b_ss.at[2, 0], b_rs.at[2, 0], {"section": 1 - s}),
            remote(routes_own.at[1 - s], routes.at[s], b_ss.at[2, 1], b_rs.at[2, 1],
                   {"section": 1 - s}),
        ]

    def expert_copy(k, local_only=False):
        there, at = (x + k // 16) % 4, (d + k % 16) % 16
        e = there * 8 + at // 4 % 2 * 4 + (at % 4 + 2 * (at // 8)) % 4
        src, dst = own.at[e], experts.at[:, block64(d), block128(x)]
        if local_only:
            return pltpu.make_async_copy(src, dst, e_rs.at[0])
        return remote(src, dst, e_ss.at[k], e_rs.at[k], {"tensor": there, "dp": at})

    def piece_copy(k, local_only=False):
        there, at = (x + k // 16) % 4, (d + k % 16) % 16
        src = expert_grad.at[:, block64(at), block128(there)]
        dst = pieces.at[z // 2, :, x * 8 + mine]
        if local_only:
            return pltpu.make_async_copy(src, dst, p_rs.at[0])
        return remote(src, dst, p_ss.at[k], p_rs.at[k], {"tensor": there, "dp": at})

    def all_but_own(copy, act, low=1, high=64):
        def one(n, carry):
            getattr(copy(n * 13 % 64), act)()
            return carry

        lax.fori_loop(low, high, one, 0)

    def push(copy, low, high):
        whole = isinstance(low, int) and low == 0
        if whole:
            copy(0, True).start()
        all_but_own(copy, "start", 1 if whole else low, high)

    def push_when(condition, copy, low, high):
        pl.when(condition)(lambda: push(copy, low, high))

    def arrive(copy):
        copy(0, True).wait()
        all_but_own(copy, "wait_recv")

    wide = (slice(0, 512), slice(512, 768), slice(768, DENSE))

    def part_copy(c, k, local_only=False):
        at = (d + k) % 16
        src = dense_grad.at[s, block64(at), wide[c]]
        dst = parts.at[d, :, wide[c]]
        if local_only:
            return pltpu.make_async_copy(src, dst, g_rs.at[c, 0])
        return remote(src, dst, g_ss.at[c, k], g_rs.at[c, k], {"dp": at})

    def share_copy(c):
        return remote(dense_grad.at[1 - s, :, wide[c]], shared.at[:, wide[c]],
                      h_ss.at[c], h_rs.at[c], {"section": 1 - s})

    def share(l, c):
        @pl.when(s != l)
        def _():
            share_copy(c).start()

    def part_push(l, c):
        @pl.when(s == l)
        def _():
            share_copy(c).wait_recv()
            both = dense_grad[l, :, wide[c]].astype(f32) + shared[:, wide[c]].astype(f32)
            dense_grad[l, :, wide[c]] = both.astype(bf16)
            part_copy(c, 0, True).start()

            def one(k, carry):
                part_copy(c, k).start()
                return carry

            lax.fori_loop(1, 16, one, 0)

    for copy in exchange_copies():
        copy.start()
    for kind in range(3):
        weight_copy(kind).start()
    routes[s] = routes_own[s]
    dense[s, z, y, :, 0:256] = query_own[...]
    dense[s, z, y, :, 256:384] = keyval_own[0]
    dense[s, z, y, :, 384:512] = keyval_own[1]
    dense[s, z, y, :, 512:768] = out_own[...]
    last = dot_tn(router_own[...], unit(E, 128, 0)) + dot_tn(gains_own[...], unit(2, 128, E))
    dense[s, z, y, :, 768:896] = last.astype(bf16)
    for part in range(2):
        for copy in spread_copies(part, 0):
            copy.start()


    @pl.when(s == 0)
    def _():
        xin[0] = boundary[0]

    @pl.when(s == 1)
    def _():
        uin[1] = boundary[1]

    for part in range(2):
        for copy in spread_copies(part, 0):
            copy.wait()
    for kind in range(3):
        weight_copy(kind).wait()

    def spread_start():
        for part in range(2):
            for copy in spread_copies(part, 1):
                copy.start()
            sibling_copy(part, 0, s).start()

    def spread_end():
        for part in range(2):
            for k in range(3):
                spread_copies(part, 1)[k].wait()
                sibling_copy(part, 3 - k, s).start()

    @pl.when(s == 0)
    def _():
        spread_start()
        push(expert_copy, 0, 64)
        spread_end()

    @pl.when(s == 1)
    def _():
        for copy in exchange_copies()[:1]:
            copy.wait()
        xin[0] = other[...]

    def weight(l, low, high):
        return dense[l, :, :, :, low:high].reshape(WIDTH, high - low)

    def forward(l, carry):
        @pl.when(s != l)
        def _():
            for part in range(2):
                for k in range(4):
                    sibling_copy(part, k, s).wait_recv()
            exchange_copies()[1].wait()

        turned[l] = weight(l, 768, 896).astype(f32).T
        values = xin[l]
        first = (values * scale_of(values) * turned[l, 32:33]).astype(bf16)
        first_in[l] = first
        made = dot(first, weight(l, 0, 512))
        cos, sin = cos_ref[...], sin_ref[...]
        for c in range(3):
            cut = slice(128 * c, 128 * c + 128)
            qkv[l, :, cut] = turn(made[:, cut], cos, sin).astype(bf16)
        qkv[l, :, 384:512] = made[:, 384:512].astype(bf16)
        seen = seen_ref[...] > 0
        keys = doubled(qkv[l, :, 256:384])
        vals = doubled(qkv[l, :, 384:512])
        for c in range(2):
            cut = slice(128 * c, 128 * c + 128)
            query = qkv[l, :, cut]
            got = [
                dot(soft(half(query, b), keys[c], seen).astype(bf16), vals[c]) for b in range(2)
            ]
            mixed[l, :, cut] = jnp.where(low_lanes(), got[0], got[1]).astype(bf16)
        scatter_start(l, 0, dot_nt(mixed[l], weight(l, 512, 768)))


        @pl.when((s == 1) & (l == 0))
        def _():
            push(expert_copy, 0, 64)

        experts_iota = lax.broadcasted_iota(jnp.int32, (E, ROWS), 0)
        named = jnp.zeros((E, ROWS), f32)
        for k in range(TOPK):
            named = named + (experts_iota == routes[l, k:k + 1]).astype(f32)
        before = (
            lax.broadcasted_iota(jnp.int32, (ROWS, ROWS), 0)
            < lax.broadcasted_iota(jnp.int32, (ROWS, ROWS), 1)
        ).astype(bf16)
        place = dot(named.astype(bf16), before)
        slots[...] = jnp.where(named > 0, place, -1.0)
        place = slots[experts_mine]
        slot_iota = lax.broadcasted_iota(jnp.int32, (CAP, ROWS), 0).astype(f32)
        for i in range(LOCAL):
            chosen[l, CAP * i:CAP * i + CAP] = (slot_iota == place[i:i + 1]).astype(bf16)

        center = xin[l, rows_mine] + scatter_end(l, 0)
        middle[l] = center
        gather_start(l, 0, center * scale_of(center) * turned[l, 33:34])
        gather_end(l, 0)

        second = ag[l, 0]
        packed[l, 0] = dot(chosen[l], second).astype(bf16)
        dispatch_copies(l, 0, 0)
        pl.when((s == 1) & (l == 0))(spread_start)
        logits = dot_nt(turned[l, 0:32].astype(bf16), second)
        logits = jnp.where(named > 0, logits, masked_score)
        raised = jnp.where(named > 0, jnp.exp(logits - jnp.max(logits, axis=0, keepdims=True)), 0.0)
        chance[l] = raised / jnp.sum(raised, axis=0, keepdims=True)
        gate = chance[l, experts_mine]
        for i in range(LOCAL):
            cut = slice(CAP * i, CAP * i + CAP)
            weighted = chosen[l, cut].astype(f32) * gate[i:i + 1]
            slot_gate[l, cut] = jnp.sum(weighted, axis=1, keepdims=True)

        @pl.when(s == l)
        def _():
            arrive(expert_copy)
            for turn_no in range(2):
                rel = (l + turn_no) % 2
                dispatch_arrived(0, rel)
                cut = pl.ds(pl.multiple_of(384 * rel, 384), 384)
                rows = x_rows[cut]
                gate_part = dot(rows, experts[0])
                up_part = dot(rows, experts[1])
                gate_s[cut] = gate_part
                up_s[cut] = up_part
                hidden = (gate_part / (1.0 + jnp.exp(-gate_part)) * up_part).astype(bf16)
                hid_s[cut] = hidden
                y_rows[0, cut] = dot_nt(hidden, experts[2]).astype(bf16)
                return_copies(l, 0, rel, 0)

        @pl.when((s == 1) & (l == 0))
        def _():
            spread_end()

        return_arrived(l, 0)
        scaled = ret[l, 0].astype(f32) * slot_gate[l]
        scatter_start(l, 1, dot_tn(chosen[l], scaled.astype(bf16)))
        gather_start(l, 1, middle[l] + scatter_end(l, 1))
        gather_end(l, 1)
        xin[l + 1] = ag[l, 1].astype(f32)
        keep_result(0, l, out_ref)
        dispatch_copies(l, 0, 1)
        return carry

    lax.fori_loop(0, 2, forward, 0)

    @pl.when(s == 0)
    def _():
        for copy in exchange_copies()[:1]:
            copy.wait()
        uin[1] = other[...]

    def backward(step, carry):
        l = 1 - step
        upstream = uin[l].astype(bf16)
        spread = dot(chosen[l], upstream)
        packed[l, 1] = (spread * slot_gate[l]).astype(bf16)
        dispatch_copies(l, 1, 0)
        inner = jnp.sum(spread * ret[l, 0].astype(f32), axis=1, keepdims=True)
        for i in range(LOCAL):
            cut = slice(CAP * i, CAP * i + CAP)
            row = jnp.sum(chosen[l, cut].astype(f32) * inner[cut], axis=0, keepdims=True)
            gate_grads[i:i + 1] = row
        small[l, 0, x, 0:8] = gate_grads[...]
        for copy in small_copies(l, 0):
            copy.start()

        @pl.when(s == l)
        def _():
            for turn_no in range(2):
                rel = (l + turn_no) % 2
                dispatch_arrived(1, rel)
                cut = pl.ds(pl.multiple_of(384 * rel, 384), 384)
                hidden_grad = dot(og_rows[cut], experts[2])
                gate_part = gate_s[cut]
                up_part = up_s[cut]
                sig = 1.0 / (1.0 + jnp.exp(-gate_part))
                gate_low = (
                    hidden_grad * up_part * sig * (1.0 + gate_part * (1.0 - sig))
                ).astype(bf16)
                up_low = (hidden_grad * gate_part * sig).astype(bf16)
                gu_low[cut, 0:FF] = gate_low
                gu_low[cut, FF:2 * FF] = up_low
                back = dot_nt(gate_low, experts[0]) + dot_nt(up_low, experts[1])
                y_rows[1, cut] = back.astype(bf16)
                return_copies(l, 1, rel, 0)
            both = dot_tn(x_rows[...], gu_low[...])
            expert_grad[0] = both[:, 0:FF].astype(bf16)
            expert_grad[1] = both[:, FF:2 * FF].astype(bf16)

        for copy in small_copies(l, 0):
            copy.wait()
        gate = chance[l]
        gate_total = jnp.concatenate([small[l, 0, p, 0:8] for p in range(4)], axis=0)
        picked = gate * (gate_total - jnp.sum(gate * gate_total, axis=0, keepdims=True))
        logit_low = picked.astype(bf16)
        router_back[...] = dot_tn(logit_low, turned[l, 0:32].astype(bf16))
        return_arrived(l, 1)
        scatter_start(l, 2, dot_tn(chosen[l], ret[l, 1]))

        @pl.when(s == l)
        def _():
            expert_grad[2] = dot_tn(og_rows[...], hid_s[...]).astype(bf16)
            push(piece_copy, 0, 16)

        router_grad = dot(logit_low, ag[l, 0])
        arrived = scatter_end(l, 2) + router_back[rows_mine]
        back, gain_two = norm_back(middle[l], turned[l, 33:34], arrived)
        kept = uin[l, rows_mine] + back
        resid[...] = kept
        gather_start(l, 2, kept)
        push_when(s == l, piece_copy, 16, 24)
        seen = seen_ref[...] > 0
        keys = doubled(qkv[l, :, 256:384])
        for h in range(4):
            query = qkv[l, :, 128 * (h // 2):128 * (h // 2) + 128]
            probs[h] = soft(half(query, h % 2), keys[h // 2], seen)
        gather_end(l, 2)

        branch = ag[l, 2]
        push_when(s == l, piece_copy, 24, 40)
        mixed_grad = dot(branch, weight(l, 512, 768)).astype(bf16)
        cos, sin = cos_ref[...], -sin_ref[...]
        left = low_lanes()
        vals = doubled(qkv[l, :, 384:512])
        key_grads, value_grads = [], []
        for c in range(2):
            cut = slice(128 * c, 128 * c + 128)
            query, above = qkv[l, :, cut], mixed_grad[:, cut]
            parts, key_grad, value_grad = [], 0.0, 0.0
            for b in range(2):
                query_half, above_half = half(query, b), half(above, b)
                prob = probs[2 * c + b]
                value_grad = value_grad + dot_tn(prob.astype(bf16), above_half)
                prob_grad = dot_nt(above_half, vals[c])
                mean = jnp.sum(prob * prob_grad, axis=1, keepdims=True)
                score_low = (prob * (prob_grad - mean)).astype(bf16)
                parts.append(dot(score_low, keys[c]))
                key_grad = key_grad + dot_tn(score_low, query_half)
            query_grad = jnp.where(left, parts[0], parts[1]) * HEAD_SIZE ** (-0.5)
            dqkv[:, cut] = turn(query_grad, cos, sin).astype(bf16)
            key_grads.append(key_grad + pltpu.roll(key_grad, 64, 1))
            value_grads.append(value_grad + pltpu.roll(value_grad, 64, 1))
        key_grad = jnp.where(left, key_grads[0], key_grads[1]) * HEAD_SIZE ** (-0.5)
        dqkv[:, 256:384] = turn(key_grad, cos, sin).astype(bf16)
        dqkv[:, 384:512] = jnp.where(left, value_grads[0], value_grads[1]).astype(bf16)
        scatter_start(l, 3, dot_nt(dqkv[...], weight(l, 0, 512)))
        push_when(s == l, piece_copy, 40, 48)
        dense_grad[l, :, 512:768] = dot_tn(branch, mixed[l]).astype(bf16)
        share(l, 1)
        dense_grad[l, :, 0:512] = dot_tn(first_in[l], dqkv[...]).astype(bf16)
        share(l, 0)
        part_push(l, 1)
        back, gain_one = norm_back(xin[l, rows_mine], turned[l, 32:33], scatter_end(l, 3))
        gather_start(l, 3, resid[...] + back)
        push_when(s == l, piece_copy, 48, 56)
        gains[l, x, 0:1] = gain_one
        gains[l, x, 1:2] = gain_two
        for k in range(1, 4):
            ref = gains.at[l, x]
            remote(ref, ref, sm_ss.at[l, 1, k - 1], sm_rs.at[l, 1, k - 1],
                   {"tensor": (x + k) % 4}).start()
        part_push(l, 0)
        gather_end(l, 3)
        uin[1 - l] = ag[l, 3].astype(f32)
        keep_result(1, l, grad_ref)
        for k in range(1, 4):
            ref = gains.at[l, x]
            remote(ref, ref, sm_ss.at[l, 1, k - 1], sm_rs.at[l, 1, k - 1],
                   {"tensor": (x + k) % 4}).wait()
        total = gains[l, 0] + gains[l, 1] + gains[l, 2] + gains[l, 3]
        last = jnp.concatenate([router_grad, total, jnp.zeros((88, WIDTH), f32)], axis=0)
        dense_grad[l, :, 768:896] = last.T.astype(bf16)
        push_when(s == l, piece_copy, 56, 64)
        share(l, 2)
        part_push(l, 2)
        dispatch_copies(l, 1, 1)
        return carry

    lax.fori_loop(0, 2, backward, 0)

    for way, ref in ((0, out_ref), (1, grad_ref)):
        swap_copy(way).wait()
        ref[1 - s] = swap_in[way]
        for rel in range(2):
            return_copies(s, way, jnp.int32(rel), 1)
    for part in range(2):
        for k in range(4):
            sibling_copy(part, k, s).wait_send()
    all_but_own(expert_copy, "wait_send")
    all_but_own(piece_copy, "wait_send")
    arrive(piece_copy)
    for c in range(3):
        share_copy(c).wait_send()
        part_copy(c, 0, True).wait()

        def one(k, carry):
            part_copy(c, k).wait()
            return carry

        lax.fori_loop(1, 16, one, 0)


def layers(*operands):
    shape = jax.ShapeDtypeStruct
    scratch = [
        pltpu.VMEM((E, 3, 64, 128), bf16),
        pltpu.VMEM((2, 4, 4, 64, DENSE), bf16),
        pltpu.VMEM((3, WIDTH, FF), bf16),
        pltpu.VMEM((2, WIDTH, DENSE), bf16),
        pltpu.VMEM((WIDTH, DENSE), bf16),
        pltpu.VMEM((3, WIDTH, FF), bf16),
        pltpu.VMEM((ROWS, WIDTH), f32),
        pltpu.VMEM((2, TOPK, ROWS), jnp.int32),
        pltpu.VMEM((ROWS, 128), f32),
        pltpu.VMEM((ROWS, 128), f32),
        pltpu.VMEM((ROWS, 128), f32),
        pltpu.VMEM((3, ROWS, WIDTH), f32),
        pltpu.VMEM((2, ROWS, WIDTH), f32),
        pltpu.VMEM((2, ROWS, WIDTH), f32),
        pltpu.VMEM((2, ROWS, WIDTH), bf16),
        pltpu.VMEM((2, ROWS, 512), bf16),
        pltpu.VMEM((2, ROWS, 256), bf16),
        pltpu.VMEM((2, PART, WIDTH), f32),
        pltpu.VMEM((2, LOCAL * CAP, ROWS), bf16),
        pltpu.VMEM((2, E, ROWS), f32),
        pltpu.VMEM((2, LOCAL * CAP, 1), f32),
        pltpu.VMEM((2, 4, ROWS, WIDTH), bf16),
        pltpu.VMEM((2, 4, 3, PART, WIDTH), bf16),
        pltpu.VMEM((2, 4, ROWS, WIDTH), bf16),
        pltpu.VMEM((2, 1, 4, 8, ROWS), f32),
        pltpu.VMEM((E, ROWS), f32),
        pltpu.VMEM((2, 2, LOCAL * CAP, WIDTH), bf16),
        pltpu.VMEM((2 * LOCAL * CAP, WIDTH), bf16),
        pltpu.VMEM((2 * LOCAL * CAP, WIDTH), bf16),
        pltpu.VMEM((2 * LOCAL * CAP, FF), f32),
        pltpu.VMEM((2 * LOCAL * CAP, FF), f32),
        pltpu.VMEM((2 * LOCAL * CAP, FF), bf16),
        pltpu.VMEM((2, 2 * LOCAL * CAP, WIDTH), bf16),
        pltpu.VMEM((2, 2, LOCAL * CAP, WIDTH), bf16),
        pltpu.VMEM((2 * LOCAL * CAP, 2 * FF), bf16),
        pltpu.VMEM((4, ROWS, ROWS), f32),
        pltpu.VMEM((8, ROWS), f32),
        pltpu.VMEM((PART, WIDTH), f32),
        pltpu.VMEM((2, 4, 8, WIDTH), f32),
        pltpu.VMEM((ROWS, WIDTH), f32),
        pltpu.VMEM((ROWS, 512), bf16),
        pltpu.VMEM((2, ROWS, WIDTH), bf16),
        pltpu.VMEM((2, ROWS, WIDTH), bf16),
        pltpu.SemaphoreType.DMA((2, 4, 3)),
        pltpu.SemaphoreType.DMA((2, 4, 3)),
        pltpu.SemaphoreType.DMA((2, 4, 3)),
        pltpu.SemaphoreType.DMA((2, 4, 3)),
        pltpu.SemaphoreType.DMA((2, 2, 3)),
        pltpu.SemaphoreType.DMA((2, 2, 3)),
        pltpu.SemaphoreType.DMA((2, 2, 8)),
        pltpu.SemaphoreType.DMA((2, 16)),
        pltpu.SemaphoreType.DMA((2, 16)),
        pltpu.SemaphoreType.DMA((2, 2, 8)),
        pltpu.SemaphoreType.DMA((2,)),
        pltpu.SemaphoreType.DMA((2,)),
        pltpu.SemaphoreType.DMA((2, 2, 3)),
        pltpu.SemaphoreType.DMA((2, 2, 3)),
        pltpu.SemaphoreType.DMA((3, 4)),
        pltpu.SemaphoreType.DMA((3, 4)),
        pltpu.SemaphoreType.DMA((64,)),
        pltpu.SemaphoreType.DMA((64,)),
        pltpu.SemaphoreType.DMA((3, 16)),
        pltpu.SemaphoreType.DMA((3, 16)),
        pltpu.SemaphoreType.DMA((64,)),
        pltpu.SemaphoreType.DMA((64,)),
        pltpu.SemaphoreType.DMA((3,)),
        pltpu.SemaphoreType.DMA((3,)),
        pltpu.SemaphoreType.DMA((3,)),
    ]
    return pl.pallas_call(
        body,
        out_shape=(
            shape((2, ROWS, WIDTH), bf16),
            shape((2, ROWS, WIDTH), bf16),
            shape((16, 64, DENSE), bf16),
            shape((2, 3, E, 64, 128), bf16),
        ),
        in_specs=[
            pl.BlockSpec(memory_space=pltpu.SMEM),
            *[pl.BlockSpec(memory_space=pltpu.VMEM) for _ in range(5)],
            *[pl.BlockSpec(memory_space=pl.ANY) for _ in range(2)],
            *[pl.BlockSpec(memory_space=pltpu.VMEM) for _ in range(2)],
        ],
        out_specs=(
            pl.BlockSpec(memory_space=pltpu.VMEM),
            pl.BlockSpec(memory_space=pltpu.VMEM),
            pl.BlockSpec(memory_space=pl.ANY),
            pl.BlockSpec(memory_space=pl.ANY),
        ),
        scratch_shapes=scratch,
        compiler_params=pltpu.CompilerParams(
            collective_id=0, has_side_effects=True, vmem_limit_bytes=60 * 1024 * 1024
        ),
        name="layers",
    )(*operands)


def local(
    boundary,
    doc_lengths,
    routes,
    norm_gains,
    w_query,
    key_value_weight,
    w_out,
    w_router,
    w_gateup,
    w_down,
):
    outs, grads, parts, pieces = layers(
        doc_lengths[:, 0], w_query[0], key_value_weight[0], w_out[0].T, w_router[0].T, norm_gains[0],
        w_gateup[0], jnp.swapaxes(w_down[0], 1, 2), boundary[0], jnp.swapaxes(routes[0], 1, 2),
    )
    parts = jnp.sum(parts.astype(f32), axis=0)
    pieces = pieces.astype(f32)
    return (
        outs.astype(f32)[None],
        grads.astype(f32)[None],
        parts[:, 800:802].T[None],
        parts[:, 0:256][None],
        jnp.stack([parts[:, 256:384], parts[:, 384:512]])[None],
        parts[:, 512:768].T[None],
        parts[:, 768:800][None],
        (pieces[0, 0:2] + pieces[1, 0:2])[None],
        jnp.swapaxes(pieces[0, 2] + pieces[1, 2], 1, 2)[None],
    )


def solution(mesh):
    placed = (
        P("section", None, "dp", None),
        P(None, "dp", None),
        P("section", None, "dp", None),
        P("section", None, "dp"),
        P("section", "dp", "tensor"),
        P("section", None, "dp", "tensor"),
        P("section", "tensor", "dp"),
        P("section", "dp", None),
        P("section", None, None, "dp", "tensor"),
        P("section", None, "tensor", "dp"),
    )
    return jax.shard_map(
        local,
        mesh=mesh,
        in_specs=placed,
        out_specs=(
            P("section", None, "dp", None),
            P("section", None, "dp", None),
            P("section", None, "dp"),
            P("section", "dp", "tensor"),
            P("section", None, "dp", "tensor"),
            P("section", "tensor", "dp"),
            P("section", "dp", None),
            P("section", None, None, "dp", "tensor"),
            P("section", None, "tensor", "dp"),
        ),
        check_vma=False,
    )
```

```python
import math

import jax
import jax.numpy as jnp
from jax import lax
from jax.experimental import pallas as pl
from jax.experimental.pallas import tpu as pltpu
from jax.sharding import PartitionSpec as P

HEAD_SIZE = 64
E = 32
TOPK = 8
CAP = 48
ROWS = 128
WIDTH = 1024
FF = 512
PART = 32
LOCAL = 8
DENSE = 896

epsilon = 1e-06
rope_base = 10000.0
masked_score = -1e30
f32 = jnp.float32
bf16 = jnp.bfloat16
MESH = pl.DeviceIdType.MESH


def dot(a, b):
    return lax.dot_general(a, b, (((1,), (0,)), ((), ())), preferred_element_type=f32)


def dot_nt(a, b):
    return lax.dot_general(a, b, (((1,), (1,)), ((), ())), preferred_element_type=f32)


def dot_tn(a, b):
    return lax.dot_general(a, b, (((0,), (0,)), ((), ())), preferred_element_type=f32)


def unit(rows, columns, shift):
    row = lax.broadcasted_iota(jnp.int32, (rows, columns), 0)
    column = lax.broadcasted_iota(jnp.int32, (rows, columns), 1)
    return (row + shift == column).astype(bf16)


def scale_of(values):
    return lax.rsqrt(jnp.mean(values * values, axis=1, keepdims=True) + epsilon)


def norm_back(values, gain_row, upstream):
    scale = scale_of(values)
    weighted = upstream * gain_row
    inner = jnp.mean(weighted * values, axis=1, keepdims=True)
    back = scale * weighted - values * (scale * scale * scale * inner)
    return back, jnp.sum(upstream * values * scale, axis=0, keepdims=True)


def low_lanes():
    return lax.broadcasted_iota(jnp.int32, (ROWS, 128), 1) < 64


def turn(chunk, cos, sin):
    place = lax.broadcasted_iota(jnp.int32, (ROWS, 128), 1) % 64
    swapped = jnp.where(place < 32, pltpu.roll(chunk, 96, 1), pltpu.roll(chunk, 32, 1))
    return chunk * cos + swapped * sin


def doubled(both):
    wide = both.astype(f32)
    other = pltpu.roll(wide, 64, 1)
    left = low_lanes()
    return (
        jnp.where(left, wide, other).astype(bf16),
        jnp.where(left, other, wide).astype(bf16),
    )


def half(chunk, which):
    left = low_lanes()
    keep = left if which == 0 else jnp.logical_not(left)
    return jnp.where(keep, chunk, jnp.zeros_like(chunk))


def soft(query_half, keys, seen):
    scores = dot_nt(query_half, keys) * HEAD_SIZE ** (-0.5)
    scores = jnp.where(seen, scores, masked_score)
    raised = jnp.exp(scores - jnp.max(scores, axis=1, keepdims=True))
    return raised / jnp.sum(raised, axis=1, keepdims=True)


def body(
    lengths, query_own, keyval_own, out_own, router_own, gains_own, gateup_own, down_own,
    boundary, routes_own,
    out_ref, grad_ref, parts, pieces,
    own, dense, experts, dense_grad, shared, expert_grad, other, routes, cos_ref, sin_ref, seen_ref,
    xin, uin, turned, first_in, qkv, mixed, middle, chosen, chance, slot_gate,
    rs_send, rs_recv, ag, small, slots, packed, x_rows, og_rows, gate_s, up_s, hid_s,
    y_rows, ret, gu_low, probs, led, gate_grads, resid, gains, router_back, dqkv, swap_out, swap_in,
    rs_ss, rs_rs, ag_ss, ag_rs, sm_ss, sm_rs, d_ss, d_rs, r_ss, r_rs, w_ss, w_rs,
    a_ss, a_rs, b_ss, b_rs, e_ss, e_rs, g_ss, g_rs, p_ss, p_rs, h_ss, h_rs, c_ss,
):
    s = lax.axis_index("section")
    x = lax.axis_index("tensor")
    d = lax.axis_index("dp")
    z, y = d // 4, d % 4
    zz = z % 2
    mine = zz * 4 + (y + 2 * (z // 2)) % 4
    rows_mine = pl.ds(pl.multiple_of(x * PART, PART), PART)
    experts_mine = pl.ds(pl.multiple_of(x * LOCAL, LOCAL), LOCAL)
    odd = (y + z) % 2
    steps = (
        (0, 0), (1, 0), (3, 0), (0, 1), (0, 3),
        (1 + 2 * odd, 1 + 2 * odd), (3 - 2 * odd, 1 + 2 * odd), (2 - 2 * odd, 2 * odd),
    )

    def holder(n):
        y2, z2 = (y + steps[n][0]) % 4, (z + steps[n][1]) % 4
        return z2 % 2 * 4 + (y2 + 2 * (z2 // 2)) % 4, z2 * 4 + y2

    def sender(n):
        return (z + 4 - steps[n][1]) % 4 * 4 + (y + 4 - steps[n][0]) % 4

    barrier = pltpu.get_barrier_semaphore()

    def greet(k, carry):
        there, at = (x + k // 16) % 4, (d + k % 16) % 16

        @pl.when(k > 0)
        def _():
            pl.semaphore_signal(
                barrier, inc=1, device_id={"tensor": there, "dp": at}, device_id_type=MESH
            )

        return carry

    lax.fori_loop(0, 64, greet, 0)
    for peer in [holder(n)[1] for n in range(8)] + [sender(5), sender(6)]:
        pl.semaphore_signal(
            barrier, inc=1, device_id={"section": 1 - s, "dp": peer}, device_id_type=MESH
        )

    row = lax.broadcasted_iota(jnp.int32, (ROWS, 128), 0)
    lane = lax.broadcasted_iota(jnp.int32, (ROWS, 128), 1)
    start, row_doc, lane_doc, end = 0, 0, 0, 0
    for k in range(3):
        size = lengths[s, k]
        end = end + size
        start = start + jnp.where(row >= end, size, 0)
        row_doc = row_doc + jnp.where(row >= end, 1, 0)
        lane_doc = lane_doc + jnp.where(lane >= end, 1, 0)
    step = (lane % 32).astype(f32) * (-2.0 / HEAD_SIZE * math.log(rope_base))
    angles = (row - start).astype(f32) * jnp.exp(step)
    sine = jnp.sin(angles)
    cos_ref[...] = jnp.cos(angles)
    sin_ref[...] = jnp.where(lane % 64 < 32, -sine, sine)
    seen_ref[...] = jnp.where((row_doc == lane_doc) & (lane <= row), 1.0, 0.0)

    pl.semaphore_wait(barrier, 73)

    def remote(src, dst, send, recv, device):
        return pltpu.make_async_remote_copy(
            src_ref=src, dst_ref=dst, send_sem=send, recv_sem=recv,
            device_id=device, device_id_type=MESH,
        )

    def scatter_copies(l, j):
        copies = []
        for k in (2, 1, 3):
            p = (x + k) % 4
            src = rs_send.at[l, j, pl.ds(pl.multiple_of(p * PART, PART), PART)]
            copies.append(
                remote(src, rs_recv.at[l, j, k - 1], rs_ss.at[l, j, k - 1],
                       rs_rs.at[l, j, k - 1], {"tensor": p})
            )
        return copies

    def scatter_start(l, j, partial):
        rs_send[l, j] = partial.astype(bf16)
        for copy in scatter_copies(l, j):
            copy.start()

    def scatter_end(l, j):
        for copy in scatter_copies(l, j):
            copy.wait()
        total = rs_send[l, j, rows_mine].astype(f32)
        for k in range(3):
            total = total + rs_recv[l, j, k].astype(f32)
        return total

    def gather_copies(l, j):
        copies = []
        for k in (2, 1, 3):
            ref = ag.at[l, j, rows_mine]
            copies.append(
                remote(ref, ref, ag_ss.at[l, j, k - 1], ag_rs.at[l, j, k - 1],
                       {"tensor": (x + k) % 4})
            )
        return copies

    def gather_start(l, j, rows):
        ag[l, j, rows_mine] = rows.astype(bf16)
        for copy in gather_copies(l, j):
            copy.start()

    def gather_end(l, j):
        for copy in gather_copies(l, j):
            copy.wait()

    def small_copies(l, j):
        copies = []
        for k in range(1, 4):
            ref = small.at[l, j, x]
            copies.append(
                remote(ref, ref, sm_ss.at[l, j, k - 1], sm_rs.at[l, j, k - 1],
                       {"tensor": (x + k) % 4})
            )
        return copies

    def block(index):
        return pl.ds(pl.multiple_of(index * CAP, CAP), CAP)

    def dispatch_copies(l, way, act):
        rel = (s + l) % 2
        target = x_rows if way == 0 else og_rows
        for n in (5, 6, 7, 1, 2, 3, 4, 0):
            i, peer = holder(n)
            src = packed.at[l, way, block(i)]
            dst = target.at[block(rel * 8 + n)]
            far = remote(src, dst, d_ss.at[l, way, n], d_rs.at[way, rel * 8 + n],
                         {"section": l, "dp": peer})
            if n == 0:
                @pl.when(s == l)
                def _():
                    if act == 0:
                        pltpu.make_async_copy(src, dst, d_rs.at[way, 0]).start()

                @pl.when(s != l)
                def _():
                    if act == 0:
                        far.start()
                    else:
                        far.wait_send()
            elif act == 0:
                far.start()
            else:
                far.wait_send()

    def dispatch_arrived(way, rel):
        target = x_rows if way == 0 else og_rows

        def far(n):
            return remote(
                packed.at[0, way, block(n)], target.at[block(rel * 8 + n)],
                d_ss.at[0, way, n], d_rs.at[way, rel * 8 + n], {"dp": holder(1)[1]},
            )

        @pl.when(rel == 0)
        def _():
            pltpu.make_async_copy(
                packed.at[0, way, block(mine)], target.at[block(0)], d_rs.at[way, 0]
            ).wait()

        @pl.when(rel != 0)
        def _():
            far(0).wait_recv()

        for n in range(1, 8):
            far(n).wait_recv()

    def return_copies(l, way, rel, act):
        for n in (5, 6, 7, 1, 2, 3, 4, 0):
            peer = sender(n)
            src = y_rows.at[way, block(rel * 8 + n)]
            dst = ret.at[l, way, block(mine)]
            def far():
                return remote(src, dst, r_ss.at[way, rel * 8 + n], r_rs.at[l, way, n],
                              {"section": (s + rel) % 2, "dp": peer})

            def go():
                if act == 0:
                    far().start()
                else:
                    far().wait_send()

            if n > 0:
                go()
            else:
                pl.when(rel != 0)(go)
                if act == 0:
                    @pl.when(rel == 0)
                    def _():
                        pltpu.make_async_copy(src, dst, r_rs.at[l, way, 0]).start()

    def return_arrived(l, way):
        for n in range(8):
            i, peer = holder(n)
            src = y_rows.at[way, block(n)]
            dst = ret.at[l, way, block(i)]
            far = remote(src, dst, r_ss.at[way, n], r_rs.at[l, way, n],
                         {"section": 1 - s, "dp": peer})
            if n == 0:
                @pl.when(s == l)
                def _():
                    pltpu.make_async_copy(src, dst, r_rs.at[l, way, 0]).wait()

                @pl.when(s != l)
                def _():
                    far.wait_recv()
            else:
                far.wait_recv()

    def swap_copy(way):
        return remote(swap_out.at[way], swap_in.at[way], w_ss.at[way], w_rs.at[way],
                      {"section": 1 - s})

    def keep_result(way, l, ref):
        @pl.when(s == l)
        def _():
            ref[s] = ag[l, 1 + 2 * way]

        @pl.when(s != l)
        def _():
            swap_out[way] = ag[l, 1 + 2 * way]
            swap_copy(way).start()

    def block64(index):
        return pl.ds(pl.multiple_of(index * 64, 64), 64)

    def block128(index):
        return pl.ds(pl.multiple_of(index * 128, 128), 128)

    left, right = slice(0, 512), slice(512, DENSE)

    def along_y(k):
        return {"dp": z * 4 + (y + k) % 4}

    def along_z(k):
        return {"dp": ((z + k) % 4) * 4 + y}

    def spread_copies(part, phase):
        copies = []
        for k in range(1, 4):
            if part == 0:
                ref = dense.at[s, z, y, :, left] if phase == 0 else dense.at[s, z, :, :, left]
                device = along_y(k) if phase == 0 else along_z(k)
            else:
                ref = dense.at[s, z, y, :, right] if phase == 0 else dense.at[s, :, y, :, right]
                device = along_z(k) if phase == 0 else along_y(k)
            n = k - 1
            copies.append(
                remote(ref, ref, a_ss.at[part, phase, n], a_rs.at[part, phase, n], device)
            )
        return copies

    def sibling_copy(part, k, layer):
        if part == 0:
            ref = dense.at[layer, (z + k) % 4, :, :, left]
        else:
            ref = dense.at[layer, :, (y + k) % 4, :, right]
        return remote(ref, ref, b_ss.at[part, k], b_rs.at[part, k], {"section": 1 - s})

    def weight_copy(kind):
        src = gateup_own.at[kind] if kind < 2 else down_own
        return pltpu.make_async_copy(src, own.at[:, kind], c_ss.at[kind])

    def exchange_copies():
        return [
            remote(boundary.at[1 - s], other, b_ss.at[2, 0], b_rs.at[2, 0], {"section": 1 - s}),
            remote(routes_own.at[1 - s], routes.at[s], b_ss.at[2, 1], b_rs.at[2, 1],
                   {"section": 1 - s}),
        ]

    def expert_copy(k, local_only=False):
        there, at = (x + k // 16) % 4, (d + k % 16) % 16
        e = there * 8 + at // 4 % 2 * 4 + (at % 4 + 2 * (at // 8)) % 4
        src, dst = own.at[e], experts.at[:, block64(d), block128(x)]
        if local_only:
            return pltpu.make_async_copy(src, dst, e_rs.at[0])
        return remote(src, dst, e_ss.at[k], e_rs.at[k], {"tensor": there, "dp": at})

    def piece_copy(k, local_only=False):
        there, at = (x + k // 16) % 4, (d + k % 16) % 16
        src = expert_grad.at[:, block64(at), block128(there)]
        dst = pieces.at[z // 2, :, x * 8 + mine]
        if local_only:
            return pltpu.make_async_copy(src, dst, p_rs.at[0])
        return remote(src, dst, p_ss.at[k], p_rs.at[k], {"tensor": there, "dp": at})

    def all_but_own(copy, act, low=1, high=64):
        def one(n, carry):
            getattr(copy(n * 13 % 64), act)()
            return carry

        lax.fori_loop(low, high, one, 0)

    def push(copy, low, high):
        whole = isinstance(low, int) and low == 0
        if whole:
            copy(0, True).start()
        all_but_own(copy, "start", 1 if whole else low, high)

    def push_when(condition, copy, low, high):
        pl.when(condition)(lambda: push(copy, low, high))

    def arrive(copy):
        copy(0, True).wait()
        all_but_own(copy, "wait_recv")

    wide = (slice(0, 512), slice(512, 768), slice(768, DENSE))

    def part_copy(c, k, local_only=False):
        at = (d + k) % 16
        src = dense_grad.at[s, block64(at), wide[c]]
        dst = parts.at[d, :, wide[c]]
        if local_only:
            return pltpu.make_async_copy(src, dst, g_rs.at[c, 0])
        return remote(src, dst, g_ss.at[c, k], g_rs.at[c, k], {"dp": at})

    def share_copy(c):
        return remote(dense_grad.at[1 - s, :, wide[c]], shared.at[:, wide[c]],
                      h_ss.at[c], h_rs.at[c], {"section": 1 - s})

    def share(l, c):
        @pl.when(s != l)
        def _():
            share_copy(c).start()

    def part_push(l, c):
        @pl.when(s == l)
        def _():
            share_copy(c).wait_recv()
            both = dense_grad[l, :, wide[c]].astype(f32) + shared[:, wide[c]].astype(f32)
            dense_grad[l, :, wide[c]] = both.astype(bf16)
            part_copy(c, 0, True).start()

            def one(k, carry):
                part_copy(c, k).start()
                return carry

            lax.fori_loop(1, 16, one, 0)

    for copy in exchange_copies():
        copy.start()
    for kind in range(3):
        weight_copy(kind).start()
    routes[s] = routes_own[s]
    dense[s, z, y, :, 0:256] = query_own[...]
    dense[s, z, y, :, 256:384] = keyval_own[0]
    dense[s, z, y, :, 384:512] = keyval_own[1]
    dense[s, z, y, :, 512:768] = out_own[...]
    last = dot_tn(router_own[...], unit(E, 128, 0)) + dot_tn(gains_own[...], unit(2, 128, E))
    dense[s, z, y, :, 768:896] = last.astype(bf16)
    for part in range(2):
        for copy in spread_copies(part, 0):
            copy.start()


    @pl.when(s == 0)
    def _():
        xin[0] = boundary[0]

    @pl.when(s == 1)
    def _():
        uin[1] = boundary[1]

    for part in range(2):
        for copy in spread_copies(part, 0):
            copy.wait()
    for kind in range(3):
        weight_copy(kind).wait()

    def spread_start():
        for part in range(2):
            for copy in spread_copies(part, 1):
                copy.start()
            sibling_copy(part, 0, s).start()

    def spread_end():
        for part in range(2):
            for k in range(3):
                spread_copies(part, 1)[k].wait()
                sibling_copy(part, 3 - k, s).start()

    @pl.when(s == 0)
    def _():
        spread_start()
        push(expert_copy, 0, 64)
        spread_end()

    @pl.when(s == 1)
    def _():
        for copy in exchange_copies()[:1]:
            copy.wait()
        xin[0] = other[...]

    def weight(l, low, high):
        return dense[l, :, :, :, low:high].reshape(WIDTH, high - low)

    def forward(l, carry):
        @pl.when(s != l)
        def _():
            for part in range(2):
                for k in range(4):
                    sibling_copy(part, k, s).wait_recv()
            exchange_copies()[1].wait()

        turned[l] = weight(l, 768, 896).astype(f32).T
        values = xin[l]
        first = (values * scale_of(values) * turned[l, 32:33]).astype(bf16)
        first_in[l] = first
        made = dot(first, weight(l, 0, 512))
        cos, sin = cos_ref[...], sin_ref[...]
        for c in range(3):
            cut = slice(128 * c, 128 * c + 128)
            qkv[l, :, cut] = turn(made[:, cut], cos, sin).astype(bf16)
        qkv[l, :, 384:512] = made[:, 384:512].astype(bf16)
        seen = seen_ref[...] > 0
        keys = doubled(qkv[l, :, 256:384])
        vals = doubled(qkv[l, :, 384:512])
        for c in range(2):
            cut = slice(128 * c, 128 * c + 128)
            query = qkv[l, :, cut]
            got = [
                dot(soft(half(query, b), keys[c], seen).astype(bf16), vals[c]) for b in range(2)
            ]
            mixed[l, :, cut] = jnp.where(low_lanes(), got[0], got[1]).astype(bf16)
        scatter_start(l, 0, dot_nt(mixed[l], weight(l, 512, 768)))


        @pl.when((s == 1) & (l == 0))
        def _():
            push(expert_copy, 0, 64)

        experts_iota = lax.broadcasted_iota(jnp.int32, (E, ROWS), 0)
        named = jnp.zeros((E, ROWS), f32)
        for k in range(TOPK):
            named = named + (experts_iota == routes[l, k:k + 1]).astype(f32)
        before = (
            lax.broadcasted_iota(jnp.int32, (ROWS, ROWS), 0)
            < lax.broadcasted_iota(jnp.int32, (ROWS, ROWS), 1)
        ).astype(bf16)
        place = dot(named.astype(bf16), before)
        slots[...] = jnp.where(named > 0, place, -1.0)
        place = slots[experts_mine]
        slot_iota = lax.broadcasted_iota(jnp.int32, (CAP, ROWS), 0).astype(f32)
        for i in range(LOCAL):
            chosen[l, CAP * i:CAP * i + CAP] = (slot_iota == place[i:i + 1]).astype(bf16)

        center = xin[l, rows_mine] + scatter_end(l, 0)
        middle[l] = center
        gather_start(l, 0, center * scale_of(center) * turned[l, 33:34])
        gather_end(l, 0)

        second = ag[l, 0]
        packed[l, 0] = dot(chosen[l], second).astype(bf16)
        dispatch_copies(l, 0, 0)
        pl.when((s == 1) & (l == 0))(spread_start)
        logits = dot_nt(turned[l, 0:32].astype(bf16), second)
        logits = jnp.where(named > 0, logits, masked_score)
        raised = jnp.where(named > 0, jnp.exp(logits - jnp.max(logits, axis=0, keepdims=True)), 0.0)
        chance[l] = raised / jnp.sum(raised, axis=0, keepdims=True)
        gate = chance[l, experts_mine]
        for i in range(LOCAL):
            cut = slice(CAP * i, CAP * i + CAP)
            weighted = chosen[l, cut].astype(f32) * gate[i:i + 1]
            slot_gate[l, cut] = jnp.sum(weighted, axis=1, keepdims=True)
            led[cut] = weighted.astype(bf16)

        @pl.when(s == l)
        def _():
            arrive(expert_copy)
            for turn_no in range(2):
                rel = (l + turn_no) % 2
                dispatch_arrived(0, rel)
                cut = pl.ds(pl.multiple_of(384 * rel, 384), 384)
                rows = x_rows[cut]
                gate_part = dot(rows, experts[0])
                up_part = dot(rows, experts[1])
                gate_s[cut] = gate_part
                up_s[cut] = up_part
                hidden = (gate_part / (1.0 + jnp.exp(-gate_part)) * up_part).astype(bf16)
                hid_s[cut] = hidden
                y_rows[0, cut] = dot_nt(hidden, experts[2]).astype(bf16)
                return_copies(l, 0, rel, 0)

        @pl.when((s == 1) & (l == 0))
        def _():
            spread_end()

        return_arrived(l, 0)
        scatter_start(l, 1, dot_tn(led[...], ret[l, 0]))
        gather_start(l, 1, middle[l] + scatter_end(l, 1))
        gather_end(l, 1)
        xin[l + 1] = ag[l, 1].astype(f32)
        keep_result(0, l, out_ref)
        dispatch_copies(l, 0, 1)
        return carry

    lax.fori_loop(0, 2, forward, 0)

    @pl.when(s == 0)
    def _():
        for copy in exchange_copies()[:1]:
            copy.wait()
        uin[1] = other[...]

    def backward(step, carry):
        l = 1 - step
        upstream = uin[l].astype(bf16)
        spread = dot(chosen[l], upstream)
        packed[l, 1] = (spread * slot_gate[l]).astype(bf16)
        dispatch_copies(l, 1, 0)
        inner = jnp.sum(spread * ret[l, 0].astype(f32), axis=1, keepdims=True)
        for i in range(LOCAL):
            cut = slice(CAP * i, CAP * i + CAP)
            row = jnp.sum(chosen[l, cut].astype(f32) * inner[cut], axis=0, keepdims=True)
            gate_grads[i:i + 1] = row
        small[l, 0, x, 0:8] = gate_grads[...]
        for copy in small_copies(l, 0):
            copy.start()

        @pl.when(s == l)
        def _():
            for turn_no in range(2):
                rel = (l + turn_no) % 2
                dispatch_arrived(1, rel)
                cut = pl.ds(pl.multiple_of(384 * rel, 384), 384)
                hidden_grad = dot(og_rows[cut], experts[2])
                gate_part = gate_s[cut]
                up_part = up_s[cut]
                sig = 1.0 / (1.0 + jnp.exp(-gate_part))
                gate_low = (
                    hidden_grad * up_part * sig * (1.0 + gate_part * (1.0 - sig))
                ).astype(bf16)
                up_low = (hidden_grad * gate_part * sig).astype(bf16)
                gu_low[cut, 0:FF] = gate_low
                gu_low[cut, FF:2 * FF] = up_low
                back = dot_nt(gate_low, experts[0]) + dot_nt(up_low, experts[1])
                y_rows[1, cut] = back.astype(bf16)
                return_copies(l, 1, rel, 0)
            both = dot_tn(x_rows[...], gu_low[...])
            expert_grad[0] = both[:, 0:FF].astype(bf16)
            expert_grad[1] = both[:, FF:2 * FF].astype(bf16)

        for copy in small_copies(l, 0):
            copy.wait()
        gate = chance[l]
        gate_total = jnp.concatenate([small[l, 0, p, 0:8] for p in range(4)], axis=0)
        picked = gate * (gate_total - jnp.sum(gate * gate_total, axis=0, keepdims=True))
        logit_low = picked.astype(bf16)
        router_back[...] = dot_tn(logit_low, turned[l, 0:32].astype(bf16))
        return_arrived(l, 1)
        scatter_start(l, 2, dot_tn(chosen[l], ret[l, 1]))

        @pl.when(s == l)
        def _():
            expert_grad[2] = dot_tn(og_rows[...], hid_s[...]).astype(bf16)
            push(piece_copy, 0, 16)

        router_grad = dot(logit_low, ag[l, 0])
        arrived = scatter_end(l, 2) + router_back[rows_mine]
        back, gain_two = norm_back(middle[l], turned[l, 33:34], arrived)
        kept = uin[l, rows_mine] + back
        resid[...] = kept
        gather_start(l, 2, kept)
        push_when(s == l, piece_copy, 16, 24)
        seen = seen_ref[...] > 0
        keys = doubled(qkv[l, :, 256:384])
        for h in range(4):
            query = qkv[l, :, 128 * (h // 2):128 * (h // 2) + 128]
            probs[h] = soft(half(query, h % 2), keys[h // 2], seen)
        gather_end(l, 2)

        branch = ag[l, 2]
        push_when(s == l, piece_copy, 24, 40)
        mixed_grad = dot(branch, weight(l, 512, 768)).astype(bf16)
        cos, sin = cos_ref[...], -sin_ref[...]
        left = low_lanes()
        vals = doubled(qkv[l, :, 384:512])
        key_grads, value_grads = [], []
        for c in range(2):
            cut = slice(128 * c, 128 * c + 128)
            query, above = qkv[l, :, cut], mixed_grad[:, cut]
            parts, key_grad, value_grad = [], 0.0, 0.0
            for b in range(2):
                query_half, above_half = half(query, b), half(above, b)
                prob = probs[2 * c + b]
                value_grad = value_grad + dot_tn(prob.astype(bf16), above_half)
                prob_grad = dot_nt(above_half, vals[c])
                mean = jnp.sum(prob * prob_grad, axis=1, keepdims=True)
                score_low = (prob * (prob_grad - mean)).astype(bf16)
                parts.append(dot(score_low, keys[c]))
                key_grad = key_grad + dot_tn(score_low, query_half)
            query_grad = jnp.where(left, parts[0], parts[1]) * HEAD_SIZE ** (-0.5)
            dqkv[:, cut] = turn(query_grad, cos, sin).astype(bf16)
            key_grads.append(key_grad + pltpu.roll(key_grad, 64, 1))
            value_grads.append(value_grad + pltpu.roll(value_grad, 64, 1))
        key_grad = jnp.where(left, key_grads[0], key_grads[1]) * HEAD_SIZE ** (-0.5)
        dqkv[:, 256:384] = turn(key_grad, cos, sin).astype(bf16)
        dqkv[:, 384:512] = jnp.where(left, value_grads[0], value_grads[1]).astype(bf16)
        scatter_start(l, 3, dot_nt(dqkv[...], weight(l, 0, 512)))
        push_when(s == l, piece_copy, 40, 48)
        dense_grad[l, :, 512:768] = dot_tn(branch, mixed[l]).astype(bf16)
        share(l, 1)
        dense_grad[l, :, 0:512] = dot_tn(first_in[l], dqkv[...]).astype(bf16)
        share(l, 0)
        part_push(l, 1)
        back, gain_one = norm_back(xin[l, rows_mine], turned[l, 32:33], scatter_end(l, 3))
        gather_start(l, 3, resid[...] + back)
        push_when(s == l, piece_copy, 48, 56)
        gains[l, x, 0:1] = gain_one
        gains[l, x, 1:2] = gain_two
        for k in range(1, 4):
            ref = gains.at[l, x]
            remote(ref, ref, sm_ss.at[l, 1, k - 1], sm_rs.at[l, 1, k - 1],
                   {"tensor": (x + k) % 4}).start()
        part_push(l, 0)
        gather_end(l, 3)
        uin[1 - l] = ag[l, 3].astype(f32)
        keep_result(1, l, grad_ref)
        for k in range(1, 4):
            ref = gains.at[l, x]
            remote(ref, ref, sm_ss.at[l, 1, k - 1], sm_rs.at[l, 1, k - 1],
                   {"tensor": (x + k) % 4}).wait()
        total = gains[l, 0] + gains[l, 1] + gains[l, 2] + gains[l, 3]
        last = jnp.concatenate([router_grad, total, jnp.zeros((88, WIDTH), f32)], axis=0)
        dense_grad[l, :, 768:896] = last.T.astype(bf16)
        push_when(s == l, piece_copy, 56, 64)
        share(l, 2)
        part_push(l, 2)
        dispatch_copies(l, 1, 1)
        return carry

    lax.fori_loop(0, 2, backward, 0)

    for way, ref in ((0, out_ref), (1, grad_ref)):
        swap_copy(way).wait()
        ref[1 - s] = swap_in[way]
        for rel in range(2):
            return_copies(s, way, jnp.int32(rel), 1)
    for part in range(2):
        for k in range(4):
            sibling_copy(part, k, s).wait_send()
    all_but_own(expert_copy, "wait_send")
    all_but_own(piece_copy, "wait_send")
    arrive(piece_copy)
    for c in range(3):
        share_copy(c).wait_send()
        part_copy(c, 0, True).wait()

        def one(k, carry):
            part_copy(c, k).wait()
            return carry

        lax.fori_loop(1, 16, one, 0)


def layers(*operands):
    shape = jax.ShapeDtypeStruct
    scratch = [
        pltpu.VMEM((E, 3, 64, 128), bf16),
        pltpu.VMEM((2, 4, 4, 64, DENSE), bf16),
        pltpu.VMEM((3, WIDTH, FF), bf16),
        pltpu.VMEM((2, WIDTH, DENSE), bf16),
        pltpu.VMEM((WIDTH, DENSE), bf16),
        pltpu.VMEM((3, WIDTH, FF), bf16),
        pltpu.VMEM((ROWS, WIDTH), f32),
        pltpu.VMEM((2, TOPK, ROWS), jnp.int32),
        pltpu.VMEM((ROWS, 128), f32),
        pltpu.VMEM((ROWS, 128), f32),
        pltpu.VMEM((ROWS, 128), f32),
        pltpu.VMEM((3, ROWS, WIDTH), f32),
        pltpu.VMEM((2, ROWS, WIDTH), f32),
        pltpu.VMEM((2, ROWS, WIDTH), f32),
        pltpu.VMEM((2, ROWS, WIDTH), bf16),
        pltpu.VMEM((2, ROWS, 512), bf16),
        pltpu.VMEM((2, ROWS, 256), bf16),
        pltpu.VMEM((2, PART, WIDTH), f32),
        pltpu.VMEM((2, LOCAL * CAP, ROWS), bf16),
        pltpu.VMEM((2, E, ROWS), f32),
        pltpu.VMEM((2, LOCAL * CAP, 1), f32),
        pltpu.VMEM((2, 4, ROWS, WIDTH), bf16),
        pltpu.VMEM((2, 4, 3, PART, WIDTH), bf16),
        pltpu.VMEM((2, 4, ROWS, WIDTH), bf16),
        pltpu.VMEM((2, 1, 4, 8, ROWS), f32),
        pltpu.VMEM((E, ROWS), f32),
        pltpu.VMEM((2, 2, LOCAL * CAP, WIDTH), bf16),
        pltpu.VMEM((2 * LOCAL * CAP, WIDTH), bf16),
        pltpu.VMEM((2 * LOCAL * CAP, WIDTH), bf16),
        pltpu.VMEM((2 * LOCAL * CAP, FF), f32),
        pltpu.VMEM((2 * LOCAL * CAP, FF), f32),
        pltpu.VMEM((2 * LOCAL * CAP, FF), bf16),
        pltpu.VMEM((2, 2 * LOCAL * CAP, WIDTH), bf16),
        pltpu.VMEM((2, 2, LOCAL * CAP, WIDTH), bf16),
        pltpu.VMEM((2 * LOCAL * CAP, 2 * FF), bf16),
        pltpu.VMEM((4, ROWS, ROWS), f32),
        pltpu.VMEM((LOCAL * CAP, ROWS), bf16),
        pltpu.VMEM((8, ROWS), f32),
        pltpu.VMEM((PART, WIDTH), f32),
        pltpu.VMEM((2, 4, 8, WIDTH), f32),
        pltpu.VMEM((ROWS, WIDTH), f32),
        pltpu.VMEM((ROWS, 512), bf16),
        pltpu.VMEM((2, ROWS, WIDTH), bf16),
        pltpu.VMEM((2, ROWS, WIDTH), bf16),
        pltpu.SemaphoreType.DMA((2, 4, 3)),
        pltpu.SemaphoreType.DMA((2, 4, 3)),
        pltpu.SemaphoreType.DMA((2, 4, 3)),
        pltpu.SemaphoreType.DMA((2, 4, 3)),
        pltpu.SemaphoreType.DMA((2, 2, 3)),
        pltpu.SemaphoreType.DMA((2, 2, 3)),
        pltpu.SemaphoreType.DMA((2, 2, 8)),
        pltpu.SemaphoreType.DMA((2, 16)),
        pltpu.SemaphoreType.DMA((2, 16)),
        pltpu.SemaphoreType.DMA((2, 2, 8)),
        pltpu.SemaphoreType.DMA((2,)),
        pltpu.SemaphoreType.DMA((2,)),
        pltpu.SemaphoreType.DMA((2, 2, 3)),
        pltpu.SemaphoreType.DMA((2, 2, 3)),
        pltpu.SemaphoreType.DMA((3, 4)),
        pltpu.SemaphoreType.DMA((3, 4)),
        pltpu.SemaphoreType.DMA((64,)),
        pltpu.SemaphoreType.DMA((64,)),
        pltpu.SemaphoreType.DMA((3, 16)),
        pltpu.SemaphoreType.DMA((3, 16)),
        pltpu.SemaphoreType.DMA((64,)),
        pltpu.SemaphoreType.DMA((64,)),
        pltpu.SemaphoreType.DMA((3,)),
        pltpu.SemaphoreType.DMA((3,)),
        pltpu.SemaphoreType.DMA((3,)),
    ]
    return pl.pallas_call(
        body,
        out_shape=(
            shape((2, ROWS, WIDTH), bf16),
            shape((2, ROWS, WIDTH), bf16),
            shape((16, 64, DENSE), bf16),
            shape((2, 3, E, 64, 128), bf16),
        ),
        in_specs=[
            pl.BlockSpec(memory_space=pltpu.SMEM),
            *[pl.BlockSpec(memory_space=pltpu.VMEM) for _ in range(5)],
            *[pl.BlockSpec(memory_space=pl.ANY) for _ in range(2)],
            *[pl.BlockSpec(memory_space=pltpu.VMEM) for _ in range(2)],
        ],
        out_specs=(
            pl.BlockSpec(memory_space=pltpu.VMEM),
            pl.BlockSpec(memory_space=pltpu.VMEM),
            pl.BlockSpec(memory_space=pl.ANY),
            pl.BlockSpec(memory_space=pl.ANY),
        ),
        scratch_shapes=scratch,
        compiler_params=pltpu.CompilerParams(
            collective_id=0, has_side_effects=True, vmem_limit_bytes=60 * 1024 * 1024
        ),
        name="layers",
    )(*operands)


def local(
    boundary,
    doc_lengths,
    routes,
    norm_gains,
    w_query,
    key_value_weight,
    w_out,
    w_router,
    w_gateup,
    w_down,
):
    outs, grads, parts, pieces = layers(
        doc_lengths[:, 0], w_query[0], key_value_weight[0], w_out[0].T, w_router[0].T, norm_gains[0],
        w_gateup[0], jnp.swapaxes(w_down[0], 1, 2), boundary[0], jnp.swapaxes(routes[0], 1, 2),
    )
    parts = jnp.sum(parts.astype(f32), axis=0)
    pieces = pieces.astype(f32)
    return (
        outs.astype(f32)[None],
        grads.astype(f32)[None],
        parts[:, 800:802].T[None],
        parts[:, 0:256][None],
        jnp.stack([parts[:, 256:384], parts[:, 384:512]])[None],
        parts[:, 512:768].T[None],
        parts[:, 768:800][None],
        (pieces[0, 0:2] + pieces[1, 0:2])[None],
        jnp.swapaxes(pieces[0, 2] + pieces[1, 2], 1, 2)[None],
    )


def solution(mesh):
    placed = (
        P("section", None, "dp", None),
        P(None, "dp", None),
        P("section", None, "dp", None),
        P("section", None, "dp"),
        P("section", "dp", "tensor"),
        P("section", None, "dp", "tensor"),
        P("section", "tensor", "dp"),
        P("section", "dp", None),
        P("section", None, None, "dp", "tensor"),
        P("section", None, "tensor", "dp"),
    )
    return jax.shard_map(
        local,
        mesh=mesh,
        in_specs=placed,
        out_specs=(
            P("section", None, "dp", None),
            P("section", None, "dp", None),
            P("section", None, "dp"),
            P("section", "dp", "tensor"),
            P("section", None, "dp", "tensor"),
            P("section", "tensor", "dp"),
            P("section", "dp", None),
            P("section", None, None, "dp", "tensor"),
            P("section", None, "tensor", "dp"),
        ),
        check_vma=False,
    )
```
